32 devices in a mesh: sec: 4 (over x, core), seq: 4 (over z), tp: 2 (over y).
Axes of the slice: x: 2, y: 2, z: 4, core: 2. Of those that a mesh axis runs over, the one named last changes fastest.
Arguments:
- vis_rows: bfloat16 [512, 3200], P('seq'), may hold values from -6 to 6
- vis_gain: float32 [3200], replicated, may hold values from 0.1 to 1.9
- key_value_proj: bfloat16 [3200, 2048], P(None, ('sec', 'tp')), may hold values from -0.109375 to 0.109375
- pieces: int32 [8], replicated, may hold values from 1 to 127, as said below
- text_kv: bfloat16 [512, 2048], P('seq', ('sec', 'tp')), may hold values from -6 to 6
- queries: bfloat16 [512, 4096], P('seq', ('sec', 'tp')), may hold values from -256 to 256
- grad_out: bfloat16 [512, 4096], P('seq', ('sec', 'tp')), may hold values from -6 to 6
Outputs:
- attended: bfloat16 [512, 4096], P('seq', ('sec', 'tp'))
- vis_grad: bfloat16 [512, 3200], P('seq')
The draws below stay inside these ranges and needn't reach their ends.
Inputs may be any that keep to these rules, and one draw needn't show every extreme that they name: `pieces`: entries alternate: the text positions before image j, then the tokens of image j, for j = 0 to 3; entries 2 j and 2 j + 1 sum to 128; image j's tokens are the leading rows of block b_j of vis_rows.
All inputs are finite; a program needn't handle non-finite values.
Results may differ from the reference program's by a relative error of at most 0.033.
Values may be sent and summed in bfloat16 or wider, within the bound.
No kernel may reach another device: no remote copies, remote signals or barrier semaphores. Data moves between devices by JAX's collectives and lax.ppermute only.
A program may use at most 64 MiB of HBM per device.

```python
import math
import jax
import jax.numpy as jnp
from jax import lax

DV = 3200
HD = 128
QH = 32
KVH = 8
TOK_DEV = 128
SEQLEN = 512


def text_base(key):
    return jnp.clip(jax.random.normal(key, (SEQLEN, KVH, 2, HD), jnp.float32), -6.0, 6.0)


def draw_pieces(key, part):
    key = jax.random.fold_in(key, 21)
    image_count = SEQLEN // TOK_DEV
    first_key, second_key = jax.random.split(key)
    image_lens = jax.random.randint(first_key, (image_count,), 1, TOK_DEV)
    picked = jax.random.randint(second_key, (), 0, image_count)
    image_lens = jnp.where(jnp.arange(image_count) == picked, TOK_DEV - 1, image_lens)
    text_lens = TOK_DEV - image_lens
    return jnp.stack([text_lens, image_lens], axis=1).reshape(2 * image_count).astype(jnp.int32)


def draw_text_kv(key, part):
    base_rows = text_base(key)
    return base_rows.reshape(SEQLEN, KVH * 2 * HD).astype(jnp.bfloat16)


def draw_queries(key, part):
    key = jax.random.fold_in(key, 12)
    fresh_rows = jnp.clip(2.5 * jax.random.normal(key, (SEQLEN, QH * HD), jnp.float32), -15.0, 15.0)
    return fresh_rows.astype(jnp.bfloat16)


def levels(own_key, shape, shards, smallest, high):
    factor_of, own = 1.0, jax.random.fold_in(own_key, 6)
    for dim, shards_of in shards:
        draws = jnp.exp(jax.random.uniform(jax.random.fold_in(own, dim), (shards_of,), jnp.float32, smallest / len(shards), high / len(shards)))
        factor_of = factor_of * jnp.repeat(draws, shape[dim] // shards_of).reshape([-1 if axis == dim else 1 for axis in range(len(shape))])
    return factor_of


def bell_draw(key, extent, spread, reach, shards=(), held_as=jnp.bfloat16):
    values = jax.random.normal(key, extent, jnp.float32) * spread
    if len(shards) > 0:
        values = levels(key, extent, shards, -0.22, 0.18) * values
    return jnp.clip(values, min=-reach, max=reach).astype(held_as)


def setup_inputs(seed: int = 0) -> dict:
    key_of = jax.random.split(jax.random.key(seed), 8)
    vis_rows = bell_draw(key_of[0], (SEQLEN, DV), 1.0, 6.0, ((0, 4),))
    vis_gain = jnp.clip(1.0 + 0.18 * jax.random.normal(key_of[1], (DV,), jnp.float32), 0.1, 1.9)
    key_value_proj = bell_draw(key_of[2], (DV, KVH * 2 * HD), DV ** -0.5, 0.109375, ((1, 8),))
    pieces = draw_pieces(jax.random.fold_in(key_of[7], 71), 0)
    text_kv = draw_text_kv(jax.random.fold_in(key_of[7], 71), 0)
    queries = draw_queries(jax.random.fold_in(key_of[7], 71), 0)
    grad_out = bell_draw(key_of[6], (SEQLEN, QH * HD), 1.0, 6.0, ((0, 4), (1, 8)))
    return dict(vis_rows=vis_rows, vis_gain=vis_gain, key_value_proj=key_value_proj, pieces=pieces, text_kv=text_kv, queries=queries, grad_out=grad_out)


EPS = 1e-06
NEG = -1e+30

def image_layout(pieces):
    totals = jnp.cumsum(pieces)
    lens_img = pieces[1::2]
    starts_img = totals[1::2] - lens_img
    return (starts_img, lens_img)

def owner_block(image_ids, image_count):
    half_count = image_count // 2
    return jnp.where(image_ids >= half_count, image_ids - half_count, half_count + (image_ids + 1) % half_count).astype(jnp.int32)

def image_held(block_ids, image_count):
    half_count = image_count // 2
    return jnp.where(block_ids < half_count, block_ids + half_count, (block_ids - half_count - 1) % half_count).astype(jnp.int32)

def normed(vis, gain_vec):
    wide_rows = vis.astype(jnp.float32)
    inverse = lax.rsqrt(lax.optimization_barrier(jnp.mean(wide_rows * wide_rows, axis=-1, keepdims=True)) + EPS)
    return wide_rows * inverse * gain_vec.astype(jnp.float32)

def compose_keys(image_all, text_all, starts_img, lens_img, rows_each):
    total_rows = text_all.shape[0]
    image_count = starts_img.shape[0]
    positions = jnp.arange(total_rows, dtype=jnp.int32)
    offset_rows = positions[:, None] - starts_img[None, :]
    inside = (offset_rows >= 0) & (offset_rows < lens_img[None, :])
    owners = owner_block(jnp.arange(image_count, dtype=jnp.int32), image_count)
    source = lax.optimization_barrier(jnp.sum(jnp.where(inside, owners[None, :] * rows_each + offset_rows, 0), axis=1)).astype(jnp.int32)
    marked = jnp.any(inside, axis=1)
    return jnp.where(marked[:, None], image_all[source], text_all)

def attend_block(query_part, grad_part, key_rows, value_rows, query_pos, score_scale):
    key_pos = jnp.arange(key_rows.shape[0], dtype=jnp.int32)
    scores = jnp.einsum('rhe,ke->hrk', query_part, key_rows) * score_scale
    allowed = key_pos[None, None, :] <= query_pos[None, :, None]
    scores = jnp.where(allowed, scores, NEG)
    row_max = lax.optimization_barrier(jnp.max(scores, axis=-1, keepdims=True))
    exp_scores = jnp.exp(scores - row_max)
    weights = exp_scores / lax.optimization_barrier(jnp.sum(exp_scores, axis=-1, keepdims=True))
    weights_low = weights.astype(jnp.bfloat16).astype(jnp.float32)
    mixed_rows = jnp.einsum('hrk,ke->rhe', weights_low, value_rows)
    row_drift = lax.optimization_barrier(jnp.sum(grad_part * mixed_rows, axis=-1))
    weight_grads = jnp.einsum('rhe,ke->hrk', grad_part, value_rows)
    score_grads = (weights * (weight_grads - jnp.transpose(row_drift)[:, :, None]) * score_scale).astype(jnp.bfloat16).astype(jnp.float32)
    key_part = jnp.einsum('hrk,rhe->ke', score_grads, query_part)
    value_part = jnp.einsum('hrk,rhe->ke', weights_low, grad_part)
    return (mixed_rows, key_part, value_part)

def reference(vis_rows, vis_gain, key_value_proj, pieces, text_kv, queries, grad_out):
    score_scale = 1.0 / math.sqrt(HD)
    group_size = QH // KVH
    starts_img, lens_img = image_layout(pieces)
    normed_rows = normed(vis_rows, vis_gain).astype(jnp.bfloat16)
    image_kv = jnp.dot(normed_rows, key_value_proj, preferred_element_type=jnp.float32).astype(jnp.bfloat16)
    seq_kv = compose_keys(image_kv, text_kv, starts_img, lens_img, TOK_DEV)
    block_rows = math.gcd(SEQLEN, 512)
    out_blocks = []
    grad_blocks = []
    for kv_head in range(KVH):
        key_rows = seq_kv[:, kv_head * 2 * HD:kv_head * 2 * HD + HD].astype(jnp.float32)
        value_rows = seq_kv[:, kv_head * 2 * HD + HD:(kv_head + 1) * 2 * HD].astype(jnp.float32)
        key_total = jnp.zeros((SEQLEN, HD), jnp.float32)
        value_total = jnp.zeros((SEQLEN, HD), jnp.float32)
        head_outs = []
        col_start = kv_head * group_size * HD
        col_stop = col_start + group_size * HD
        for block_start in range(0, SEQLEN, block_rows):
            block_end = block_start + block_rows
            query_part = queries[block_start:block_end, col_start:col_stop].reshape(block_rows, group_size, HD).astype(jnp.float32)
            grad_part = grad_out[block_start:block_end, col_start:col_stop].reshape(block_rows, group_size, HD).astype(jnp.float32)
            query_pos = jnp.arange(block_start, block_end, dtype=jnp.int32)
            mixed_rows, key_part, value_part = attend_block(query_part, grad_part, key_rows[:block_end], value_rows[:block_end], query_pos, score_scale)
            head_outs.append(mixed_rows.reshape(block_rows, group_size * HD).astype(jnp.bfloat16))
            key_total = key_total.at[:block_end].add(key_part)
            value_total = value_total.at[:block_end].add(value_part)
        out_blocks.append(jnp.concatenate(head_outs, axis=0))
        grad_blocks.append(key_total)
        grad_blocks.append(value_total)
    attended = jnp.concatenate(out_blocks, axis=1)
    key_grad_seq = jnp.concatenate(grad_blocks, axis=1)
    image_count = starts_img.shape[0]
    held = image_held(jnp.arange(image_count, dtype=jnp.int32), image_count)
    starts_blk = starts_img[held]
    lens_blk = lens_img[held]
    row_ids = jnp.arange(TOK_DEV, dtype=jnp.int32)
    targets = jnp.clip(starts_blk[:, None] + row_ids[None, :], 0, SEQLEN - 1).reshape(-1).astype(jnp.int32)
    is_valid = (row_ids[None, :] < lens_blk[:, None]).reshape(-1)
    image_grad = jnp.where(is_valid[:, None], key_grad_seq[targets], 0.0).astype(jnp.bfloat16)
    feature_grad = jnp.dot(image_grad, key_value_proj.T, preferred_element_type=jnp.float32)
    _, pull_back = jax.vjp(lambda inputs: normed(inputs, vis_gain), vis_rows.astype(jnp.float32))
    vis_grad = pull_back(feature_grad)[0].astype(jnp.bfloat16)
    return (attended, vis_grad)
```

```python
import math

import jax
import jax.numpy as jnp
from jax import lax
from jax.sharding import PartitionSpec as P

HD = 128
EPS = 1e-06
NEG = -1e30


def owner_block(image, count):
    half = count // 2
    return image - half if image >= half else half + (image + 1) % half


def shift_rows(rows, shift, length, offset):
    count = rows.shape[0]
    r = lax.broadcasted_iota(jnp.int32, (count, count), 0)
    c = lax.broadcasted_iota(jnp.int32, (count, count), 1)
    pick = (c == r + offset) & (r + shift >= 0) & (r + shift < length)
    return jnp.dot(pick.astype(jnp.bfloat16), rows, preferred_element_type=jnp.float32)


def on_device(vis_rows, vis_gain, key_value_proj, pieces, text_kv, queries, grad_out):
    rows, width = vis_rows.shape
    group = queries.shape[1] // HD
    scale = 1.0 / math.sqrt(HD)
    seq_n = lax.axis_size("seq")
    me = lax.axis_index("seq")
    owners = [owner_block(j, seq_n) for j in range(seq_n)]
    held = [owners.index(b) for b in range(seq_n)]
    my_image = jnp.array(held, jnp.int32)[me]
    texts_len = pieces[0::2]

    text_in = [text_kv]
    for k in range(1, seq_n):
        text_in.append(lax.ppermute(text_kv, "seq", [(j, j + k) for j in range(seq_n - k)]))

    wide = vis_rows.astype(jnp.float32)
    inverse = lax.rsqrt(jnp.mean(wide * wide, axis=-1, keepdims=True) + EPS)
    normed = (wide * inverse * vis_gain).astype(jnp.bfloat16)
    image_kv = jnp.dot(normed, key_value_proj, preferred_element_type=jnp.float32).astype(jnp.bfloat16)

    rounds = []
    for k in range(seq_n):
        pairs = [(owners[j], j + k) for j in range(seq_n - k)]
        rounds.append([p for p in pairs if p[0] != p[1]])
    blocks = []
    for k in range(seq_n):
        got = jnp.zeros_like(image_kv)
        if rounds[k]:
            got = lax.ppermute(image_kv, "seq", rounds[k])
        if any(owners[j] == j + k for j in range(seq_n - k)):
            got = jnp.where(my_image == me - k, image_kv, got)
        before = texts_len[jnp.maximum(me - k, 0)]
        placed = shift_rows(got, -before, rows, -before).astype(jnp.bfloat16)
        row_ids = jnp.arange(rows, dtype=jnp.int32)
        blocks.append(jnp.where((row_ids < before)[:, None], text_in[k], placed))
    keys = jnp.concatenate([b[:, :HD] for b in blocks], axis=0)
    values = jnp.concatenate([b[:, HD:] for b in blocks], axis=0)

    q = queries.reshape(rows, group, HD)
    g = grad_out.reshape(rows, group, HD)
    scores = jnp.einsum("rhe,ke->hrk", q, keys, preferred_element_type=jnp.float32) * scale
    key_ids = jnp.arange(seq_n * rows, dtype=jnp.int32)
    row_ids = jnp.arange(rows, dtype=jnp.int32)
    block_ids = key_ids // rows
    allowed = jnp.where(block_ids == 0, key_ids[None, :] <= row_ids[:, None], (block_ids <= me)[None, :])
    scores = jnp.where(allowed[None], scores, NEG)
    top = jnp.max(scores, axis=-1, keepdims=True)
    weights = jnp.exp(scores - top)
    weights = weights / jnp.sum(weights, axis=-1, keepdims=True)
    low = weights.astype(jnp.bfloat16)
    mixed = jnp.einsum("hrk,ke->rhe", low, values, preferred_element_type=jnp.float32)
    drift = jnp.transpose(jnp.sum(g.astype(jnp.float32) * mixed, axis=-1))
    dprob = jnp.einsum("rhe,ke->hrk", g, values, preferred_element_type=jnp.float32)
    dscore = (weights * (dprob - drift[:, :, None]) * scale).astype(jnp.bfloat16)
    dkeys = jnp.einsum("hrk,rhe->ke", dscore, q, preferred_element_type=jnp.float32)
    dvalues = jnp.einsum("hrk,rhe->ke", low, g, preferred_element_type=jnp.float32)
    dkv = jnp.concatenate([dkeys, dvalues], axis=1).astype(jnp.bfloat16)
    attended = mixed.reshape(rows, group * HD).astype(jnp.bfloat16)

    total = jnp.zeros((rows, 2 * HD), jnp.float32)
    for k in range(seq_n):
        part = dkv[k * rows : (k + 1) * rows]
        if rounds[k]:
            total += lax.ppermute(part, "seq", [(d, s) for s, d in rounds[k]]).astype(jnp.float32)
        if any(owners[j] == j + k for j in range(seq_n - k)):
            total += jnp.where(my_image == me - k, part, 0).astype(jnp.float32)

    names = ("sec", "tp")
    tp_n = lax.axis_size("tp")
    n = lax.axis_size("sec") * tp_n
    piece = rows // n
    mine = lax.axis_index("sec") * tp_n + lax.axis_index("tp")
    odd = (mine // 2) % 2
    slot = lax.broadcasted_iota(jnp.int32, (rows, rows), 0)
    source = lax.broadcasted_iota(jnp.int32, (rows, rows), 1)
    q_id = slot // piece
    y_first = (q_id // 4) ^ odd == 1
    first = jnp.where(y_first, 1, 4)
    second = jnp.where(y_first, 4, 1)
    rel = (q_id // 4) * 2 + ((q_id // 2) % 2) * first + (q_id % 2) * second
    row = (rel ^ mine) * piece + slot % piece
    text_mine = texts_len[my_image]
    pick = (source == row + text_mine) & (row < rows - text_mine)
    image_grad = jnp.dot(pick.astype(jnp.bfloat16), total.astype(jnp.bfloat16), preferred_element_type=jnp.float32)
    image_grad = image_grad.astype(jnp.bfloat16)
    part = lax.dot_general(
        image_grad, key_value_proj, (((1,), (1,)), ((), ())), preferred_element_type=jnp.float32
    ).astype(jnp.bfloat16)

    core_pairs = [(i, i ^ 2) for i in range(n)]
    one = [(i, i ^ (1 if (i // 2) % 2 else 4)) for i in range(n)]
    two = [(i, i ^ (4 if (i // 2) % 2 else 1)) for i in range(n)]
    for pairs in (core_pairs, one, two):
        half = part.shape[0] // 2
        got = lax.ppermute(part[half:], names, pairs)
        part = (part[:half].astype(jnp.float32) + got.astype(jnp.float32)).astype(jnp.bfloat16)

    own = lax.dynamic_slice_in_dim(vis_rows, mine * piece, piece, 0).astype(jnp.float32)
    own_inverse = lax.rsqrt(jnp.mean(own * own, axis=-1, keepdims=True) + EPS)
    scaled = part.astype(jnp.float32) * vis_gain
    stat = jnp.mean(own * scaled, axis=-1, keepdims=True)
    out = (scaled * own_inverse - own * own_inverse * own_inverse * own_inverse * stat).astype(jnp.bfloat16)

    for pairs in (two, one, core_pairs):
        out = jnp.concatenate([out, lax.ppermute(out, names, pairs)], axis=0)
    dest = jnp.arange(n, dtype=jnp.int32) ^ mine
    bit_core, bit_x, bit_y = (dest // 2) % 2, dest // 4, dest % 2
    where_from = bit_core * 4 + jnp.where(odd ^ bit_core == 1, bit_y * 2 + bit_x, bit_x * 2 + bit_y)
    vis_grad = out.reshape(n, piece, width)[where_from].reshape(rows, width)
    return (attended, vis_grad)


def solution(mesh):
    in_specs = (
        P("seq", None),
        P(),
        P(None, ("sec", "tp")),
        P(),
        P("seq", ("sec", "tp")),
        P("seq", ("sec", "tp")),
        P("seq", ("sec", "tp")),
    )
    out_specs = (P("seq", ("sec", "tp")), P("seq", None))
    return jax.shard_map(
        on_device, mesh=mesh, in_specs=in_specs, out_specs=out_specs, check_vma=False
    )
```

```python
import functools
import math

import jax
import jax.numpy as jnp
from jax import lax
from jax.experimental import pallas as pl
from jax.experimental.pallas import tpu as pltpu
from jax.sharding import PartitionSpec as P

HD = 128
EPS = 1e-06
NEG = -1e30
VMEM_LIMIT = 48 * 1024 * 1024
WIDE_LIMIT = 60 * 1024 * 1024
WHOLE = pl.BlockSpec(memory_space=pltpu.VMEM)
SCALARS = pl.BlockSpec(memory_space=pltpu.SMEM)


def owner_block(image, count):
    half = count // 2
    return image - half if image >= half else half + (image + 1) % half


def held_image(block, count):
    half = count // 2
    return jnp.where(block < half, block + half, lax.rem(block + half - 1, half))


def group_place():
    sec, tp = lax.axis_index("sec"), lax.axis_index("tp")
    return lax.rem(sec, 2), lax.div(sec, 2) * lax.axis_size("tp") + tp


def dot(a, b, dims):
    return lax.dot_general(a, b, (dims, ((), ())), preferred_element_type=jnp.float32)


def call(body, out_shape, in_specs, out_specs, flops, moved, limit=VMEM_LIMIT, **more):
    return pl.pallas_call(
        body,
        out_shape=out_shape,
        in_specs=in_specs,
        out_specs=out_specs,
        compiler_params=pltpu.CompilerParams(vmem_limit_bytes=limit),
        cost_estimate=pl.CostEstimate(flops=flops, bytes_accessed=moved, transcendentals=0),
        **more,
    )


def cuts(width):
    size = max(width // (4 * 256), 1) * 256
    edges = [i * size for i in range(4)] + [width]
    return list(zip(edges[:-1], edges[1:]))


def project_body(piece, vis_hbm, gain_hbm, proj_hbm, kv_ref, own_ref, vis, gain_ref, proj, vis_sems, proj_sems, gain_sem):
    rows, width = vis.shape
    gain_copy = pltpu.make_async_copy(gain_hbm, gain_ref, gain_sem)
    gain_copy.start()
    copies = []
    for n, (low, high) in enumerate(cuts(width)):
        vis_copy = pltpu.make_async_copy(vis_hbm.at[:, low:high], vis.at[:, low:high], vis_sems.at[n])
        proj_copy = pltpu.make_async_copy(proj_hbm.at[low:high, :], proj.at[low:high, :], proj_sems.at[n])
        vis_copy.start()
        proj_copy.start()
        copies.append((vis_copy, proj_copy))
    gain_copy.wait()
    squares = jnp.zeros((rows, HD), jnp.float32)
    total = jnp.zeros(kv_ref.shape, jnp.float32)
    for (low, high), (vis_copy, proj_copy) in zip(cuts(width), copies):
        vis_copy.wait()
        scaled = []
        for c in range(low, high, HD):
            wide = vis[:, c : c + HD].astype(jnp.float32)
            squares += wide * wide
            scaled.append((wide * gain_ref[c // HD : c // HD + 1, :]).astype(jnp.bfloat16))
        proj_copy.wait()
        total += jnp.dot(jnp.concatenate(scaled, axis=1), proj[low:high, :], preferred_element_type=jnp.float32)
    inverse = lax.rsqrt(jnp.sum(squares, axis=1, keepdims=True) / width + EPS)
    kv_ref[...] = (total * inverse).astype(jnp.bfloat16)
    parity, place = group_place()
    start = pl.multiple_of(parity * (rows // 2) + place * piece, piece)
    own_ref[...] = vis[pl.ds(start, piece), :]


def place_body(seq_n, pieces_ref, image_ref, text_ref, out_ref):
    rows = image_ref.shape[0]
    before = pieces_ref[2 * held_image(lax.axis_index("seq"), seq_n)]
    to = lax.broadcasted_iota(jnp.int32, (rows, rows), 0)
    source = lax.broadcasted_iota(jnp.int32, (rows, rows), 1)
    pick = jnp.where(source == to - before, 1.0, 0.0).astype(jnp.bfloat16)
    moved = jnp.dot(pick, image_ref[...], preferred_element_type=jnp.float32)
    row = lax.broadcasted_iota(jnp.int32, moved.shape, 0)
    out_ref[...] = jnp.where(row < before, text_ref[...].astype(jnp.float32), moved).astype(jnp.bfloat16)


def pick_static(table, index):
    value = jnp.int32(table[0])
    for n in range(1, len(table)):
        value = jnp.where(index == n, table[n], value)
    return value


def attend_body(seq_n, tables, q_ref, g_ref, own_ref, *refs):
    got_refs, out_ref, grad_refs = refs[: len(tables)], refs[len(tables)], refs[len(tables) + 1 :]
    rows = q_ref.shape[0]
    group = q_ref.shape[1] // HD
    scale = 1.0 / math.sqrt(HD)
    me = lax.axis_index("seq")
    images = [held_image(me, seq_n)] + [pick_static(table, me) for table in tables]
    kv = jnp.concatenate([own_ref[...]] + [ref[...] for ref in got_refs], axis=0)
    keys, values = kv[:, :HD], kv[:, HD:]
    together = group if kv.shape[0] <= 1024 else 1
    span = together * rows
    offset = lax.broadcasted_iota(jnp.int32, (rows, span), 0)
    offset = offset - lax.rem(lax.broadcasted_iota(jnp.int32, (rows, span), 1), rows)
    masks = [offset <= (me - image) * rows for image in images]
    key_total = value_total = None
    for first in range(0, group, together):
        heads = range(first, first + together)
        q = jnp.concatenate([q_ref[:, h * HD : (h + 1) * HD] for h in heads], axis=0)
        g = jnp.concatenate([g_ref[:, h * HD : (h + 1) * HD] for h in heads], axis=0)
        scores = dot(keys, q, ((1,), (1,)))
        scores = jnp.concatenate(
            [jnp.where(mask, scores[n * rows : (n + 1) * rows], NEG) for n, mask in enumerate(masks)], axis=0
        )
        top = jnp.max(scores, axis=0, keepdims=True)
        weights = jnp.exp((scores - top) * scale)
        weights = weights * (1.0 / jnp.sum(weights, axis=0, keepdims=True))
        low = weights.astype(jnp.bfloat16)
        mixed = dot(values, low, ((0,), (0,)))
        dprob = dot(values, g, ((1,), (1,)))
        drift = jnp.sum(low.astype(jnp.float32) * dprob, axis=0, keepdims=True)
        dscore = (weights * (dprob - drift) * scale).astype(jnp.bfloat16)
        dkeys = jnp.dot(dscore, q, preferred_element_type=jnp.float32)
        dvalues = jnp.dot(low, g, preferred_element_type=jnp.float32)
        key_total = dkeys if key_total is None else key_total + dkeys
        value_total = dvalues if value_total is None else value_total + dvalues
        for n, h in enumerate(heads):
            part = jnp.transpose(mixed[:, n * rows : (n + 1) * rows])
            out_ref[:, h * HD : (h + 1) * HD] = part.astype(jnp.bfloat16)
    for n, ref in enumerate(grad_refs):
        ref[:, :HD] = key_total[n * rows : (n + 1) * rows].astype(jnp.bfloat16)
        ref[:, HD:] = value_total[n * rows : (n + 1) * rows].astype(jnp.bfloat16)


def back_body(seq_n, piece, pieces_ref, proj_ref, *refs):
    part_refs, (keep_ref, send_ref) = refs[:-2], refs[-2:]
    rows = part_refs[0].shape[0]
    half = rows // 2
    before = pieces_ref[2 * held_image(lax.axis_index("seq"), seq_n)]
    parity, place = group_place()
    total = part_refs[0][...].astype(jnp.float32)
    for ref in part_refs[1:]:
        total += ref[...].astype(jnp.float32)
    slot = lax.broadcasted_iota(jnp.int32, (rows, rows), 0)
    to = (lax.div(slot, half) ^ parity) * half
    to += (lax.div(lax.rem(slot, half), piece) ^ place) * piece + lax.rem(slot, piece)
    source = lax.broadcasted_iota(jnp.int32, (rows, rows), 1)
    pick = jnp.where(source == to + before, 1.0, 0.0).astype(jnp.bfloat16)
    image_grad = jnp.dot(pick, total.astype(jnp.bfloat16), preferred_element_type=jnp.float32)
    product = dot(image_grad.astype(jnp.bfloat16), proj_ref[...], ((1,), (1,)))
    keep_ref[...] = product[:half]
    send_ref[...] = product[half:].astype(jnp.bfloat16)


def pair_body(piece, keep_ref, other_ref, own_ref, *send_refs):
    own_ref[...] = keep_ref[:piece] + other_ref[:piece].astype(jnp.float32)
    for n, ref in enumerate(send_refs):
        part = slice((n + 1) * piece, (n + 2) * piece)
        ref[...] = (keep_ref[part] + other_ref[part].astype(jnp.float32)).astype(jnp.bfloat16)


def final_body(total_ref, own_ref, gain_ref, *refs):
    out_ref = refs[-1]
    width = own_ref.shape[1]
    square = stat = None
    scaled = []
    for c in range(0, width, HD):
        cols = slice(c, c + HD)
        total = total_ref[:, cols]
        for ref in refs[:-1]:
            total += ref[:, cols].astype(jnp.float32)
        own = own_ref[:, cols].astype(jnp.float32)
        grad = total * gain_ref[c // HD : c // HD + 1, :]
        scaled.append(grad)
        square = own * own if square is None else square + own * own
        stat = own * grad if stat is None else stat + own * grad
    inverse = lax.rsqrt(jnp.sum(square, axis=1, keepdims=True) / width + EPS)
    lead = inverse * inverse * inverse * (jnp.sum(stat, axis=1, keepdims=True) / width)
    for n, c in enumerate(range(0, width, HD)):
        own = own_ref[:, c : c + HD].astype(jnp.float32)
        out_ref[:, c : c + HD] = (scaled[n] * inverse - own * lead).astype(jnp.bfloat16)


def gather_body(count, *refs):
    part_refs, out_hbm, sems = refs[: 2 * count], refs[2 * count], refs[2 * count + 1]
    piece = part_refs[0].shape[0]
    parity, place = group_place()
    copies = []
    for n, ref in enumerate(part_refs):
        core, step = divmod(n, count)
        row = ((parity ^ core) * count + (place ^ step)) * piece
        copy = pltpu.make_async_copy(ref, out_hbm.at[pl.ds(pl.multiple_of(row, piece), piece), :], sems.at[n])
        copy.start()
        copies.append(copy)
    for copy in copies:
        copy.wait()


def rounds_of(edges):
    rounds = []
    for source, target in sorted(edges, key=lambda e: (-abs(e[0] - e[1]), e)):
        for pairs in rounds:
            if all(source != s and target != t for s, t in pairs):
                pairs.append((source, target))
                break
        else:
            rounds.append([(source, target)])
    return rounds


def on_device(vis_rows, vis_gain, key_value_proj, pieces, text_kv, queries, grad_out):
    rows, width = vis_rows.shape
    columns = key_value_proj.shape[1]
    seq_n = lax.axis_size("seq")
    tp_n = lax.axis_size("tp")
    n = lax.axis_size("sec") * tp_n
    count = n // 2
    piece = rows // n
    bf16, f32 = jnp.bfloat16, jnp.float32
    owners = [owner_block(j, seq_n) for j in range(seq_n)]
    names = ("sec", "tp")
    core_pairs = [(i, (i // tp_n ^ 1) * tp_n + i % tp_n) for i in range(n)]

    def far_pairs(step):
        pairs = []
        for i in range(n):
            sec, tp = divmod(i, tp_n)
            place = (sec // 2 * tp_n + tp) ^ step
            pairs.append((i, (place // tp_n * 2 + sec % 2) * tp_n + place % tp_n))
        return pairs

    gain = vis_gain.reshape(width // HD, HD)
    text = lax.ppermute(text_kv, "seq", [(j, owners[j]) for j in range(seq_n)])
    chunks = len(cuts(width))
    hbm = pl.BlockSpec(memory_space=pltpu.HBM)
    image_kv, own_rows = call(
        functools.partial(project_body, piece),
        [jax.ShapeDtypeStruct((rows, columns), bf16), jax.ShapeDtypeStruct((piece, width), bf16)],
        [hbm, hbm, hbm],
        [WHOLE, WHOLE],
        2 * rows * width * columns,
        2 * width * (rows + columns),
        limit=WIDE_LIMIT,
        scratch_shapes=[
            pltpu.VMEM((rows, width), bf16),
            pltpu.VMEM(gain.shape, f32),
            pltpu.VMEM((width, columns), bf16),
            pltpu.SemaphoreType.DMA((chunks,)),
            pltpu.SemaphoreType.DMA((chunks,)),
            pltpu.SemaphoreType.DMA,
        ],
    )(vis_rows, gain, key_value_proj)
    block = call(
        functools.partial(place_body, seq_n),
        jax.ShapeDtypeStruct((rows, columns), bf16),
        [SCALARS, WHOLE, WHOLE],
        WHOLE,
        2 * rows * rows * columns,
        6 * rows * columns,
    )(pieces, image_kv, text)

    rounds = rounds_of([(owners[j], s) for j in range(seq_n) for s in range(j, seq_n) if owners[j] != s])
    held = [owners.index(b) for b in range(seq_n)]
    tables = []
    for pairs in rounds:
        table = [seq_n] * seq_n
        for source, target in pairs:
            table[target] = held[source]
        tables.append(table)
    got = [lax.ppermute(block, "seq", pairs) for pairs in rounds]
    attended, own_grad, *grads = call(
        functools.partial(attend_body, seq_n, tables),
        [jax.ShapeDtypeStruct(queries.shape, bf16)] + [jax.ShapeDtypeStruct((rows, columns), bf16)] * (1 + len(got)),
        [WHOLE] * (3 + len(got)),
        [WHOLE] * (2 + len(got)),
        10 * seq_n * rows * rows * queries.shape[1],
        6 * rows * queries.shape[1] + 4 * seq_n * rows * columns,
    )(queries, grad_out, block, *got)
    parts = [lax.ppermute(g, "seq", [(t, s) for s, t in pairs]) for g, pairs in zip(grads, rounds)]

    keep, send = call(
        functools.partial(back_body, seq_n, piece),
        [jax.ShapeDtypeStruct((rows // 2, width), f32), jax.ShapeDtypeStruct((rows // 2, width), bf16)],
        [SCALARS] + [WHOLE] * (2 + len(parts)),
        [WHOLE, WHOLE],
        2 * rows * width * columns,
        2 * width * columns + 3 * rows * width,
    )(pieces, key_value_proj, own_grad, *parts)
    other = lax.ppermute(send, names, core_pairs)
    steps = list(range(1, count))
    own_sum, *sends = call(
        functools.partial(pair_body, piece),
        [jax.ShapeDtypeStruct((piece, width), f32)] + [jax.ShapeDtypeStruct((piece, width), bf16)] * len(steps),
        [WHOLE, WHOLE],
        [WHOLE] * count,
        0,
        6 * rows // 2 * width,
    )(keep, other)
    far_first = steps[::-1]
    shares = [lax.ppermute(sends[d - 1], names, far_pairs(d)) for d in far_first]
    mine = call(
        final_body,
        jax.ShapeDtypeStruct((piece, width), bf16),
        [WHOLE] * (3 + len(shares)),
        WHOLE,
        0,
        12 * piece * width,
    )(own_sum, own_rows, gain, *shares)
    mines = {0: mine}
    for d in far_first:
        mines[d] = lax.ppermute(mine, names, far_pairs(d))
    theirs = {d: lax.ppermute(mines[d], names, core_pairs) for d in [0] + far_first}
    vis_grad = call(
        functools.partial(gather_body, count),
        jax.ShapeDtypeStruct((rows, width), bf16),
        [WHOLE] * n,
        hbm,
        0,
        4 * rows * width,
        scratch_shapes=[pltpu.SemaphoreType.DMA((n,))],
    )(*[mines[d] for d in range(count)], *[theirs[d] for d in range(count)])
    return (attended, vis_grad)


def solution(mesh):
    in_specs = (
        P("seq", None),
        P(),
        P(None, ("sec", "tp")),
        P(),
        P("seq", ("sec", "tp")),
        P("seq", ("sec", "tp")),
        P("seq", ("sec", "tp")),
    )
    out_specs = (P("seq", ("sec", "tp")), P("seq", None))
    return jax.shard_map(
        on_device, mesh=mesh, in_specs=in_specs, out_specs=out_specs, check_vma=False
    )
```

```python
import functools
import math

import jax
import jax.numpy as jnp
from jax import lax
from jax.experimental import pallas as pl
from jax.experimental.pallas import tpu as pltpu
from jax.sharding import PartitionSpec as P

HD = 128
EPS = 1e-06
NEG = -1e30
VMEM_LIMIT = 48 * 1024 * 1024
WHOLE = pl.BlockSpec(memory_space=pltpu.VMEM)
SCALARS = pl.BlockSpec(memory_space=pltpu.SMEM)


def owner_block(image, count):
    half = count // 2
    return image - half if image >= half else half + (image + 1) % half


def held_image(block, count):
    half = count // 2
    return jnp.where(block < half, block + half, lax.rem(block + half - 1, half))


def group_place():
    sec, tp = lax.axis_index("sec"), lax.axis_index("tp")
    return lax.rem(sec, 2), lax.div(sec, 2) * lax.axis_size("tp") + tp


def dot(a, b, dims):
    return lax.dot_general(a, b, (dims, ((), ())), preferred_element_type=jnp.float32)


def call(body, out_shape, in_specs, out_specs, flops, moved, **more):
    return pl.pallas_call(
        body,
        out_shape=out_shape,
        in_specs=in_specs,
        out_specs=out_specs,
        compiler_params=pltpu.CompilerParams(vmem_limit_bytes=VMEM_LIMIT),
        cost_estimate=pl.CostEstimate(flops=flops, bytes_accessed=moved, transcendentals=0),
        **more,
    )


def cuts(width):
    size = max(width // (4 * 256), 1) * 256
    edges = [i * size for i in range(4)] + [width]
    return list(zip(edges[:-1], edges[1:]))


def project_body(piece, vis_hbm, gain_hbm, proj_hbm, kv_ref, own_ref, vis, gain_ref, proj, vis_sems, proj_sems, gain_sem):
    rows, width = vis.shape
    gain_copy = pltpu.make_async_copy(gain_hbm, gain_ref, gain_sem)
    gain_copy.start()
    copies = []
    for n, (low, high) in enumerate(cuts(width)):
        vis_copy = pltpu.make_async_copy(vis_hbm.at[:, low:high], vis.at[:, low:high], vis_sems.at[n])
        proj_copy = pltpu.make_async_copy(proj_hbm.at[low:high, :], proj.at[low:high, :], proj_sems.at[n])
        vis_copy.start()
        proj_copy.start()
        copies.append((vis_copy, proj_copy))
    gain_copy.wait()
    squares = jnp.zeros((rows, HD), jnp.float32)
    total = jnp.zeros(kv_ref.shape, jnp.float32)
    for (low, high), (vis_copy, proj_copy) in zip(cuts(width), copies):
        vis_copy.wait()
        scaled = []
        for c in range(low, high, HD):
            wide = vis[:, c : c + HD].astype(jnp.float32)
            squares += wide * wide
            scaled.append((wide * gain_ref[c // HD : c // HD + 1, :]).astype(jnp.bfloat16))
        proj_copy.wait()
        total += jnp.dot(jnp.concatenate(scaled, axis=1), proj[low:high, :], preferred_element_type=jnp.float32)
    inverse = lax.rsqrt(jnp.sum(squares, axis=1, keepdims=True) / width + EPS)
    kv_ref[...] = (total * inverse).astype(jnp.bfloat16)
    parity, place = group_place()
    start = pl.multiple_of(parity * (rows // 2) + place * piece, piece)
    own_ref[...] = vis[pl.ds(start, piece), :]


def place_body(seq_n, pieces_ref, image_ref, text_ref, out_ref):
    rows = image_ref.shape[0]
    before = pieces_ref[2 * held_image(lax.axis_index("seq"), seq_n)]
    to = lax.broadcasted_iota(jnp.int32, (rows, rows), 0)
    source = lax.broadcasted_iota(jnp.int32, (rows, rows), 1)
    pick = jnp.where(source == to - before, 1.0, 0.0).astype(jnp.bfloat16)
    moved = jnp.dot(pick, image_ref[...], preferred_element_type=jnp.float32)
    row = lax.broadcasted_iota(jnp.int32, moved.shape, 0)
    block = jnp.where(row < before, text_ref[...].astype(jnp.float32), moved).astype(jnp.bfloat16)
    for d in range(seq_n):
        out_ref[d] = block


def attend_body(seq_n, owners, q_ref, g_ref, kv_ref, out_ref, grad_ref):
    rows = q_ref.shape[0]
    group = q_ref.shape[1] // HD
    scale = 1.0 / math.sqrt(HD)
    me = lax.axis_index("seq")
    kv = jnp.concatenate([kv_ref[b] for b in owners], axis=0)
    keys, values = kv[:, :HD], kv[:, HD:]
    together = group if kv.shape[0] <= 1024 else 1
    span = together * rows
    offset = lax.broadcasted_iota(jnp.int32, (rows, span), 0)
    offset = offset - lax.rem(lax.broadcasted_iota(jnp.int32, (rows, span), 1), rows)
    masks = [offset <= (me - j) * rows for j in range(seq_n)]
    key_total = value_total = None
    for first in range(0, group, together):
        heads = range(first, first + together)
        q = jnp.concatenate([q_ref[:, h * HD : (h + 1) * HD] for h in heads], axis=0)
        g = jnp.concatenate([g_ref[:, h * HD : (h + 1) * HD] for h in heads], axis=0)
        scores = dot(keys, q, ((1,), (1,)))
        scores = jnp.concatenate(
            [jnp.where(mask, scores[n * rows : (n + 1) * rows], NEG) for n, mask in enumerate(masks)], axis=0
        )
        top = jnp.max(scores, axis=0, keepdims=True)
        weights = jnp.exp((scores - top) * scale)
        weights = weights * (1.0 / jnp.sum(weights, axis=0, keepdims=True))
        low = weights.astype(jnp.bfloat16)
        mixed = dot(values, low, ((0,), (0,)))
        dprob = dot(values, g, ((1,), (1,)))
        drift = jnp.sum(low.astype(jnp.float32) * dprob, axis=0, keepdims=True)
        dscore = (weights * (dprob - drift) * scale).astype(jnp.bfloat16)
        dkeys = jnp.dot(dscore, q, preferred_element_type=jnp.float32)
        dvalues = jnp.dot(low, g, preferred_element_type=jnp.float32)
        key_total = dkeys if key_total is None else key_total + dkeys
        value_total = dvalues if value_total is None else value_total + dvalues
        for n, h in enumerate(heads):
            part = jnp.transpose(mixed[:, n * rows : (n + 1) * rows])
            out_ref[:, h * HD : (h + 1) * HD] = part.astype(jnp.bfloat16)
    for j, b in enumerate(owners):
        grad_ref[b, :, :HD] = key_total[j * rows : (j + 1) * rows].astype(jnp.bfloat16)
        grad_ref[b, :, HD:] = value_total[j * rows : (j + 1) * rows].astype(jnp.bfloat16)


def back_body(seq_n, piece, pieces_ref, proj_ref, part_ref, keep_ref, send_ref):
    rows = part_ref.shape[1]
    half = rows // 2
    before = pieces_ref[2 * held_image(lax.axis_index("seq"), seq_n)]
    parity, place = group_place()
    total = part_ref[0].astype(jnp.float32)
    for b in range(1, seq_n):
        total += part_ref[b].astype(jnp.float32)
    slot = lax.broadcasted_iota(jnp.int32, (rows, rows), 0)
    to = (lax.div(slot, half) ^ parity) * half
    to += (lax.div(lax.rem(slot, half), piece) ^ place) * piece + lax.rem(slot, piece)
    source = lax.broadcasted_iota(jnp.int32, (rows, rows), 1)
    pick = jnp.where(source == to + before, 1.0, 0.0).astype(jnp.bfloat16)
    image_grad = jnp.dot(pick, total.astype(jnp.bfloat16), preferred_element_type=jnp.float32)
    product = dot(image_grad.astype(jnp.bfloat16), proj_ref[...], ((1,), (1,)))
    keep_ref[...] = product[:half]
    send_ref[...] = product[half:].astype(jnp.bfloat16)


def pair_body(piece, keep_ref, other_ref, own_ref, *send_refs):
    own_ref[...] = keep_ref[:piece] + other_ref[:piece].astype(jnp.float32)
    for n, ref in enumerate(send_refs):
        part = slice((n + 1) * piece, (n + 2) * piece)
        ref[...] = (keep_ref[part] + other_ref[part].astype(jnp.float32)).astype(jnp.bfloat16)


def final_body(total_ref, own_ref, gain_ref, *refs):
    out_ref = refs[-1]
    width = own_ref.shape[1]
    square = stat = None
    scaled = []
    for c in range(0, width, HD):
        cols = slice(c, c + HD)
        total = total_ref[:, cols]
        for ref in refs[:-1]:
            total += ref[:, cols].astype(jnp.float32)
        own = own_ref[:, cols].astype(jnp.float32)
        grad = total * gain_ref[c // HD : c // HD + 1, :]
        scaled.append(grad)
        square = own * own if square is None else square + own * own
        stat = own * grad if stat is None else stat + own * grad
    inverse = lax.rsqrt(jnp.sum(square, axis=1, keepdims=True) / width + EPS)
    lead = inverse * inverse * inverse * (jnp.sum(stat, axis=1, keepdims=True) / width)
    for n, c in enumerate(range(0, width, HD)):
        own = own_ref[:, c : c + HD].astype(jnp.float32)
        out_ref[:, c : c + HD] = (scaled[n] * inverse - own * lead).astype(jnp.bfloat16)


def gather_body(count, *refs):
    part_refs, out_hbm, sems = refs[: 2 * count], refs[2 * count], refs[2 * count + 1]
    piece = part_refs[0].shape[0]
    parity, place = group_place()
    copies = []
    for n, ref in enumerate(part_refs):
        core, step = divmod(n, count)
        row = ((parity ^ core) * count + (place ^ step)) * piece
        copy = pltpu.make_async_copy(ref, out_hbm.at[pl.ds(pl.multiple_of(row, piece), piece), :], sems.at[n])
        copy.start()
        copies.append(copy)
    for copy in copies:
        copy.wait()


def on_device(vis_rows, vis_gain, key_value_proj, pieces, text_kv, queries, grad_out):
    rows, width = vis_rows.shape
    columns = key_value_proj.shape[1]
    seq_n = lax.axis_size("seq")
    tp_n = lax.axis_size("tp")
    n = lax.axis_size("sec") * tp_n
    count = n // 2
    piece = rows // n
    bf16, f32 = jnp.bfloat16, jnp.float32
    owners = [owner_block(j, seq_n) for j in range(seq_n)]
    names = ("sec", "tp")
    core_pairs = [(i, (i // tp_n ^ 1) * tp_n + i % tp_n) for i in range(n)]

    def far_pairs(step):
        pairs = []
        for i in range(n):
            sec, tp = divmod(i, tp_n)
            place = (sec // 2 * tp_n + tp) ^ step
            pairs.append((i, (place // tp_n * 2 + sec % 2) * tp_n + place % tp_n))
        return pairs

    gain = vis_gain.reshape(width // HD, HD)
    text = lax.ppermute(text_kv, "seq", [(j, owners[j]) for j in range(seq_n)])
    chunks = len(cuts(width))
    hbm = pl.BlockSpec(memory_space=pltpu.HBM)
    image_kv, own_rows = call(
        functools.partial(project_body, piece),
        [jax.ShapeDtypeStruct((rows, columns), bf16), jax.ShapeDtypeStruct((piece, width), bf16)],
        [hbm, hbm, hbm],
        [WHOLE, WHOLE],
        2 * rows * width * columns,
        2 * width * (rows + columns),
        scratch_shapes=[
            pltpu.VMEM((rows, width), bf16),
            pltpu.VMEM(gain.shape, f32),
            pltpu.VMEM((width, columns), bf16),
            pltpu.SemaphoreType.DMA((chunks,)),
            pltpu.SemaphoreType.DMA((chunks,)),
            pltpu.SemaphoreType.DMA,
        ],
    )(vis_rows, gain, key_value_proj)
    copies = call(
        functools.partial(place_body, seq_n),
        jax.ShapeDtypeStruct((seq_n, rows, columns), bf16),
        [SCALARS, WHOLE, WHOLE],
        WHOLE,
        2 * rows * rows * columns,
        6 * rows * columns,
    )(pieces, image_kv, text)

    blocks = lax.all_to_all(copies, "seq", 0, 0)
    attended, grads = call(
        functools.partial(attend_body, seq_n, owners),
        [jax.ShapeDtypeStruct(queries.shape, bf16), jax.ShapeDtypeStruct(blocks.shape, bf16)],
        [WHOLE] * 3,
        [WHOLE, WHOLE],
        10 * seq_n * rows * rows * queries.shape[1],
        6 * rows * queries.shape[1] + 4 * seq_n * rows * columns,
    )(queries, grad_out, blocks)
    parts = lax.all_to_all(grads, "seq", 0, 0)

    keep, send = call(
        functools.partial(back_body, seq_n, piece),
        [jax.ShapeDtypeStruct((rows // 2, width), f32), jax.ShapeDtypeStruct((rows // 2, width), bf16)],
        [SCALARS, WHOLE, WHOLE],
        [WHOLE, WHOLE],
        2 * rows * width * columns,
        2 * width * columns + 3 * rows * width,
    )(pieces, key_value_proj, parts)
    other = lax.ppermute(send, names, core_pairs)
    steps = list(range(1, count))
    own_sum, *sends = call(
        functools.partial(pair_body, piece),
        [jax.ShapeDtypeStruct((piece, width), f32)] + [jax.ShapeDtypeStruct((piece, width), bf16)] * len(steps),
        [WHOLE, WHOLE],
        [WHOLE] * count,
        0,
        6 * rows // 2 * width,
    )(keep, other)
    far_first = steps[::-1]
    shares = [lax.ppermute(sends[d - 1], names, far_pairs(d)) for d in far_first]
    mine = call(
        final_body,
        jax.ShapeDtypeStruct((piece, width), bf16),
        [WHOLE] * (3 + len(shares)),
        WHOLE,
        0,
        12 * piece * width,
    )(own_sum, own_rows, gain, *shares)
    mines = {0: mine}
    for d in far_first:
        mines[d] = lax.ppermute(mine, names, far_pairs(d))
    theirs = {d: lax.ppermute(mines[d], names, core_pairs) for d in [0] + far_first}
    vis_grad = call(
        functools.partial(gather_body, count),
        jax.ShapeDtypeStruct((rows, width), bf16),
        [WHOLE] * n,
        hbm,
        0,
        4 * rows * width,
        scratch_shapes=[pltpu.SemaphoreType.DMA((n,))],
    )(*[mines[d] for d in range(count)], *[theirs[d] for d in range(count)])
    return (attended, vis_grad)


def solution(mesh):
    in_specs = (
        P("seq", None),
        P(),
        P(None, ("sec", "tp")),
        P(),
        P("seq", ("sec", "tp")),
        P("seq", ("sec", "tp")),
        P("seq", ("sec", "tp")),
    )
    out_specs = (P("seq", ("sec", "tp")), P("seq", None))
    return jax.shard_map(
        on_device, mesh=mesh, in_specs=in_specs, out_specs=out_specs, check_vma=False
    )
```

```python
import functools
import math

import jax
import jax.numpy as jnp
from jax import lax
from jax.experimental import pallas as pl
from jax.experimental.pallas import tpu as pltpu
from jax.sharding import PartitionSpec as P

HD = 128
EPS = 1e-06
NEG = -1e30
VMEM_LIMIT = 48 * 1024 * 1024
WIDE_LIMIT = 60 * 1024 * 1024
WHOLE = pl.BlockSpec(memory_space=pltpu.VMEM)
SCALARS = pl.BlockSpec(memory_space=pltpu.SMEM)


def owner_block(image, count):
    half = count // 2
    return image - half if image >= half else half + (image + 1) % half


def held_image(block, count):
    half = count // 2
    return jnp.where(block < half, block + half, lax.rem(block + half - 1, half))


def group_place():
    sec, tp = lax.axis_index("sec"), lax.axis_index("tp")
    return lax.rem(sec, 2), lax.div(sec, 2) * lax.axis_size("tp") + tp


def dot(a, b, dims):
    return lax.dot_general(a, b, (dims, ((), ())), preferred_element_type=jnp.float32)


def call(body, out_shape, in_specs, out_specs, flops, moved, limit=VMEM_LIMIT, **more):
    return pl.pallas_call(
        body,
        out_shape=out_shape,
        in_specs=in_specs,
        out_specs=out_specs,
        compiler_params=pltpu.CompilerParams(vmem_limit_bytes=limit),
        cost_estimate=pl.CostEstimate(flops=flops, bytes_accessed=moved, transcendentals=0),
        **more,
    )


def cuts(width):
    size = max(width // (4 * 256), 1) * 256
    edges = [i * size for i in range(4)] + [width]
    return list(zip(edges[:-1], edges[1:]))


def project_body(piece, vis_hbm, gain_hbm, proj_hbm, kv_ref, own_ref, vis, gain_ref, proj, vis_sems, proj_sems, gain_sem):
    rows, width = vis.shape
    gain_copy = pltpu.make_async_copy(gain_hbm, gain_ref, gain_sem)
    gain_copy.start()
    copies = []
    for n, (low, high) in enumerate(cuts(width)):
        vis_copy = pltpu.make_async_copy(vis_hbm.at[:, low:high], vis.at[:, low:high], vis_sems.at[n])
        proj_copy = pltpu.make_async_copy(proj_hbm.at[low:high, :], proj.at[low:high, :], proj_sems.at[n])
        vis_copy.start()
        proj_copy.start()
        copies.append((vis_copy, proj_copy))
    gain_copy.wait()
    squares = jnp.zeros((rows, HD), jnp.float32)
    total = jnp.zeros(kv_ref.shape, jnp.float32)
    for (low, high), (vis_copy, proj_copy) in zip(cuts(width), copies):
        vis_copy.wait()
        scaled = []
        for c in range(low, high, HD):
            wide = vis[:, c : c + HD].astype(jnp.float32)
            squares += wide * wide
            scaled.append((wide * gain_ref[c // HD : c // HD + 1, :]).astype(jnp.bfloat16))
        proj_copy.wait()
        total += jnp.dot(jnp.concatenate(scaled, axis=1), proj[low:high, :], preferred_element_type=jnp.float32)
    inverse = lax.rsqrt(jnp.sum(squares, axis=1, keepdims=True) / width + EPS)
    kv_ref[...] = (total * inverse).astype(jnp.bfloat16)
    parity, place = group_place()
    start = pl.multiple_of(parity * (rows // 2) + place * piece, piece)
    own_ref[...] = vis[pl.ds(start, piece), :]


def shift_body(seq_n, pieces_ref, image_ref, out_ref):
    rows = image_ref.shape[0]
    before = pieces_ref[2 * held_image(lax.axis_index("seq"), seq_n)]
    to = lax.broadcasted_iota(jnp.int32, (rows, rows), 0)
    source = lax.broadcasted_iota(jnp.int32, (rows, rows), 1)
    pick = jnp.where(source == to - before, 1.0, 0.0).astype(jnp.bfloat16)
    out_ref[...] = jnp.dot(pick, image_ref[...], preferred_element_type=jnp.float32).astype(jnp.bfloat16)


def place_body(seq_n, pieces_ref, image_ref, text_ref, out_ref):
    before = pieces_ref[2 * held_image(lax.axis_index("seq"), seq_n)]
    row = lax.broadcasted_iota(jnp.int32, image_ref.shape, 0)
    text, image = text_ref[...].astype(jnp.float32), image_ref[...].astype(jnp.float32)
    block = jnp.where(row < before, text, image).astype(jnp.bfloat16)
    for d in range(seq_n):
        out_ref[d] = block


def attend_body(seq_n, owners, q_ref, g_ref, kv_ref, out_ref, grad_ref):
    rows = q_ref.shape[0]
    group = q_ref.shape[1] // HD
    scale = 1.0 / math.sqrt(HD)
    me = lax.axis_index("seq")
    kv = jnp.concatenate([kv_ref[b] for b in owners], axis=0)
    keys, values = kv[:, :HD], kv[:, HD:]
    together = group if kv.shape[0] <= 1024 else 1
    span = together * rows
    offset = lax.broadcasted_iota(jnp.int32, (rows, span), 0)
    offset = offset - lax.rem(lax.broadcasted_iota(jnp.int32, (rows, span), 1), rows)
    masks = [offset <= (me - j) * rows for j in range(seq_n)]
    key_total = value_total = None
    for first in range(0, group, together):
        heads = range(first, first + together)
        q = jnp.concatenate([q_ref[:, h * HD : (h + 1) * HD] for h in heads], axis=0)
        g = jnp.concatenate([g_ref[:, h * HD : (h + 1) * HD] for h in heads], axis=0)
        scores = dot(keys, q, ((1,), (1,)))
        scores = jnp.concatenate(
            [jnp.where(mask, scores[n * rows : (n + 1) * rows], NEG) for n, mask in enumerate(masks)], axis=0
        )
        top = jnp.max(scores, axis=0, keepdims=True)
        weights = jnp.exp2((scores - top) * (scale * math.log2(math.e)))
        weights = weights * (1.0 / jnp.sum(weights, axis=0, keepdims=True))
        low = weights.astype(jnp.bfloat16)
        mixed = dot(values, low, ((0,), (0,)))
        dprob = dot(values, g, ((1,), (1,)))
        drift = jnp.sum(low.astype(jnp.float32) * dprob, axis=0, keepdims=True)
        dscore = (weights * (dprob - drift)).astype(jnp.bfloat16)
        dkeys = jnp.dot(dscore, q, preferred_element_type=jnp.float32)
        dvalues = jnp.dot(low, g, preferred_element_type=jnp.float32)
        key_total = dkeys if key_total is None else key_total + dkeys
        value_total = dvalues if value_total is None else value_total + dvalues
        for n, h in enumerate(heads):
            part = jnp.transpose(mixed[:, n * rows : (n + 1) * rows])
            out_ref[:, h * HD : (h + 1) * HD] = part.astype(jnp.bfloat16)
    for j, b in enumerate(owners):
        grad_ref[b, :, :HD] = (key_total[j * rows : (j + 1) * rows] * scale).astype(jnp.bfloat16)
        grad_ref[b, :, HD:] = value_total[j * rows : (j + 1) * rows].astype(jnp.bfloat16)


def back_body(seq_n, piece, pieces_ref, proj_ref, part_ref, keep_ref, send_ref):
    rows = part_ref.shape[1]
    half = rows // 2
    before = pieces_ref[2 * held_image(lax.axis_index("seq"), seq_n)]
    parity, place = group_place()
    total = part_ref[0].astype(jnp.float32)
    for b in range(1, seq_n):
        total += part_ref[b].astype(jnp.float32)
    slot = lax.broadcasted_iota(jnp.int32, (rows, rows), 0)
    to = (lax.div(slot, half) ^ parity) * half
    to += (lax.div(lax.rem(slot, half), piece) ^ place) * piece + lax.rem(slot, piece)
    source = lax.broadcasted_iota(jnp.int32, (rows, rows), 1)
    pick = jnp.where(source == to + before, 1.0, 0.0).astype(jnp.bfloat16)
    image_grad = jnp.dot(pick, total.astype(jnp.bfloat16), preferred_element_type=jnp.float32)
    product = dot(image_grad.astype(jnp.bfloat16), proj_ref[...], ((1,), (1,)))
    keep_ref[...] = product[:half]
    send_ref[...] = product[half:].astype(jnp.bfloat16)


def pair_body(piece, keep_ref, other_ref, own_ref, *send_refs):
    own_ref[...] = keep_ref[:piece] + other_ref[:piece].astype(jnp.float32)
    for n, ref in enumerate(send_refs):
        part = slice((n + 1) * piece, (n + 2) * piece)
        ref[...] = (keep_ref[part] + other_ref[part].astype(jnp.float32)).astype(jnp.bfloat16)


def final_body(total_ref, own_ref, gain_ref, *refs):
    out_ref = refs[-1]
    width = own_ref.shape[1]
    square = stat = None
    scaled = []
    for c in range(0, width, HD):
        cols = slice(c, c + HD)
        total = total_ref[:, cols]
        for ref in refs[:-1]:
            total += ref[:, cols].astype(jnp.float32)
        own = own_ref[:, cols].astype(jnp.float32)
        grad = total * gain_ref[c // HD : c // HD + 1, :]
        scaled.append(grad)
        square = own * own if square is None else square + own * own
        stat = own * grad if stat is None else stat + own * grad
    inverse = lax.rsqrt(jnp.sum(square, axis=1, keepdims=True) / width + EPS)
    lead = inverse * inverse * inverse * (jnp.sum(stat, axis=1, keepdims=True) / width)
    for n, c in enumerate(range(0, width, HD)):
        own = own_ref[:, c : c + HD].astype(jnp.float32)
        out_ref[:, c : c + HD] = (scaled[n] * inverse - own * lead).astype(jnp.bfloat16)


def gather_body(count, *refs):
    part_refs, out_hbm, sems = refs[: 2 * count], refs[2 * count], refs[2 * count + 1]
    piece = part_refs[0].shape[0]
    parity, place = group_place()
    copies = []
    for n, ref in enumerate(part_refs):
        core, step = n // count, count - 1 - n % count
        row = ((parity ^ core) * count + (place ^ step)) * piece
        copy = pltpu.make_async_copy(ref, out_hbm.at[pl.ds(pl.multiple_of(row, piece), piece), :], sems.at[n])
        copy.start()
        copies.append(copy)
    for copy in copies:
        copy.wait()


def on_device(vis_rows, vis_gain, key_value_proj, pieces, text_kv, queries, grad_out):
    rows, width = vis_rows.shape
    columns = key_value_proj.shape[1]
    seq_n = lax.axis_size("seq")
    tp_n = lax.axis_size("tp")
    n = lax.axis_size("sec") * tp_n
    count = n // 2
    piece = rows // n
    bf16, f32 = jnp.bfloat16, jnp.float32
    owners = [owner_block(j, seq_n) for j in range(seq_n)]
    names = ("sec", "tp")
    core_pairs = [(i, (i // tp_n ^ 1) * tp_n + i % tp_n) for i in range(n)]

    def far_pairs(step):
        pairs = []
        for i in range(n):
            sec, tp = divmod(i, tp_n)
            place = (sec // 2 * tp_n + tp) ^ step
            pairs.append((i, (place // tp_n * 2 + sec % 2) * tp_n + place % tp_n))
        return pairs

    gain = vis_gain.reshape(width // HD, HD)
    text = lax.ppermute(text_kv, "seq", [(j, owners[j]) for j in range(seq_n)])
    chunks = len(cuts(width))
    hbm = pl.BlockSpec(memory_space=pltpu.HBM)
    image_kv, own_rows = call(
        functools.partial(project_body, piece),
        [jax.ShapeDtypeStruct((rows, columns), bf16), jax.ShapeDtypeStruct((piece, width), bf16)],
        [hbm, hbm, hbm],
        [WHOLE, WHOLE],
        2 * rows * width * columns,
        2 * width * (rows + columns),
        limit=WIDE_LIMIT,
        scratch_shapes=[
            pltpu.VMEM((rows, width), bf16),
            pltpu.VMEM(gain.shape, f32),
            pltpu.VMEM((width, columns), bf16),
            pltpu.SemaphoreType.DMA((chunks,)),
            pltpu.SemaphoreType.DMA((chunks,)),
            pltpu.SemaphoreType.DMA,
        ],
    )(vis_rows, gain, key_value_proj)
    shifted = call(
        functools.partial(shift_body, seq_n),
        jax.ShapeDtypeStruct((rows, columns), bf16),
        [SCALARS, WHOLE],
        WHOLE,
        2 * rows * rows * columns,
        4 * rows * columns,
    )(pieces, image_kv)
    copies = call(
        functools.partial(place_body, seq_n),
        jax.ShapeDtypeStruct((seq_n, rows, columns), bf16),
        [SCALARS, WHOLE, WHOLE],
        WHOLE,
        0,
        6 * rows * columns,
    )(pieces, shifted, text)

    blocks = lax.all_to_all(copies, "seq", 0, 0)
    attended, grads = call(
        functools.partial(attend_body, seq_n, owners),
        [jax.ShapeDtypeStruct(queries.shape, bf16), jax.ShapeDtypeStruct(blocks.shape, bf16)],
        [WHOLE] * 3,
        [WHOLE, WHOLE],
        10 * seq_n * rows * rows * queries.shape[1],
        6 * rows * queries.shape[1] + 4 * seq_n * rows * columns,
    )(queries, grad_out, blocks)
    parts = lax.all_to_all(grads, "seq", 0, 0)

    keep, send = call(
        functools.partial(back_body, seq_n, piece),
        [jax.ShapeDtypeStruct((rows // 2, width), f32), jax.ShapeDtypeStruct((rows // 2, width), bf16)],
        [SCALARS, WHOLE, WHOLE],
        [WHOLE, WHOLE],
        2 * rows * width * columns,
        2 * width * columns + 3 * rows * width,
    )(pieces, key_value_proj, parts)
    other = lax.ppermute(send, names, core_pairs)
    steps = list(range(1, count))
    own_sum, *sends = call(
        functools.partial(pair_body, piece),
        [jax.ShapeDtypeStruct((piece, width), f32)] + [jax.ShapeDtypeStruct((piece, width), bf16)] * len(steps),
        [WHOLE, WHOLE],
        [WHOLE] * count,
        0,
        6 * rows // 2 * width,
    )(keep, other)
    shares = [lax.ppermute(sends[d - 1], names, far_pairs(d)) for d in steps]
    mine = call(
        final_body,
        jax.ShapeDtypeStruct((piece, width), bf16),
        [WHOLE] * (3 + len(shares)),
        WHOLE,
        0,
        12 * piece * width,
    )(own_sum, own_rows, gain, *shares)
    mines = {0: mine}
    for d in steps:
        mines[d] = lax.ppermute(mine, names, far_pairs(d))
    theirs = {d: lax.ppermute(mines[d], names, core_pairs) for d in range(count)}
    vis_grad = call(
        functools.partial(gather_body, count),
        jax.ShapeDtypeStruct((rows, width), bf16),
        [WHOLE] * n,
        hbm,
        0,
        4 * rows * width,
        scratch_shapes=[pltpu.SemaphoreType.DMA((n,))],
    )(*[mines[d] for d in reversed(range(count))], *[theirs[d] for d in reversed(range(count))])
    return (attended, vis_grad)


def solution(mesh):
    in_specs = (
        P("seq", None),
        P(),
        P(None, ("sec", "tp")),
        P(),
        P("seq", ("sec", "tp")),
        P("seq", ("sec", "tp")),
        P("seq", ("sec", "tp")),
    )
    out_specs = (P("seq", ("sec", "tp")), P("seq", None))
    return jax.shard_map(
        on_device, mesh=mesh, in_specs=in_specs, out_specs=out_specs, check_vma=False
    )
```

```python
import functools
import math

import jax
import jax.numpy as jnp
from jax import lax
from jax.experimental import pallas as pl
from jax.experimental.pallas import tpu as pltpu
from jax.sharding import PartitionSpec as P

HD = 128
EPS = 1e-06
NEG = -1e30
VMEM_LIMIT = 48 * 1024 * 1024
WIDE_LIMIT = 60 * 1024 * 1024
WHOLE = pl.BlockSpec(memory_space=pltpu.VMEM)
SCALARS = pl.BlockSpec(memory_space=pltpu.SMEM)


def held_image(block, count):
    half = count // 2
    return jnp.where(block < half, block + half, lax.rem(block + half - 1, half))


def group_place():
    sec, tp = lax.axis_index("sec"), lax.axis_index("tp")
    return lax.rem(sec, 2), lax.div(sec, 2) * lax.axis_size("tp") + tp


def dot(a, b, dims):
    return lax.dot_general(a, b, (dims, ((), ())), preferred_element_type=jnp.float32)


def call(body, out_shape, in_specs, out_specs, flops, moved, limit=VMEM_LIMIT, **more):
    return pl.pallas_call(
        body,
        out_shape=out_shape,
        in_specs=in_specs,
        out_specs=out_specs,
        compiler_params=pltpu.CompilerParams(vmem_limit_bytes=limit),
        cost_estimate=pl.CostEstimate(flops=flops, bytes_accessed=moved, transcendentals=0),
        **more,
    )


def cuts(width):
    size = max(width // (4 * 256), 1) * 256
    edges = [i * size for i in range(4)] + [width]
    return list(zip(edges[:-1], edges[1:]))


def project_body(piece, vis_hbm, gain_hbm, proj_hbm, kv_ref, own_ref, vis, gain_ref, proj, vis_sems, proj_sems, gain_sem):
    rows, width = vis.shape
    gain_copy = pltpu.make_async_copy(gain_hbm, gain_ref, gain_sem)
    gain_copy.start()
    copies = []
    for n, (low, high) in enumerate(cuts(width)):
        vis_copy = pltpu.make_async_copy(vis_hbm.at[:, low:high], vis.at[:, low:high], vis_sems.at[n])
        proj_copy = pltpu.make_async_copy(proj_hbm.at[low:high, :], proj.at[low:high, :], proj_sems.at[n])
        vis_copy.start()
        proj_copy.start()
        copies.append((vis_copy, proj_copy))
    gain_copy.wait()
    squares = jnp.zeros((rows, HD), jnp.float32)
    total = jnp.zeros(kv_ref.shape, jnp.float32)
    for (low, high), (vis_copy, proj_copy) in zip(cuts(width), copies):
        vis_copy.wait()
        scaled = []
        for c in range(low, high, HD):
            wide = vis[:, c : c + HD].astype(jnp.float32)
            squares += wide * wide
            scaled.append((wide * gain_ref[c // HD : c // HD + 1, :]).astype(jnp.bfloat16))
        proj_copy.wait()
        total += jnp.dot(jnp.concatenate(scaled, axis=1), proj[low:high, :], preferred_element_type=jnp.float32)
    inverse = lax.rsqrt(jnp.sum(squares, axis=1, keepdims=True) / width + EPS)
    kv_ref[...] = (total * inverse).astype(jnp.bfloat16)
    parity, place = group_place()
    start = pl.multiple_of(parity * (rows // 2) + place * piece, piece)
    own_ref[...] = vis[pl.ds(start, piece), :]


def attend_body(seq_n, pieces_ref, q_ref, g_ref, *refs):
    image_refs, text_refs = refs[:seq_n], refs[seq_n : 2 * seq_n]
    out_ref, grad_refs = refs[2 * seq_n], refs[2 * seq_n + 1 : 3 * seq_n + 1]
    image, text = refs[3 * seq_n + 1 :]
    rows = q_ref.shape[0]
    group = q_ref.shape[1] // HD
    scale = 1.0 / math.sqrt(HD)
    me = lax.axis_index("seq")
    for r in range(seq_n):
        image[held_image(me ^ r, seq_n)] = image_refs[r][...]
        text[me ^ r] = text_refs[r][...]
    ahead = lax.broadcasted_iota(jnp.int32, (rows, rows), 0) - lax.broadcasted_iota(jnp.int32, (rows, rows), 1)
    row = lax.broadcasted_iota(jnp.int32, image.shape[1:], 0)
    blocks = []
    for j in range(seq_n):
        before = pieces_ref[2 * j]
        pick = jnp.where(ahead == before, 1.0, 0.0).astype(jnp.bfloat16)
        placed = jnp.dot(pick, image[j], preferred_element_type=jnp.float32)
        blocks.append(jnp.where(row < before, text[j].astype(jnp.float32), placed).astype(jnp.bfloat16))
    kv = jnp.concatenate(blocks, axis=0)
    keys, values = kv[:, :HD], kv[:, HD:]
    together = group if kv.shape[0] <= 1024 else 1
    span = together * rows
    offset = lax.broadcasted_iota(jnp.int32, (rows, span), 0)
    offset = offset - lax.rem(lax.broadcasted_iota(jnp.int32, (rows, span), 1), rows)
    masks = [offset <= (me - j) * rows for j in range(seq_n)]
    key_total = value_total = None
    for first in range(0, group, together):
        heads = range(first, first + together)
        q = jnp.concatenate([q_ref[:, h * HD : (h + 1) * HD] for h in heads], axis=0)
        g = jnp.concatenate([g_ref[:, h * HD : (h + 1) * HD] for h in heads], axis=0)
        scores = dot(keys, q, ((1,), (1,)))
        scores = jnp.concatenate(
            [jnp.where(mask, scores[n * rows : (n + 1) * rows], NEG) for n, mask in enumerate(masks)], axis=0
        )
        top = jnp.max(scores, axis=0, keepdims=True)
        weights = jnp.exp2((scores - top) * (scale * math.log2(math.e)))
        weights = weights * (1.0 / jnp.sum(weights, axis=0, keepdims=True))
        low = weights.astype(jnp.bfloat16)
        mixed = dot(values, low, ((0,), (0,)))
        dprob = dot(values, g, ((1,), (1,)))
        drift = jnp.sum(low.astype(jnp.float32) * dprob, axis=0, keepdims=True)
        dscore = (weights * (dprob - drift)).astype(jnp.bfloat16)
        dkeys = jnp.dot(dscore, q, preferred_element_type=jnp.float32)
        dvalues = jnp.dot(low, g, preferred_element_type=jnp.float32)
        key_total = dkeys if key_total is None else key_total + dkeys
        value_total = dvalues if value_total is None else value_total + dvalues
        for n, h in enumerate(heads):
            part = jnp.transpose(mixed[:, n * rows : (n + 1) * rows])
            out_ref[:, h * HD : (h + 1) * HD] = part.astype(jnp.bfloat16)
    for j in range(seq_n):
        image[j, :, :HD] = (key_total[j * rows : (j + 1) * rows] * scale).astype(jnp.bfloat16)
        image[j, :, HD:] = value_total[j * rows : (j + 1) * rows].astype(jnp.bfloat16)
    for r, ref in enumerate(grad_refs):
        ref[...] = image[held_image(me ^ r, seq_n)]


def back_body(seq_n, piece, pieces_ref, proj_ref, *refs):
    part_refs, (keep_ref, send_ref) = refs[:-2], refs[-2:]
    rows = part_refs[0].shape[0]
    half = rows // 2
    before = pieces_ref[2 * held_image(lax.axis_index("seq"), seq_n)]
    parity, place = group_place()
    total = part_refs[0][...].astype(jnp.float32)
    for ref in part_refs[1:]:
        total += ref[...].astype(jnp.float32)
    slot = lax.broadcasted_iota(jnp.int32, (rows, rows), 0)
    to = (lax.div(slot, half) ^ parity) * half
    to += (lax.div(lax.rem(slot, half), piece) ^ place) * piece + lax.rem(slot, piece)
    source = lax.broadcasted_iota(jnp.int32, (rows, rows), 1)
    pick = jnp.where(source == to + before, 1.0, 0.0).astype(jnp.bfloat16)
    image_grad = jnp.dot(pick, total.astype(jnp.bfloat16), preferred_element_type=jnp.float32)
    product = dot(image_grad.astype(jnp.bfloat16), proj_ref[...], ((1,), (1,)))
    keep_ref[...] = product[:half]
    send_ref[...] = product[half:].astype(jnp.bfloat16)


def pair_body(piece, keep_ref, other_ref, own_ref, *send_refs):
    own_ref[...] = keep_ref[:piece] + other_ref[:piece].astype(jnp.float32)
    for n, ref in enumerate(send_refs):
        part = slice((n + 1) * piece, (n + 2) * piece)
        ref[...] = (keep_ref[part] + other_ref[part].astype(jnp.float32)).astype(jnp.bfloat16)


def final_body(total_ref, own_ref, gain_ref, *refs):
    out_ref = refs[-1]
    width = own_ref.shape[1]
    square = stat = None
    scaled = []
    for c in range(0, width, HD):
        cols = slice(c, c + HD)
        total = total_ref[:, cols]
        for ref in refs[:-1]:
            total += ref[:, cols].astype(jnp.float32)
        own = own_ref[:, cols].astype(jnp.float32)
        grad = total * gain_ref[c // HD : c // HD + 1, :]
        scaled.append(grad)
        square = own * own if square is None else square + own * own
        stat = own * grad if stat is None else stat + own * grad
    inverse = lax.rsqrt(jnp.sum(square, axis=1, keepdims=True) / width + EPS)
    lead = inverse * inverse * inverse * (jnp.sum(stat, axis=1, keepdims=True) / width)
    for n, c in enumerate(range(0, width, HD)):
        own = own_ref[:, c : c + HD].astype(jnp.float32)
        out_ref[:, c : c + HD] = (scaled[n] * inverse - own * lead).astype(jnp.bfloat16)


def gather_body(count, *refs):
    part_refs, out_hbm, sems = refs[: 2 * count], refs[2 * count], refs[2 * count + 1]
    piece = part_refs[0].shape[0]
    parity, place = group_place()
    copies = []
    for n, ref in enumerate(part_refs):
        core, step = n // count, count - 1 - n % count
        row = ((parity ^ core) * count + (place ^ step)) * piece
        copy = pltpu.make_async_copy(ref, out_hbm.at[pl.ds(pl.multiple_of(row, piece), piece), :], sems.at[n])
        copy.start()
        copies.append(copy)
    for copy in copies:
        copy.wait()


def on_device(vis_rows, vis_gain, key_value_proj, pieces, text_kv, queries, grad_out):
    rows, width = vis_rows.shape
    columns = key_value_proj.shape[1]
    seq_n = lax.axis_size("seq")
    tp_n = lax.axis_size("tp")
    n = lax.axis_size("sec") * tp_n
    count = n // 2
    piece = rows // n
    bf16, f32 = jnp.bfloat16, jnp.float32
    names = ("sec", "tp")
    core_pairs = [(i, (i // tp_n ^ 1) * tp_n + i % tp_n) for i in range(n)]

    def far_pairs(step):
        pairs = []
        for i in range(n):
            sec, tp = divmod(i, tp_n)
            place = (sec // 2 * tp_n + tp) ^ step
            pairs.append((i, (place // tp_n * 2 + sec % 2) * tp_n + place % tp_n))
        return pairs

    gain = vis_gain.reshape(width // HD, HD)
    far = sorted(range(1, seq_n), reverse=True)
    partners = {r: [(d, d ^ r) for d in range(seq_n)] for r in far}
    text = {r: lax.ppermute(text_kv, "seq", partners[r]) for r in far}
    text[0] = text_kv
    chunks = len(cuts(width))
    hbm = pl.BlockSpec(memory_space=pltpu.HBM)
    image_kv, own_rows = call(
        functools.partial(project_body, piece),
        [jax.ShapeDtypeStruct((rows, columns), bf16), jax.ShapeDtypeStruct((piece, width), bf16)],
        [hbm, hbm, hbm],
        [WHOLE, WHOLE],
        2 * rows * width * columns,
        2 * width * (rows + columns),
        limit=WIDE_LIMIT,
        scratch_shapes=[
            pltpu.VMEM((rows, width), bf16),
            pltpu.VMEM(gain.shape, f32),
            pltpu.VMEM((width, columns), bf16),
            pltpu.SemaphoreType.DMA((chunks,)),
            pltpu.SemaphoreType.DMA((chunks,)),
            pltpu.SemaphoreType.DMA,
        ],
    )(vis_rows, gain, key_value_proj)
    image = {r: lax.ppermute(image_kv, "seq", partners[r]) for r in far}
    image[0] = image_kv
    order = range(seq_n)
    attended, *grads = call(
        functools.partial(attend_body, seq_n),
        [jax.ShapeDtypeStruct(queries.shape, bf16)] + [jax.ShapeDtypeStruct((rows, columns), bf16)] * seq_n,
        [SCALARS] + [WHOLE] * (2 + 2 * seq_n),
        [WHOLE] * (1 + seq_n),
        10 * seq_n * rows * rows * queries.shape[1],
        6 * rows * queries.shape[1] + 4 * seq_n * rows * columns,
        scratch_shapes=[pltpu.VMEM((seq_n, rows, columns), bf16)] * 2,
    )(pieces, queries, grad_out, *[image[r] for r in order], *[text[r] for r in order])
    parts = {r: lax.ppermute(grads[r], "seq", partners[r]) for r in far}
    parts[0] = grads[0]

    keep, send = call(
        functools.partial(back_body, seq_n, piece),
        [jax.ShapeDtypeStruct((rows // 2, width), f32), jax.ShapeDtypeStruct((rows // 2, width), bf16)],
        [SCALARS] + [WHOLE] * (1 + seq_n),
        [WHOLE, WHOLE],
        2 * rows * width * columns,
        2 * width * columns + 3 * rows * width,
    )(pieces, key_value_proj, parts[0], *[parts[r] for r in far])
    other = lax.ppermute(send, names, core_pairs)
    steps = list(range(1, count))
    own_sum, *sends = call(
        functools.partial(pair_body, piece),
        [jax.ShapeDtypeStruct((piece, width), f32)] + [jax.ShapeDtypeStruct((piece, width), bf16)] * len(steps),
        [WHOLE, WHOLE],
        [WHOLE] * count,
        0,
        6 * rows // 2 * width,
    )(keep, other)
    shares = [lax.ppermute(sends[d - 1], names, far_pairs(d)) for d in steps]
    mine = call(
        final_body,
        jax.ShapeDtypeStruct((piece, width), bf16),
        [WHOLE] * (3 + len(shares)),
        WHOLE,
        0,
        12 * piece * width,
    )(own_sum, own_rows, gain, *shares)
    mines = {0: mine}
    for d in steps:
        mines[d] = lax.ppermute(mine, names, far_pairs(d))
    theirs = {d: lax.ppermute(mines[d], names, core_pairs) for d in range(count)}
    vis_grad = call(
        functools.partial(gather_body, count),
        jax.ShapeDtypeStruct((rows, width), bf16),
        [WHOLE] * n,
        hbm,
        0,
        4 * rows * width,
        scratch_shapes=[pltpu.SemaphoreType.DMA((n,))],
    )(*[mines[d] for d in reversed(range(count))], *[theirs[d] for d in reversed(range(count))])
    return (attended, vis_grad)


def solution(mesh):
    in_specs = (
        P("seq", None),
        P(),
        P(None, ("sec", "tp")),
        P(),
        P("seq", ("sec", "tp")),
        P("seq", ("sec", "tp")),
        P("seq", ("sec", "tp")),
    )
    out_specs = (P("seq", ("sec", "tp")), P("seq", None))
    return jax.shard_map(
        on_device, mesh=mesh, in_specs=in_specs, out_specs=out_specs, check_vma=False
    )
```

```python
import functools
import math

import jax
import jax.numpy as jnp
from jax import lax
from jax.experimental import pallas as pl
from jax.experimental.pallas import tpu as pltpu
from jax.sharding import PartitionSpec as P

HD = 128
EPS = 1e-06
NEG = -1e30
VMEM_LIMIT = 48 * 1024 * 1024
WIDE_LIMIT = 854 * 64 * 1024
WHOLE = pl.BlockSpec(memory_space=pltpu.VMEM)
SCALARS = pl.BlockSpec(memory_space=pltpu.SMEM)


def owner_block(image, count):
    half = count // 2
    return image - half if image >= half else half + (image + 1) % half


def held_image(block, count):
    half = count // 2
    return jnp.where(block < half, block + half, lax.rem(block + half - 1, half))


def group_place():
    sec, tp = lax.axis_index("sec"), lax.axis_index("tp")
    return lax.rem(sec, 2), lax.div(sec, 2) * lax.axis_size("tp") + tp


def dot(a, b, dims):
    return lax.dot_general(a, b, (dims, ((), ())), preferred_element_type=jnp.float32)


def call(body, out_shape, in_specs, out_specs, flops, moved, limit=VMEM_LIMIT, **more):
    return pl.pallas_call(
        body,
        out_shape=out_shape,
        in_specs=in_specs,
        out_specs=out_specs,
        compiler_params=pltpu.CompilerParams(vmem_limit_bytes=limit),
        cost_estimate=pl.CostEstimate(flops=flops, bytes_accessed=moved, transcendentals=0),
        **more,
    )


def cuts(width):
    size = max(width // (4 * 256), 1) * 256
    edges = [i * size for i in range(4)] + [width]
    return list(zip(edges[:-1], edges[1:]))


def project_body(piece, vis_hbm, gain_hbm, proj_hbm, kv_ref, own_ref, vis, gain_ref, proj, vis_sems, proj_sems, gain_sem):
    rows, width = vis.shape
    gain_copy = pltpu.make_async_copy(gain_hbm, gain_ref, gain_sem)
    gain_copy.start()
    copies = []
    for n, (low, high) in enumerate(cuts(width)):
        vis_copy = pltpu.make_async_copy(vis_hbm.at[:, low:high], vis.at[:, low:high], vis_sems.at[n])
        proj_copy = pltpu.make_async_copy(proj_hbm.at[low:high, :], proj.at[low:high, :], proj_sems.at[n])
        vis_copy.start()
        proj_copy.start()
        copies.append((vis_copy, proj_copy))
    gain_copy.wait()
    squares = jnp.zeros((rows, HD), jnp.float32)
    total = jnp.zeros(kv_ref.shape, jnp.float32)
    for (low, high), (vis_copy, proj_copy) in zip(cuts(width), copies):
        vis_copy.wait()
        scaled = []
        for c in range(low, high, HD):
            wide = vis[:, c : c + HD].astype(jnp.float32)
            squares += wide * wide
            scaled.append((wide * gain_ref[c // HD : c // HD + 1, :]).astype(jnp.bfloat16))
        proj_copy.wait()
        total += jnp.dot(jnp.concatenate(scaled, axis=1), proj[low:high, :], preferred_element_type=jnp.float32)
    inverse = lax.rsqrt(jnp.sum(squares, axis=1, keepdims=True) / width + EPS)
    kv_ref[...] = (total * inverse).astype(jnp.bfloat16)
    parity, place = group_place()
    start = pl.multiple_of(parity * (rows // 2) + place * piece, piece)
    own_ref[...] = vis[pl.ds(start, piece), :]


def shift_body(seq_n, pieces_ref, image_ref, out_ref):
    rows = image_ref.shape[0]
    before = pieces_ref[2 * held_image(lax.axis_index("seq"), seq_n)]
    to = lax.broadcasted_iota(jnp.int32, (rows, rows), 0)
    source = lax.broadcasted_iota(jnp.int32, (rows, rows), 1)
    pick = jnp.where(source == to - before, 1.0, 0.0).astype(jnp.bfloat16)
    out_ref[...] = jnp.dot(pick, image_ref[...], preferred_element_type=jnp.float32).astype(jnp.bfloat16)


def place_body(seq_n, pieces_ref, image_ref, text_ref, out_ref):
    before = pieces_ref[2 * held_image(lax.axis_index("seq"), seq_n)]
    row = lax.broadcasted_iota(jnp.int32, image_ref.shape, 0)
    text, image = text_ref[...].astype(jnp.float32), image_ref[...].astype(jnp.float32)
    out_ref[...] = jnp.where(row < before, text, image).astype(jnp.bfloat16)


def attend_body(seq_n, q_ref, g_ref, *refs):
    block_refs, out_ref, grad_refs = refs[:seq_n], refs[seq_n], refs[seq_n + 1 :]
    rows = q_ref.shape[0]
    group = q_ref.shape[1] // HD
    scale = 1.0 / math.sqrt(HD)
    me = lax.axis_index("seq")
    kv = jnp.concatenate([ref[...] for ref in block_refs], axis=0)
    keys, values = kv[:, :HD], kv[:, HD:]
    together = group if kv.shape[0] <= 1024 else 1
    span = together * rows
    offset = lax.broadcasted_iota(jnp.int32, (rows, span), 0)
    offset = offset - lax.rem(lax.broadcasted_iota(jnp.int32, (rows, span), 1), rows)
    masks = [offset <= (me - held_image(me ^ r, seq_n)) * rows for r in range(seq_n)]
    key_total = value_total = None
    for first in range(0, group, together):
        heads = range(first, first + together)
        q = jnp.concatenate([q_ref[:, h * HD : (h + 1) * HD] for h in heads], axis=0)
        g = jnp.concatenate([g_ref[:, h * HD : (h + 1) * HD] for h in heads], axis=0)
        scores = dot(keys, q, ((1,), (1,)))
        scores = jnp.concatenate(
            [jnp.where(mask, scores[n * rows : (n + 1) * rows], NEG) for n, mask in enumerate(masks)], axis=0
        )
        top = jnp.max(scores, axis=0, keepdims=True)
        weights = jnp.exp2((scores - top) * (scale * math.log2(math.e)))
        weights = weights * (1.0 / jnp.sum(weights, axis=0, keepdims=True))
        low = weights.astype(jnp.bfloat16)
        mixed = dot(values, low, ((0,), (0,)))
        dprob = dot(values, g, ((1,), (1,)))
        drift = jnp.sum(low.astype(jnp.float32) * dprob, axis=0, keepdims=True)
        dscore = (weights * (dprob - drift)).astype(jnp.bfloat16)
        dkeys = jnp.dot(dscore, q, preferred_element_type=jnp.float32)
        dvalues = jnp.dot(low, g, preferred_element_type=jnp.float32)
        key_total = dkeys if key_total is None else key_total + dkeys
        value_total = dvalues if value_total is None else value_total + dvalues
        for n, h in enumerate(heads):
            part = jnp.transpose(mixed[:, n * rows : (n + 1) * rows])
            out_ref[:, h * HD : (h + 1) * HD] = part.astype(jnp.bfloat16)
    for r, ref in enumerate(grad_refs):
        ref[:, :HD] = (key_total[r * rows : (r + 1) * rows] * scale).astype(jnp.bfloat16)
        ref[:, HD:] = value_total[r * rows : (r + 1) * rows].astype(jnp.bfloat16)


def back_body(seq_n, piece, pieces_ref, proj_ref, *refs):
    part_refs, (keep_ref, send_ref) = refs[:-2], refs[-2:]
    rows = part_refs[0].shape[0]
    half = rows // 2
    before = pieces_ref[2 * held_image(lax.axis_index("seq"), seq_n)]
    parity, place = group_place()
    total = part_refs[0][...].astype(jnp.float32)
    for ref in part_refs[1:]:
        total += ref[...].astype(jnp.float32)
    slot = lax.broadcasted_iota(jnp.int32, (rows, rows), 0)
    to = (lax.div(slot, half) ^ parity) * half
    to += (lax.div(lax.rem(slot, half), piece) ^ place) * piece + lax.rem(slot, piece)
    source = lax.broadcasted_iota(jnp.int32, (rows, rows), 1)
    pick = jnp.where(source == to + before, 1.0, 0.0).astype(jnp.bfloat16)
    image_grad = jnp.dot(pick, total.astype(jnp.bfloat16), preferred_element_type=jnp.float32)
    product = dot(image_grad.astype(jnp.bfloat16), proj_ref[...], ((1,), (1,)))
    keep_ref[...] = product[:half]
    send_ref[...] = product[half:].astype(jnp.bfloat16)


def pair_body(piece, keep_ref, other_ref, own_ref, *send_refs):
    own_ref[...] = keep_ref[:piece] + other_ref[:piece].astype(jnp.float32)
    for n, ref in enumerate(send_refs):
        part = slice((n + 1) * piece, (n + 2) * piece)
        ref[...] = (keep_ref[part] + other_ref[part].astype(jnp.float32)).astype(jnp.bfloat16)


def final_body(total_ref, own_ref, gain_ref, *refs):
    out_ref = refs[-1]
    width = own_ref.shape[1]
    square = stat = None
    scaled = []
    for c in range(0, width, HD):
        cols = slice(c, c + HD)
        total = total_ref[:, cols]
        for ref in refs[:-1]:
            total += ref[:, cols].astype(jnp.float32)
        own = own_ref[:, cols].astype(jnp.float32)
        grad = total * gain_ref[c // HD : c // HD + 1, :]
        scaled.append(grad)
        square = own * own if square is None else square + own * own
        stat = own * grad if stat is None else stat + own * grad
    inverse = lax.rsqrt(jnp.sum(square, axis=1, keepdims=True) / width + EPS)
    lead = inverse * inverse * inverse * (jnp.sum(stat, axis=1, keepdims=True) / width)
    for n, c in enumerate(range(0, width, HD)):
        own = own_ref[:, c : c + HD].astype(jnp.float32)
        out_ref[:, c : c + HD] = (scaled[n] * inverse - own * lead).astype(jnp.bfloat16)


def gather_body(count, *refs):
    part_refs, out_hbm, sems = refs[: 2 * count], refs[2 * count], refs[2 * count + 1]
    piece = part_refs[0].shape[0]
    parity, place = group_place()
    copies = []
    for n, ref in enumerate(part_refs):
        core, step = n // count, count - 1 - n % count
        row = ((parity ^ core) * count + (place ^ step)) * piece
        copy = pltpu.make_async_copy(ref, out_hbm.at[pl.ds(pl.multiple_of(row, piece), piece), :], sems.at[n])
        copy.start()
        copies.append(copy)
    for copy in copies:
        copy.wait()


def on_device(vis_rows, vis_gain, key_value_proj, pieces, text_kv, queries, grad_out):
    rows, width = vis_rows.shape
    columns = key_value_proj.shape[1]
    seq_n = lax.axis_size("seq")
    tp_n = lax.axis_size("tp")
    n = lax.axis_size("sec") * tp_n
    count = n // 2
    piece = rows // n
    bf16, f32 = jnp.bfloat16, jnp.float32
    names = ("sec", "tp")
    core_pairs = [(i, (i // tp_n ^ 1) * tp_n + i % tp_n) for i in range(n)]

    def far_pairs(step):
        pairs = []
        for i in range(n):
            sec, tp = divmod(i, tp_n)
            place = (sec // 2 * tp_n + tp) ^ step
            pairs.append((i, (place // tp_n * 2 + sec % 2) * tp_n + place % tp_n))
        return pairs

    gain = vis_gain.reshape(width // HD, HD)
    far = sorted(range(1, seq_n), reverse=True)
    partners = {r: [(d, d ^ r) for d in range(seq_n)] for r in far}
    text = lax.ppermute(text_kv, "seq", [(j, owner_block(j, seq_n)) for j in range(seq_n)])
    chunks = len(cuts(width))
    hbm = pl.BlockSpec(memory_space=pltpu.HBM)
    image_kv, own_rows = call(
        functools.partial(project_body, piece),
        [jax.ShapeDtypeStruct((rows, columns), bf16), jax.ShapeDtypeStruct((piece, width), bf16)],
        [hbm, hbm, hbm],
        [WHOLE, WHOLE],
        2 * rows * width * columns,
        2 * width * (rows + columns),
        limit=WIDE_LIMIT,
        scratch_shapes=[
            pltpu.VMEM((rows, width), bf16),
            pltpu.VMEM(gain.shape, f32),
            pltpu.VMEM((width, columns), bf16),
            pltpu.SemaphoreType.DMA((chunks,)),
            pltpu.SemaphoreType.DMA((chunks,)),
            pltpu.SemaphoreType.DMA,
        ],
    )(vis_rows, gain, key_value_proj)
    shifted = call(
        functools.partial(shift_body, seq_n),
        jax.ShapeDtypeStruct((rows, columns), bf16),
        [SCALARS, WHOLE],
        WHOLE,
        2 * rows * rows * columns,
        4 * rows * columns,
    )(pieces, image_kv)
    block = call(
        functools.partial(place_body, seq_n),
        jax.ShapeDtypeStruct((rows, columns), bf16),
        [SCALARS, WHOLE, WHOLE],
        WHOLE,
        0,
        6 * rows * columns,
    )(pieces, shifted, text)
    blocks = {r: lax.ppermute(block, "seq", partners[r]) for r in far}
    attended, *grads = call(
        functools.partial(attend_body, seq_n),
        [jax.ShapeDtypeStruct(queries.shape, bf16)] + [jax.ShapeDtypeStruct((rows, columns), bf16)] * seq_n,
        [WHOLE] * (2 + seq_n),
        [WHOLE] * (1 + seq_n),
        10 * seq_n * rows * rows * queries.shape[1],
        6 * rows * queries.shape[1] + 4 * seq_n * rows * columns,
    )(queries, grad_out, block, *[blocks[r] for r in range(1, seq_n)])
    parts = {r: lax.ppermute(grads[r], "seq", partners[r]) for r in far}
    parts[0] = grads[0]

    keep, send = call(
        functools.partial(back_body, seq_n, piece),
        [jax.ShapeDtypeStruct((rows // 2, width), f32), jax.ShapeDtypeStruct((rows // 2, width), bf16)],
        [SCALARS] + [WHOLE] * (1 + seq_n),
        [WHOLE, WHOLE],
        2 * rows * width * columns,
        2 * width * columns + 3 * rows * width,
    )(pieces, key_value_proj, parts[0], *[parts[r] for r in far])
    other = lax.ppermute(send, names, core_pairs)
    steps = list(range(1, count))
    own_sum, *sends = call(
        functools.partial(pair_body, piece),
        [jax.ShapeDtypeStruct((piece, width), f32)] + [jax.ShapeDtypeStruct((piece, width), bf16)] * len(steps),
        [WHOLE, WHOLE],
        [WHOLE] * count,
        0,
        6 * rows // 2 * width,
    )(keep, other)
    shares = [lax.ppermute(sends[d - 1], names, far_pairs(d)) for d in steps]
    mine = call(
        final_body,
        jax.ShapeDtypeStruct((piece, width), bf16),
        [WHOLE] * (3 + len(shares)),
        WHOLE,
        0,
        12 * piece * width,
    )(own_sum, own_rows, gain, *shares)
    mines = {0: mine}
    for d in steps:
        mines[d] = lax.ppermute(mine, names, far_pairs(d))
    theirs = {d: lax.ppermute(mines[d], names, core_pairs) for d in range(count)}
    vis_grad = call(
        functools.partial(gather_body, count),
        jax.ShapeDtypeStruct((rows, width), bf16),
        [WHOLE] * n,
        hbm,
        0,
        4 * rows * width,
        scratch_shapes=[pltpu.SemaphoreType.DMA((n,))],
    )(*[mines[d] for d in reversed(range(count))], *[theirs[d] for d in reversed(range(count))])
    return (attended, vis_grad)


def solution(mesh):
    in_specs = (
        P("seq", None),
        P(),
        P(None, ("sec", "tp")),
        P(),
        P("seq", ("sec", "tp")),
        P("seq", ("sec", "tp")),
        P("seq", ("sec", "tp")),
    )
    out_specs = (P("seq", ("sec", "tp")), P("seq", None))
    return jax.shard_map(
        on_device, mesh=mesh, in_specs=in_specs, out_specs=out_specs, check_vma=False
    )
```

```python
import functools
import math
import random

import jax
import jax.numpy as jnp
from jax import lax
from jax.experimental import pallas as pl
from jax.experimental.pallas import tpu as pltpu
from jax.sharding import PartitionSpec as P

HD = 128
EPS = 1e-06
NEG = -1e30
VMEM_LIMIT = 48 * 1024 * 1024
WIDE_LIMIT = 854 * 64 * 1024
WHOLE = pl.BlockSpec(memory_space=pltpu.VMEM)
SCALARS = pl.BlockSpec(memory_space=pltpu.SMEM)


def owner_block(image, count):
    half = count // 2
    return image - half if image >= half else half + (image + 1) % half


def held_image(block, count):
    half = count // 2
    return jnp.where(block < half, block + half, lax.rem(block + half - 1, half))


def colour(edges, count):
    sent, got = [{} for _ in range(count)], [{} for _ in range(count)]
    for s, t in edges:
        a = min(c for c in range(count) if c not in sent[s])
        b = min(c for c in range(count) if c not in got[t])
        if a != b:
            path, at, back, c = [], t, True, a
            while c in (got if back else sent)[at]:
                near = (got if back else sent)[at][c]
                path.append((near, at, c) if back else (at, near, c))
                at, back, c = near, not back, a + b - c
            for u, v, c in path:
                del sent[u][c], got[v][c]
            for u, v, c in path:
                sent[u][a + b - c], got[v][a + b - c] = v, u
        sent[s][a], got[t][a] = t, s
    return [{s: sent[s][c] for s in range(count) if c in sent[s]} for c in sorted({c for x in sent for c in x})]


def completed(pairs, count):
    sources = [s for s in range(count) if s not in pairs]
    targets = [t for t in range(count) if t not in pairs.values()]
    full = dict(pairs)
    for d in sources:
        if d in targets:
            full[d] = d
    full.update(zip([s for s in sources if s not in targets], [t for t in targets if t not in sources]))
    return full


def crossings(rounds, count):
    flows = [0] * (2 * count)
    for pairs in rounds:
        for s, t in completed(pairs, count).items():
            for k in range(min(s, t), max(s, t)):
                flows[2 * k + (t > s)] += 1
    return len(rounds), max(flows), sum(flows)


def rounds_of(edges, count):
    draw, tries = random.Random(0), [list(edges)]
    for _ in range(300 if count <= 8 else 0):
        tries.append(draw.sample(edges, len(edges)))
    return min((colour(order, count) for order in tries), key=lambda rounds: crossings(rounds, count))


def pick_static(table, index):
    value = jnp.int32(table[0])
    for n in range(1, len(table)):
        value = jnp.where(index == n, table[n], value)
    return value


def group_place():
    sec, tp = lax.axis_index("sec"), lax.axis_index("tp")
    return lax.rem(sec, 2), lax.div(sec, 2) * lax.axis_size("tp") + tp


def dot(a, b, dims):
    return lax.dot_general(a, b, (dims, ((), ())), preferred_element_type=jnp.float32)


def call(body, out_shape, in_specs, out_specs, flops, moved, limit=VMEM_LIMIT, **more):
    return pl.pallas_call(
        body,
        out_shape=out_shape,
        in_specs=in_specs,
        out_specs=out_specs,
        compiler_params=pltpu.CompilerParams(vmem_limit_bytes=limit),
        cost_estimate=pl.CostEstimate(flops=flops, bytes_accessed=moved, transcendentals=0),
        **more,
    )


def cuts(width):
    size = max(width // (4 * 256), 1) * 256
    edges = [i * size for i in range(4)] + [width]
    return list(zip(edges[:-1], edges[1:]))


def project_body(piece, vis_hbm, gain_hbm, proj_hbm, kv_ref, own_ref, vis, gain_ref, proj, vis_sems, proj_sems, gain_sem):
    rows, width = vis.shape
    gain_copy = pltpu.make_async_copy(gain_hbm, gain_ref, gain_sem)
    gain_copy.start()
    copies = []
    for n, (low, high) in enumerate(cuts(width)):
        vis_copy = pltpu.make_async_copy(vis_hbm.at[:, low:high], vis.at[:, low:high], vis_sems.at[n])
        proj_copy = pltpu.make_async_copy(proj_hbm.at[low:high, :], proj.at[low:high, :], proj_sems.at[n])
        vis_copy.start()
        proj_copy.start()
        copies.append((vis_copy, proj_copy))
    gain_copy.wait()
    squares = jnp.zeros((rows, HD), jnp.float32)
    total = jnp.zeros(kv_ref.shape, jnp.float32)
    for (low, high), (vis_copy, proj_copy) in zip(cuts(width), copies):
        vis_copy.wait()
        scaled = []
        for c in range(low, high, HD):
            wide = vis[:, c : c + HD].astype(jnp.float32)
            squares += wide * wide
            scaled.append((wide * gain_ref[c // HD : c // HD + 1, :]).astype(jnp.bfloat16))
        proj_copy.wait()
        total += jnp.dot(jnp.concatenate(scaled, axis=1), proj[low:high, :], preferred_element_type=jnp.float32)
    inverse = lax.rsqrt(jnp.sum(squares, axis=1, keepdims=True) / width + EPS)
    kv_ref[...] = (total * inverse).astype(jnp.bfloat16)
    parity, place = group_place()
    start = pl.multiple_of(parity * (rows // 2) + place * piece, piece)
    own_ref[...] = vis[pl.ds(start, piece), :]


def shift_body(seq_n, pieces_ref, image_ref, out_ref):
    rows = image_ref.shape[0]
    before = pieces_ref[2 * held_image(lax.axis_index("seq"), seq_n)]
    to = lax.broadcasted_iota(jnp.int32, (rows, rows), 0)
    source = lax.broadcasted_iota(jnp.int32, (rows, rows), 1)
    pick = jnp.where(source == to - before, 1.0, 0.0).astype(jnp.bfloat16)
    out_ref[...] = jnp.dot(pick, image_ref[...], preferred_element_type=jnp.float32).astype(jnp.bfloat16)


def place_body(seq_n, pieces_ref, image_ref, text_ref, out_ref):
    before = pieces_ref[2 * held_image(lax.axis_index("seq"), seq_n)]
    row = lax.broadcasted_iota(jnp.int32, image_ref.shape, 0)
    text, image = text_ref[...].astype(jnp.float32), image_ref[...].astype(jnp.float32)
    out_ref[...] = jnp.where(row < before, text, image).astype(jnp.bfloat16)


def attend_body(seq_n, tables, q_ref, g_ref, *refs):
    held = len(tables) + 1
    block_refs, out_ref, grad_refs = refs[:held], refs[held], refs[held + 1 :]
    rows = q_ref.shape[0]
    group = q_ref.shape[1] // HD
    scale = 1.0 / math.sqrt(HD)
    me = lax.axis_index("seq")
    kv = jnp.concatenate([ref[...] for ref in block_refs], axis=0)
    keys, values = kv[:, :HD], kv[:, HD:]
    together = group if kv.shape[0] <= 1024 else 1
    span = together * rows
    offset = lax.broadcasted_iota(jnp.int32, (rows, span), 0)
    offset = offset - lax.rem(lax.broadcasted_iota(jnp.int32, (rows, span), 1), rows)
    images = [held_image(me, seq_n)] + [pick_static(table, me) for table in tables]
    masks = [offset <= (me - image) * rows for image in images]
    key_total = value_total = None
    for first in range(0, group, together):
        heads = range(first, first + together)
        q = jnp.concatenate([q_ref[:, h * HD : (h + 1) * HD] for h in heads], axis=0)
        g = jnp.concatenate([g_ref[:, h * HD : (h + 1) * HD] for h in heads], axis=0)
        scores = dot(keys, q, ((1,), (1,)))
        scores = jnp.concatenate(
            [jnp.where(mask, scores[n * rows : (n + 1) * rows], NEG) for n, mask in enumerate(masks)], axis=0
        )
        top = jnp.max(scores, axis=0, keepdims=True)
        weights = jnp.exp2((scores - top) * (scale * math.log2(math.e)))
        weights = weights * (1.0 / jnp.sum(weights, axis=0, keepdims=True))
        low = weights.astype(jnp.bfloat16)
        mixed = dot(values, low, ((0,), (0,)))
        dprob = dot(values, g, ((1,), (1,)))
        drift = jnp.sum(low.astype(jnp.float32) * dprob, axis=0, keepdims=True)
        dscore = (weights * (dprob - drift)).astype(jnp.bfloat16)
        dkeys = jnp.dot(dscore, q, preferred_element_type=jnp.float32)
        dvalues = jnp.dot(low, g, preferred_element_type=jnp.float32)
        key_total = dkeys if key_total is None else key_total + dkeys
        value_total = dvalues if value_total is None else value_total + dvalues
        for n, h in enumerate(heads):
            part = jnp.transpose(mixed[:, n * rows : (n + 1) * rows])
            out_ref[:, h * HD : (h + 1) * HD] = part.astype(jnp.bfloat16)
    for r, ref in enumerate(grad_refs):
        ref[:, :HD] = (key_total[r * rows : (r + 1) * rows] * scale).astype(jnp.bfloat16)
        ref[:, HD:] = value_total[r * rows : (r + 1) * rows].astype(jnp.bfloat16)


def back_body(seq_n, piece, pieces_ref, proj_ref, *refs):
    part_refs, (grad_ref, send_ref) = refs[:-2], refs[-2:]
    rows = part_refs[0].shape[0]
    half = rows // 2
    before = pieces_ref[2 * held_image(lax.axis_index("seq"), seq_n)]
    parity, place = group_place()
    total = part_refs[0][...].astype(jnp.float32)
    for ref in part_refs[1:]:
        total += ref[...].astype(jnp.float32)
    slot = lax.broadcasted_iota(jnp.int32, (rows, rows), 0)
    to = (1 - (lax.div(slot, half) ^ parity)) * half
    to += (lax.div(lax.rem(slot, half), piece) ^ place) * piece + lax.rem(slot, piece)
    source = lax.broadcasted_iota(jnp.int32, (rows, rows), 1)
    pick = jnp.where(source == to + before, 1.0, 0.0).astype(jnp.bfloat16)
    image_grad = jnp.dot(pick, total.astype(jnp.bfloat16), preferred_element_type=jnp.float32)
    image_grad = image_grad.astype(jnp.bfloat16)
    send_ref[...] = dot(image_grad[:half], proj_ref[...], ((1,), (1,))).astype(jnp.bfloat16)
    grad_ref[...] = image_grad[half:]


def keep_body(grad_ref, proj_ref, keep_ref):
    keep_ref[...] = dot(grad_ref[...], proj_ref[...], ((1,), (1,)))


def pair_body(piece, keep_ref, other_ref, own_ref, *send_refs):
    own_ref[...] = keep_ref[:piece] + other_ref[:piece].astype(jnp.float32)
    for n, ref in enumerate(send_refs):
        part = slice((n + 1) * piece, (n + 2) * piece)
        ref[...] = (keep_ref[part] + other_ref[part].astype(jnp.float32)).astype(jnp.bfloat16)


def final_body(total_ref, own_ref, gain_ref, *refs):
    out_ref = refs[-1]
    width = own_ref.shape[1]
    square = stat = None
    scaled = []
    for c in range(0, width, HD):
        cols = slice(c, c + HD)
        total = total_ref[:, cols]
        for ref in refs[:-1]:
            total += ref[:, cols].astype(jnp.float32)
        own = own_ref[:, cols].astype(jnp.float32)
        grad = total * gain_ref[c // HD : c // HD + 1, :]
        scaled.append(grad)
        square = own * own if square is None else square + own * own
        stat = own * grad if stat is None else stat + own * grad
    inverse = lax.rsqrt(jnp.sum(square, axis=1, keepdims=True) / width + EPS)
    lead = inverse * inverse * inverse * (jnp.sum(stat, axis=1, keepdims=True) / width)
    for n, c in enumerate(range(0, width, HD)):
        own = own_ref[:, c : c + HD].astype(jnp.float32)
        out_ref[:, c : c + HD] = (scaled[n] * inverse - own * lead).astype(jnp.bfloat16)


def gather_body(count, core, *refs):
    part_refs, (out_hbm, sems) = refs[:count], refs[-2:]
    piece = part_refs[0].shape[0]
    parity, place = group_place()
    copies = []
    for n, ref in enumerate(part_refs):
        row = ((parity ^ core) * count + (place ^ (count - 1 - n))) * piece
        copy = pltpu.make_async_copy(ref, out_hbm.at[pl.ds(pl.multiple_of(row, piece), piece), :], sems.at[n])
        copy.start()
        copies.append(copy)
    for copy in copies:
        copy.wait()


def on_device(vis_rows, vis_gain, key_value_proj, pieces, text_kv, queries, grad_out):
    rows, width = vis_rows.shape
    columns = key_value_proj.shape[1]
    seq_n = lax.axis_size("seq")
    tp_n = lax.axis_size("tp")
    n = lax.axis_size("sec") * tp_n
    count = n // 2
    piece = rows // n
    bf16, f32 = jnp.bfloat16, jnp.float32
    names = ("sec", "tp")
    core_pairs = [(i, (i // tp_n ^ 1) * tp_n + i % tp_n) for i in range(n)]

    def far_pairs(step):
        pairs = []
        for i in range(n):
            sec, tp = divmod(i, tp_n)
            place = (sec // 2 * tp_n + tp) ^ step
            pairs.append((i, (place // tp_n * 2 + sec % 2) * tp_n + place % tp_n))
        return pairs

    gain = vis_gain.reshape(width // HD, HD)
    owners = [owner_block(j, seq_n) for j in range(seq_n)]
    held = [owners.index(b) for b in range(seq_n)]
    edges = [(owners[j], d) for j in range(seq_n) for d in range(j, seq_n) if owners[j] != d]
    rounds = rounds_of(edges, seq_n)
    forth = [sorted(completed(pairs, seq_n).items()) for pairs in rounds]
    tables = [[next((held[s] for s, t in pairs.items() if t == d), seq_n) for d in range(seq_n)] for pairs in rounds]
    text = lax.ppermute(text_kv, "seq", list(enumerate(owners)))
    chunks = len(cuts(width))
    hbm = pl.BlockSpec(memory_space=pltpu.HBM)
    image_kv, own_rows = call(
        functools.partial(project_body, piece),
        [jax.ShapeDtypeStruct((rows, columns), bf16), jax.ShapeDtypeStruct((piece, width), bf16)],
        [hbm, hbm, hbm],
        [WHOLE, WHOLE],
        2 * rows * width * columns,
        2 * width * (rows + columns),
        limit=WIDE_LIMIT,
        scratch_shapes=[
            pltpu.VMEM((rows, width), bf16),
            pltpu.VMEM(gain.shape, f32),
            pltpu.VMEM((width, columns), bf16),
            pltpu.SemaphoreType.DMA((chunks,)),
            pltpu.SemaphoreType.DMA((chunks,)),
            pltpu.SemaphoreType.DMA,
        ],
    )(vis_rows, gain, key_value_proj)
    shifted = call(
        functools.partial(shift_body, seq_n),
        jax.ShapeDtypeStruct((rows, columns), bf16),
        [SCALARS, WHOLE],
        WHOLE,
        2 * rows * rows * columns,
        4 * rows * columns,
    )(pieces, image_kv)
    block = call(
        functools.partial(place_body, seq_n),
        jax.ShapeDtypeStruct((rows, columns), bf16),
        [SCALARS, WHOLE, WHOLE],
        WHOLE,
        0,
        6 * rows * columns,
    )(pieces, shifted, text)
    blocks = [lax.ppermute(block, "seq", pairs) for pairs in forth]
    attended, *grads = call(
        functools.partial(attend_body, seq_n, tables),
        [jax.ShapeDtypeStruct(queries.shape, bf16)]
        + [jax.ShapeDtypeStruct((rows, columns), bf16)] * (1 + len(blocks)),
        [WHOLE] * (3 + len(blocks)),
        [WHOLE] * (2 + len(blocks)),
        10 * seq_n * rows * rows * queries.shape[1],
        6 * rows * queries.shape[1] + 4 * seq_n * rows * columns,
    )(queries, grad_out, block, *blocks)
    parts = [lax.ppermute(g, "seq", [(t, s) for s, t in pairs]) for g, pairs in zip(grads[1:], forth)]

    half = rows // 2
    grad_rows, send = call(
        functools.partial(back_body, seq_n, piece),
        [jax.ShapeDtypeStruct((half, columns), bf16), jax.ShapeDtypeStruct((half, width), bf16)],
        [SCALARS] + [WHOLE] * (2 + len(parts)),
        [WHOLE, WHOLE],
        rows * width * columns,
        2 * width * columns + rows * width,
    )(pieces, key_value_proj, grads[0], *parts)
    keep = call(
        keep_body,
        jax.ShapeDtypeStruct((half, width), f32),
        [WHOLE, WHOLE],
        WHOLE,
        rows * width * columns,
        2 * width * columns + 2 * rows * width,
    )(grad_rows, key_value_proj)
    other = lax.ppermute(send, names, core_pairs)
    steps = list(range(1, count))
    own_sum, *sends = call(
        functools.partial(pair_body, piece),
        [jax.ShapeDtypeStruct((piece, width), f32)] + [jax.ShapeDtypeStruct((piece, width), bf16)] * len(steps),
        [WHOLE, WHOLE],
        [WHOLE] * count,
        0,
        6 * rows // 2 * width,
    )(keep, other)
    shares = [lax.ppermute(sends[d - 1], names, far_pairs(d)) for d in steps]
    mine = call(
        final_body,
        jax.ShapeDtypeStruct((piece, width), bf16),
        [WHOLE] * (3 + len(shares)),
        WHOLE,
        0,
        12 * piece * width,
    )(own_sum, own_rows, gain, *shares)
    mines = {0: mine}
    for d in steps:
        mines[d] = lax.ppermute(mine, names, far_pairs(d))
    theirs = {d: lax.ppermute(mines[d], names, core_pairs) for d in range(count)}
    vis_grad = None
    for core, parts in enumerate((mines, theirs)):
        done = [] if vis_grad is None else [vis_grad]
        vis_grad = call(
            functools.partial(gather_body, count, core),
            jax.ShapeDtypeStruct((rows, width), bf16),
            [WHOLE] * count + [hbm] * len(done),
            hbm,
            0,
            2 * rows * width,
            scratch_shapes=[pltpu.SemaphoreType.DMA((count,))],
            input_output_aliases={count: 0} if done else {},
        )(*[parts[d] for d in reversed(range(count))], *done)
    return (attended, vis_grad)


def solution(mesh):
    in_specs = (
        P("seq", None),
        P(),
        P(None, ("sec", "tp")),
        P(),
        P("seq", ("sec", "tp")),
        P("seq", ("sec", "tp")),
        P("seq", ("sec", "tp")),
    )
    out_specs = (P("seq", ("sec", "tp")), P("seq", None))
    return jax.shard_map(
        on_device, mesh=mesh, in_specs=in_specs, out_specs=out_specs, check_vma=False
    )
```

```python
import functools
import itertools
import math

import jax
import jax.numpy as jnp
from jax import lax
from jax.experimental import pallas as pl
from jax.experimental.pallas import tpu as pltpu
from jax.sharding import PartitionSpec as P

HD = 128
EPS = 1e-06
NEG = -1e30
VMEM_LIMIT = 48 * 1024 * 1024
WIDE_LIMIT = 854 * 64 * 1024
WHOLE = pl.BlockSpec(memory_space=pltpu.VMEM)
SCALARS = pl.BlockSpec(memory_space=pltpu.SMEM)


def owner_block(image, count):
    half = count // 2
    return image - half if image >= half else half + (image + 1) % half


def held_image(block, count):
    half = count // 2
    return jnp.where(block < half, block + half, lax.rem(block + half - 1, half))


def flows(rounds, count):
    load = [0] * (2 * count)
    for pairs in rounds:
        for s, t in enumerate(pairs):
            for k in range(min(s, t), max(s, t)):
                load[2 * k + (t > s)] += 1
    return max(load), sum(load)


def rounds_of(edges, count):
    best = [tuple(d ^ r for d in range(count)) for r in range(count - 1, 0, -1)]
    if count > 4:
        return best
    whole = [p for p in itertools.permutations(range(count)) if all(s != t for s, t in enumerate(p))]
    for size in range(1, count):
        found = [c for c in itertools.combinations(whole, size) if all(any(p[s] == t for p in c) for s, t in edges)]
        if found:
            far = lambda p: max(abs(s - t) for s, t in enumerate(p))
            return sorted(min(found, key=lambda c: flows(c, count)), key=far)
    return best


def pick_static(table, index):
    value = jnp.int32(table[0])
    for n in range(1, len(table)):
        value = jnp.where(index == n, table[n], value)
    return value


def group_place():
    sec, tp = lax.axis_index("sec"), lax.axis_index("tp")
    return lax.rem(sec, 2), lax.div(sec, 2) * lax.axis_size("tp") + tp


def dot(a, b, dims):
    return lax.dot_general(a, b, (dims, ((), ())), preferred_element_type=jnp.float32)


def call(body, out_shape, in_specs, out_specs, flops, moved, limit=VMEM_LIMIT, **more):
    return pl.pallas_call(
        body,
        out_shape=out_shape,
        in_specs=in_specs,
        out_specs=out_specs,
        compiler_params=pltpu.CompilerParams(vmem_limit_bytes=limit),
        cost_estimate=pl.CostEstimate(flops=flops, bytes_accessed=moved, transcendentals=0),
        **more,
    )


def cuts(width):
    size = max(width // (4 * 256), 1) * 256
    edges = [i * size for i in range(4)] + [width]
    return list(zip(edges[:-1], edges[1:]))


def project_body(piece, vis_hbm, gain_hbm, proj_hbm, kv_ref, own_ref, vis, gain_ref, proj, vis_sems, proj_sems, gain_sem):
    rows, width = vis.shape
    gain_copy = pltpu.make_async_copy(gain_hbm, gain_ref, gain_sem)
    gain_copy.start()
    copies = []
    for n, (low, high) in enumerate(cuts(width)):
        vis_copy = pltpu.make_async_copy(vis_hbm.at[:, low:high], vis.at[:, low:high], vis_sems.at[n])
        proj_copy = pltpu.make_async_copy(proj_hbm.at[low:high, :], proj.at[low:high, :], proj_sems.at[n])
        vis_copy.start()
        proj_copy.start()
        copies.append((vis_copy, proj_copy))
    gain_copy.wait()
    squares = jnp.zeros((rows, HD), jnp.float32)
    total = jnp.zeros(kv_ref.shape, jnp.float32)
    for (low, high), (vis_copy, proj_copy) in zip(cuts(width), copies):
        vis_copy.wait()
        scaled = []
        for c in range(low, high, HD):
            wide = vis[:, c : c + HD].astype(jnp.float32)
            squares += wide * wide
            scaled.append((wide * gain_ref[c // HD : c // HD + 1, :]).astype(jnp.bfloat16))
        proj_copy.wait()
        total += jnp.dot(jnp.concatenate(scaled, axis=1), proj[low:high, :], preferred_element_type=jnp.float32)
    inverse = lax.rsqrt(jnp.sum(squares, axis=1, keepdims=True) / width + EPS)
    kv_ref[...] = (total * inverse).astype(jnp.bfloat16)
    parity, place = group_place()
    start = pl.multiple_of(parity * (rows // 2) + place * piece, piece)
    own_ref[...] = vis[pl.ds(start, piece), :]


def shift_body(seq_n, pieces_ref, image_ref, out_ref):
    rows = image_ref.shape[0]
    before = pieces_ref[2 * held_image(lax.axis_index("seq"), seq_n)]
    to = lax.broadcasted_iota(jnp.int32, (rows, rows), 0)
    source = lax.broadcasted_iota(jnp.int32, (rows, rows), 1)
    pick = jnp.where(source == to - before, 1.0, 0.0).astype(jnp.bfloat16)
    out_ref[...] = jnp.dot(pick, image_ref[...], preferred_element_type=jnp.float32).astype(jnp.bfloat16)


def place_body(seq_n, pieces_ref, image_ref, text_ref, out_ref):
    before = pieces_ref[2 * held_image(lax.axis_index("seq"), seq_n)]
    row = lax.broadcasted_iota(jnp.int32, image_ref.shape, 0)
    text, image = text_ref[...].astype(jnp.float32), image_ref[...].astype(jnp.float32)
    out_ref[...] = jnp.where(row < before, text, image).astype(jnp.bfloat16)


def heads_of(ref, heads):
    return jnp.concatenate([ref[:, h * HD : (h + 1) * HD] for h in heads], axis=0)


def head_groups(group, keys):
    together = group if keys <= 1024 else 1
    return [range(first, first + together) for first in range(0, group, together)]


def grad_parts(chosen, rows, scale, low_ref, dscore_ref, q_ref, g_ref, grad_refs):
    totals = [None] * len(chosen)
    for heads in head_groups(q_ref.shape[1] // HD, low_ref.shape[0]):
        q, g = heads_of(q_ref, heads), heads_of(g_ref, heads)
        span = slice(heads[0] * rows, (heads[-1] + 1) * rows)
        for n, r in enumerate(chosen):
            part = slice(r * rows, (r + 1) * rows)
            dkeys = jnp.dot(dscore_ref[part, span], q, preferred_element_type=jnp.float32)
            dvalues = jnp.dot(low_ref[part, span], g, preferred_element_type=jnp.float32)
            if totals[n] is not None:
                dkeys, dvalues = totals[n][0] + dkeys, totals[n][1] + dvalues
            totals[n] = dkeys, dvalues
    for (dkeys, dvalues), ref in zip(totals, grad_refs):
        ref[:, :HD] = (dkeys * scale).astype(jnp.bfloat16)
        ref[:, HD:] = dvalues.astype(jnp.bfloat16)


def weigh_body(seq_n, tables, early, pieces_ref, q_ref, g_ref, text_ref, own_ref, raw_ref, *refs):
    count = len(tables)
    block_refs, (low_ref, dscore_ref, values_ref) = refs[:count], refs[count : count + 3]
    grad_refs = refs[count + 3 :]
    rows = q_ref.shape[0]
    group = q_ref.shape[1] // HD
    scale = 1.0 / math.sqrt(HD)
    me = lax.axis_index("seq")
    before = pieces_ref[2 * me]
    ahead = lax.broadcasted_iota(jnp.int32, (rows, rows), 0) - lax.broadcasted_iota(jnp.int32, (rows, rows), 1)
    pick = jnp.where(ahead == before, 1.0, 0.0).astype(jnp.bfloat16)
    placed = jnp.dot(pick, raw_ref[...], preferred_element_type=jnp.float32)
    row = lax.broadcasted_iota(jnp.int32, placed.shape, 0)
    mine = jnp.where(row < before, text_ref[...].astype(jnp.float32), placed).astype(jnp.bfloat16)
    kv = jnp.concatenate([own_ref[...], mine] + [ref[...] for ref in block_refs], axis=0)
    keys, values = kv[:, :HD], kv[:, HD:]
    values_ref[...] = values
    images = [held_image(me, seq_n), me] + [pick_static(table, me) for table in tables]
    for heads in head_groups(group, kv.shape[0]):
        q, g = heads_of(q_ref, heads), heads_of(g_ref, heads)
        offset = lax.broadcasted_iota(jnp.int32, (rows, q.shape[0]), 0)
        offset = offset - lax.rem(lax.broadcasted_iota(jnp.int32, (rows, q.shape[0]), 1), rows)
        scores = dot(keys, q, ((1,), (1,)))
        scores = jnp.concatenate(
            [
                jnp.where(offset <= (me - image) * rows, scores[n * rows : (n + 1) * rows], NEG)
                for n, image in enumerate(images)
            ],
            axis=0,
        )
        top = jnp.max(scores, axis=0, keepdims=True)
        weights = jnp.exp2((scores - top) * (scale * math.log2(math.e)))
        weights = weights * (1.0 / jnp.sum(weights, axis=0, keepdims=True))
        low = weights.astype(jnp.bfloat16)
        dprob = dot(values, g, ((1,), (1,)))
        drift = jnp.sum(low.astype(jnp.float32) * dprob, axis=0, keepdims=True)
        span = slice(heads[0] * rows, (heads[-1] + 1) * rows)
        low_ref[:, span] = low
        dscore_ref[:, span] = (weights * (dprob - drift)).astype(jnp.bfloat16)
    grad_parts(early, rows, scale, low_ref, dscore_ref, q_ref, g_ref, grad_refs)


def mix_body(late, q_ref, g_ref, low_ref, dscore_ref, values_ref, out_ref, *grad_refs):
    rows = q_ref.shape[0]
    grad_parts(late, rows, 1.0 / math.sqrt(HD), low_ref, dscore_ref, q_ref, g_ref, grad_refs)
    for heads in head_groups(q_ref.shape[1] // HD, low_ref.shape[0]):
        span = slice(heads[0] * rows, (heads[-1] + 1) * rows)
        mixed = dot(values_ref[...], low_ref[:, span], ((0,), (0,)))
        for n, h in enumerate(heads):
            part = jnp.transpose(mixed[:, n * rows : (n + 1) * rows])
            out_ref[:, h * HD : (h + 1) * HD] = part.astype(jnp.bfloat16)


def back_body(seq_n, piece, pieces_ref, proj_ref, *refs):
    part_refs, (keep_ref, send_ref) = refs[:-2], refs[-2:]
    rows = part_refs[0].shape[0]
    half = rows // 2
    before = pieces_ref[2 * held_image(lax.axis_index("seq"), seq_n)]
    parity, place = group_place()
    total = part_refs[0][...].astype(jnp.float32)
    for ref in part_refs[1:]:
        total += ref[...].astype(jnp.float32)
    slot = lax.broadcasted_iota(jnp.int32, (rows, rows), 0)
    to = (lax.div(slot, half) ^ parity) * half
    to += (lax.div(lax.rem(slot, half), piece) ^ place) * piece + lax.rem(slot, piece)
    source = lax.broadcasted_iota(jnp.int32, (rows, rows), 1)
    pick = jnp.where(source == to + before, 1.0, 0.0).astype(jnp.bfloat16)
    image_grad = jnp.dot(pick, total.astype(jnp.bfloat16), preferred_element_type=jnp.float32)
    product = dot(image_grad.astype(jnp.bfloat16), proj_ref[...], ((1,), (1,)))
    keep_ref[...] = product[:half]
    send_ref[...] = product[half:].astype(jnp.bfloat16)


def pair_body(piece, keep_ref, other_ref, own_ref, *send_refs):
    own_ref[...] = keep_ref[:piece] + other_ref[:piece].astype(jnp.float32)
    for n, ref in enumerate(send_refs):
        part = slice((n + 1) * piece, (n + 2) * piece)
        ref[...] = (keep_ref[part] + other_ref[part].astype(jnp.float32)).astype(jnp.bfloat16)


def final_body(total_ref, own_ref, gain_ref, *refs):
    out_ref = refs[-1]
    width = own_ref.shape[1]
    square = stat = None
    scaled = []
    for c in range(0, width, HD):
        cols = slice(c, c + HD)
        total = total_ref[:, cols]
        for ref in refs[:-1]:
            total += ref[:, cols].astype(jnp.float32)
        own = own_ref[:, cols].astype(jnp.float32)
        grad = total * gain_ref[c // HD : c // HD + 1, :]
        scaled.append(grad)
        square = own * own if square is None else square + own * own
        stat = own * grad if stat is None else stat + own * grad
    inverse = lax.rsqrt(jnp.sum(square, axis=1, keepdims=True) / width + EPS)
    lead = inverse * inverse * inverse * (jnp.sum(stat, axis=1, keepdims=True) / width)
    for n, c in enumerate(range(0, width, HD)):
        own = own_ref[:, c : c + HD].astype(jnp.float32)
        out_ref[:, c : c + HD] = (scaled[n] * inverse - own * lead).astype(jnp.bfloat16)


def gather_body(count, core, *refs):
    part_refs, (out_hbm, sems) = refs[:count], refs[-2:]
    piece = part_refs[0].shape[0]
    parity, place = group_place()
    copies = []
    for n, ref in enumerate(part_refs):
        row = ((parity ^ core) * count + (place ^ (count - 1 - n))) * piece
        copy = pltpu.make_async_copy(ref, out_hbm.at[pl.ds(pl.multiple_of(row, piece), piece), :], sems.at[n])
        copy.start()
        copies.append(copy)
    for copy in copies:
        copy.wait()


def on_device(vis_rows, vis_gain, key_value_proj, pieces, text_kv, queries, grad_out):
    rows, width = vis_rows.shape
    columns = key_value_proj.shape[1]
    seq_n = lax.axis_size("seq")
    tp_n = lax.axis_size("tp")
    n = lax.axis_size("sec") * tp_n
    count = n // 2
    piece = rows // n
    bf16, f32 = jnp.bfloat16, jnp.float32
    names = ("sec", "tp")
    core_pairs = [(i, (i // tp_n ^ 1) * tp_n + i % tp_n) for i in range(n)]

    def far_pairs(step):
        pairs = []
        for i in range(n):
            sec, tp = divmod(i, tp_n)
            place = (sec // 2 * tp_n + tp) ^ step
            pairs.append((i, (place // tp_n * 2 + sec % 2) * tp_n + place % tp_n))
        return pairs

    gain = vis_gain.reshape(width // HD, HD)
    owners = [owner_block(j, seq_n) for j in range(seq_n)]
    held = [owners.index(b) for b in range(seq_n)]
    home = [(owners[j], j) for j in range(seq_n)]
    edges = {(owners[j], d) for j in range(seq_n) for d in range(j + 1, seq_n) if owners[j] != d}
    tables, forth, left = [], [], set(edges)
    for pairs in rounds_of(sorted(edges), seq_n):
        table = [seq_n] * seq_n
        for s, t in enumerate(pairs):
            if (s, t) in left:
                table[t] = held[s]
        left -= set(enumerate(pairs))
        tables.append(table)
        forth.append(list(enumerate(pairs)))
    text = lax.ppermute(text_kv, "seq", list(enumerate(owners)))
    chunks = len(cuts(width))
    hbm = pl.BlockSpec(memory_space=pltpu.HBM)
    image_kv, own_rows = call(
        functools.partial(project_body, piece),
        [jax.ShapeDtypeStruct((rows, columns), bf16), jax.ShapeDtypeStruct((piece, width), bf16)],
        [hbm, hbm, hbm],
        [WHOLE, WHOLE],
        2 * rows * width * columns,
        2 * width * (rows + columns),
        limit=WIDE_LIMIT,
        scratch_shapes=[
            pltpu.VMEM((rows, width), bf16),
            pltpu.VMEM(gain.shape, f32),
            pltpu.VMEM((width, columns), bf16),
            pltpu.SemaphoreType.DMA((chunks,)),
            pltpu.SemaphoreType.DMA((chunks,)),
            pltpu.SemaphoreType.DMA,
        ],
    )(vis_rows, gain, key_value_proj)
    raw = lax.ppermute(image_kv, "seq", home)
    shifted = call(
        functools.partial(shift_body, seq_n),
        jax.ShapeDtypeStruct((rows, columns), bf16),
        [SCALARS, WHOLE],
        WHOLE,
        2 * rows * rows * columns,
        4 * rows * columns,
    )(pieces, image_kv)
    block = call(
        functools.partial(place_body, seq_n),
        jax.ShapeDtypeStruct((rows, columns), bf16),
        [SCALARS, WHOLE, WHOLE],
        WHOLE,
        0,
        6 * rows * columns,
    )(pieces, shifted, text)
    blocks = [lax.ppermute(block, "seq", pairs) for pairs in forth]
    total = 2 + len(blocks)
    early, late = list(range(1, total)), [0]
    kv_shape = jax.ShapeDtypeStruct((rows, columns), bf16)
    wide_shape = jax.ShapeDtypeStruct((total * rows, queries.shape[1] // HD * rows), bf16)
    low, dscore, values, *grads = call(
        functools.partial(weigh_body, seq_n, tables, early),
        [wide_shape, wide_shape, jax.ShapeDtypeStruct((total * rows, HD), bf16)] + [kv_shape] * len(early),
        [SCALARS] + [WHOLE] * (3 + total),
        [WHOLE] * (3 + len(early)),
        8 * total * rows * rows * queries.shape[1],
        4 * rows * queries.shape[1] + 4 * total * rows * columns,
    )(pieces, queries, grad_out, text_kv, block, raw, *blocks)
    attended, own_grad = call(
        functools.partial(mix_body, late),
        [jax.ShapeDtypeStruct(queries.shape, bf16)] + [kv_shape] * len(late),
        [WHOLE] * 5,
        [WHOLE] * (1 + len(late)),
        2 * total * rows * rows * queries.shape[1],
        6 * rows * queries.shape[1] + 4 * total * rows * columns,
    )(queries, grad_out, low, dscore, values)
    back = list(zip(grads, [home] + forth))
    parts = [lax.ppermute(g, "seq", [(t, s) for s, t in pairs]) for g, pairs in back[:1] + back[:0:-1]]

    keep, send = call(
        functools.partial(back_body, seq_n, piece),
        [jax.ShapeDtypeStruct((rows // 2, width), f32), jax.ShapeDtypeStruct((rows // 2, width), bf16)],
        [SCALARS] + [WHOLE] * (2 + len(parts)),
        [WHOLE, WHOLE],
        2 * rows * width * columns,
        2 * width * columns + 3 * rows * width,
    )(pieces, key_value_proj, own_grad, *parts)
    other = lax.ppermute(send, names, core_pairs)
    steps = list(range(1, count))
    own_sum, *sends = call(
        functools.partial(pair_body, piece),
        [jax.ShapeDtypeStruct((piece, width), f32)] + [jax.ShapeDtypeStruct((piece, width), bf16)] * len(steps),
        [WHOLE, WHOLE],
        [WHOLE] * count,
        0,
        6 * rows // 2 * width,
    )(keep, other)
    shares = [lax.ppermute(sends[d - 1], names, far_pairs(d)) for d in steps[::-1]]
    mine = call(
        final_body,
        jax.ShapeDtypeStruct((piece, width), bf16),
        [WHOLE] * (3 + len(shares)),
        WHOLE,
        0,
        12 * piece * width,
    )(own_sum, own_rows, gain, *shares)
    mines = {0: mine}
    for d in steps:
        mines[d] = lax.ppermute(mine, names, far_pairs(d))
    theirs = {d: lax.ppermute(mines[d], names, core_pairs) for d in range(count)}
    vis_grad = None
    for core, parts in enumerate((mines, theirs)):
        done = [] if vis_grad is None else [vis_grad]
        vis_grad = call(
            functools.partial(gather_body, count, core),
            jax.ShapeDtypeStruct((rows, width), bf16),
            [WHOLE] * count + [hbm] * len(done),
            hbm,
            0,
            2 * rows * width,
            scratch_shapes=[pltpu.SemaphoreType.DMA((count,))],
            input_output_aliases={count: 0} if done else {},
        )(*[parts[d] for d in reversed(range(count))], *done)
    return (attended, vis_grad)


def solution(mesh):
    in_specs = (
        P("seq", None),
        P(),
        P(None, ("sec", "tp")),
        P(),
        P("seq", ("sec", "tp")),
        P("seq", ("sec", "tp")),
        P("seq", ("sec", "tp")),
    )
    out_specs = (P("seq", ("sec", "tp")), P("seq", None))
    return jax.shard_map(
        on_device, mesh=mesh, in_specs=in_specs, out_specs=out_specs, check_vma=False
    )
```

```python
import functools
import itertools
import math

import jax
import jax.numpy as jnp
from jax import lax
from jax.experimental import pallas as pl
from jax.experimental.pallas import tpu as pltpu
from jax.sharding import PartitionSpec as P

HD = 128
EPS = 1e-06
NEG = -1e30
VMEM_LIMIT = 48 * 1024 * 1024
WIDE_LIMIT = 854 * 64 * 1024
WHOLE = pl.BlockSpec(memory_space=pltpu.VMEM)
SCALARS = pl.BlockSpec(memory_space=pltpu.SMEM)


def owner_block(image, count):
    half = count // 2
    return image - half if image >= half else half + (image + 1) % half


def held_image(block, count):
    half = count // 2
    return jnp.where(block < half, block + half, lax.rem(block + half - 1, half))


def flows(rounds, count):
    load = [0] * (2 * count)
    for pairs in rounds:
        for s, t in enumerate(pairs):
            for k in range(min(s, t), max(s, t)):
                load[2 * k + (t > s)] += 1
    return max(load), sum(load)


def rounds_of(edges, count):
    best = [tuple(d ^ r for d in range(count)) for r in range(count - 1, 0, -1)]
    if count > 4:
        return best
    whole = [p for p in itertools.permutations(range(count)) if all(s != t for s, t in enumerate(p))]
    for size in range(1, count):
        found = [c for c in itertools.combinations(whole, size) if all(any(p[s] == t for p in c) for s, t in edges)]
        if found:
            far = lambda p: max(abs(s - t) for s, t in enumerate(p))
            return sorted(min(found, key=lambda c: flows(c, count)), key=far)
    return best


def pick_static(table, index):
    value = jnp.int32(table[0])
    for n in range(1, len(table)):
        value = jnp.where(index == n, table[n], value)
    return value


def group_place():
    sec, tp = lax.axis_index("sec"), lax.axis_index("tp")
    return lax.rem(sec, 2), lax.div(sec, 2) * lax.axis_size("tp") + tp


def dot(a, b, dims):
    return lax.dot_general(a, b, (dims, ((), ())), preferred_element_type=jnp.float32)


def call(body, out_shape, in_specs, out_specs, flops, moved, limit=VMEM_LIMIT, **more):
    return pl.pallas_call(
        body,
        out_shape=out_shape,
        in_specs=in_specs,
        out_specs=out_specs,
        compiler_params=pltpu.CompilerParams(vmem_limit_bytes=limit),
        cost_estimate=pl.CostEstimate(flops=flops, bytes_accessed=moved, transcendentals=0),
        **more,
    )


def cuts(width):
    size = max(width // (4 * 256), 1) * 256
    edges = [i * size for i in range(4)] + [width]
    return list(zip(edges[:-1], edges[1:]))


def project_body(piece, vis_hbm, gain_hbm, proj_hbm, kv_ref, own_ref, vis, gain_ref, proj, vis_sems, proj_sems, gain_sem):
    rows, width = vis.shape
    gain_copy = pltpu.make_async_copy(gain_hbm, gain_ref, gain_sem)
    gain_copy.start()
    copies = []
    for n, (low, high) in enumerate(cuts(width)):
        vis_copy = pltpu.make_async_copy(vis_hbm.at[:, low:high], vis.at[:, low:high], vis_sems.at[n])
        proj_copy = pltpu.make_async_copy(proj_hbm.at[low:high, :], proj.at[low:high, :], proj_sems.at[n])
        vis_copy.start()
        proj_copy.start()
        copies.append((vis_copy, proj_copy))
    gain_copy.wait()
    squares = jnp.zeros((rows, HD), jnp.float32)
    total = jnp.zeros(kv_ref.shape, jnp.float32)
    for (low, high), (vis_copy, proj_copy) in zip(cuts(width), copies):
        vis_copy.wait()
        scaled = []
        for c in range(low, high, HD):
            wide = vis[:, c : c + HD].astype(jnp.float32)
            squares += wide * wide
            scaled.append((wide * gain_ref[c // HD : c // HD + 1, :]).astype(jnp.bfloat16))
        proj_copy.wait()
        total += jnp.dot(jnp.concatenate(scaled, axis=1), proj[low:high, :], preferred_element_type=jnp.float32)
    inverse = lax.rsqrt(jnp.sum(squares, axis=1, keepdims=True) / width + EPS)
    kv_ref[...] = (total * inverse).astype(jnp.bfloat16)
    parity, place = group_place()
    start = pl.multiple_of(parity * (rows // 2) + place * piece, piece)
    own_ref[...] = vis[pl.ds(start, piece), :]


def placed(before, rows, image_ref, text_ref):
    ahead = lax.broadcasted_iota(jnp.int32, (rows, rows), 0) - lax.broadcasted_iota(jnp.int32, (rows, rows), 1)
    pick = jnp.where(ahead == before, 1.0, 0.0).astype(jnp.bfloat16)
    image = jnp.dot(pick, image_ref[...], preferred_element_type=jnp.float32)
    row = lax.broadcasted_iota(jnp.int32, image.shape, 0)
    return jnp.where(row < before, text_ref[...].astype(jnp.float32), image).astype(jnp.bfloat16)


def place_body(seq_n, pieces_ref, image_ref, text_ref, out_ref):
    rows = image_ref.shape[0]
    before = pieces_ref[2 * held_image(lax.axis_index("seq"), seq_n)]
    out_ref[...] = placed(before, rows, image_ref, text_ref)


def heads_of(ref, heads):
    return jnp.concatenate([ref[:, h * HD : (h + 1) * HD] for h in heads], axis=0)


def head_groups(group, keys):
    together = group if keys <= 1024 else 1
    return [range(first, first + together) for first in range(0, group, together)]


def grad_parts(chosen, rows, scale, low_ref, dscore_ref, q_ref, g_ref, grad_refs):
    totals = [None] * len(chosen)
    for heads in head_groups(q_ref.shape[1] // HD, low_ref.shape[0]):
        q, g = heads_of(q_ref, heads), heads_of(g_ref, heads)
        span = slice(heads[0] * rows, (heads[-1] + 1) * rows)
        for n, r in enumerate(chosen):
            part = pl.ds(pl.multiple_of(r * rows, rows), rows)
            dkeys = jnp.dot(dscore_ref[part, span], q, preferred_element_type=jnp.float32)
            dvalues = jnp.dot(low_ref[part, span], g, preferred_element_type=jnp.float32)
            if totals[n] is not None:
                dkeys, dvalues = totals[n][0] + dkeys, totals[n][1] + dvalues
            totals[n] = dkeys, dvalues
    for (dkeys, dvalues), ref in zip(totals, grad_refs):
        ref[:, :HD] = (dkeys * scale).astype(jnp.bfloat16)
        ref[:, HD:] = dvalues.astype(jnp.bfloat16)


def weigh_body(seq_n, tables, backs, pieces_ref, q_ref, g_ref, text_ref, own_ref, raw_ref, *refs):
    count = len(tables)
    block_refs, (low_ref, dscore_ref, values_ref) = refs[:count], refs[count : count + 3]
    grad_refs = refs[count + 3 :]
    rows = q_ref.shape[0]
    group = q_ref.shape[1] // HD
    scale = 1.0 / math.sqrt(HD)
    me = lax.axis_index("seq")
    mine = placed(pieces_ref[2 * me], rows, raw_ref, text_ref)
    kv = jnp.concatenate([own_ref[...], mine] + [ref[...] for ref in block_refs], axis=0)
    keys, values = kv[:, :HD], kv[:, HD:]
    values_ref[...] = values
    images = [held_image(me, seq_n), me] + [pick_static(table, me) for table in tables]
    for heads in head_groups(group, kv.shape[0]):
        q, g = heads_of(q_ref, heads), heads_of(g_ref, heads)
        offset = lax.broadcasted_iota(jnp.int32, (rows, q.shape[0]), 0)
        offset = offset - lax.rem(lax.broadcasted_iota(jnp.int32, (rows, q.shape[0]), 1), rows)
        scores = dot(keys, q, ((1,), (1,)))
        scores = jnp.concatenate(
            [
                jnp.where(offset <= (me - image) * rows, scores[n * rows : (n + 1) * rows], NEG)
                for n, image in enumerate(images)
            ],
            axis=0,
        )
        top = jnp.max(scores, axis=0, keepdims=True)
        weights = jnp.exp2((scores - top) * (scale * math.log2(math.e)))
        weights = weights * (1.0 / jnp.sum(weights, axis=0, keepdims=True))
        low = weights.astype(jnp.bfloat16)
        dprob = dot(values, g, ((1,), (1,)))
        drift = jnp.sum(low.astype(jnp.float32) * dprob, axis=0, keepdims=True)
        span = slice(heads[0] * rows, (heads[-1] + 1) * rows)
        low_ref[:, span] = low
        dscore_ref[:, span] = (weights * (dprob - drift)).astype(jnp.bfloat16)
    early = [pick_static(table, me) for table in backs]
    grad_parts(early, rows, scale, low_ref, dscore_ref, q_ref, g_ref, grad_refs)


def mix_body(late, q_ref, g_ref, low_ref, dscore_ref, values_ref, out_ref, *grad_refs):
    rows = q_ref.shape[0]
    grad_parts(late, rows, 1.0 / math.sqrt(HD), low_ref, dscore_ref, q_ref, g_ref, grad_refs)
    for heads in head_groups(q_ref.shape[1] // HD, low_ref.shape[0]):
        span = slice(heads[0] * rows, (heads[-1] + 1) * rows)
        mixed = dot(values_ref[...], low_ref[:, span], ((0,), (0,)))
        for n, h in enumerate(heads):
            part = jnp.transpose(mixed[:, n * rows : (n + 1) * rows])
            out_ref[:, h * HD : (h + 1) * HD] = part.astype(jnp.bfloat16)


def back_body(seq_n, piece, pieces_ref, proj_ref, *refs):
    part_refs, (keep_ref, send_ref) = refs[:-2], refs[-2:]
    rows = part_refs[0].shape[0]
    half = rows // 2
    before = pieces_ref[2 * held_image(lax.axis_index("seq"), seq_n)]
    parity, place = group_place()
    total = part_refs[0][...].astype(jnp.float32)
    for ref in part_refs[1:]:
        total += ref[...].astype(jnp.float32)
    slot = lax.broadcasted_iota(jnp.int32, (rows, rows), 0)
    to = (lax.div(slot, half) ^ parity) * half
    to += (lax.div(lax.rem(slot, half), piece) ^ place) * piece + lax.rem(slot, piece)
    source = lax.broadcasted_iota(jnp.int32, (rows, rows), 1)
    pick = jnp.where(source == to + before, 1.0, 0.0).astype(jnp.bfloat16)
    image_grad = jnp.dot(pick, total.astype(jnp.bfloat16), preferred_element_type=jnp.float32)
    product = dot(image_grad.astype(jnp.bfloat16), proj_ref[...], ((1,), (1,)))
    keep_ref[...] = product[:half]
    send_ref[...] = product[half:].astype(jnp.bfloat16)


def pair_body(piece, keep_ref, other_ref, own_ref, *send_refs):
    own_ref[...] = keep_ref[:piece] + other_ref[:piece].astype(jnp.float32)
    for n, ref in enumerate(send_refs):
        part = slice((n + 1) * piece, (n + 2) * piece)
        ref[...] = (keep_ref[part] + other_ref[part].astype(jnp.float32)).astype(jnp.bfloat16)


def final_body(total_ref, own_ref, gain_ref, *refs):
    out_ref = refs[-1]
    width = own_ref.shape[1]
    square = stat = None
    scaled = []
    for c in range(0, width, HD):
        cols = slice(c, c + HD)
        total = total_ref[:, cols]
        for ref in refs[:-1]:
            total += ref[:, cols].astype(jnp.float32)
        own = own_ref[:, cols].astype(jnp.float32)
        grad = total * gain_ref[c // HD : c // HD + 1, :]
        scaled.append(grad)
        square = own * own if square is None else square + own * own
        stat = own * grad if stat is None else stat + own * grad
    inverse = lax.rsqrt(jnp.sum(square, axis=1, keepdims=True) / width + EPS)
    lead = inverse * inverse * inverse * (jnp.sum(stat, axis=1, keepdims=True) / width)
    for n, c in enumerate(range(0, width, HD)):
        own = own_ref[:, c : c + HD].astype(jnp.float32)
        out_ref[:, c : c + HD] = (scaled[n] * inverse - own * lead).astype(jnp.bfloat16)


def gather_body(count, core, *refs):
    part_refs, (out_hbm, sems) = refs[:count], refs[-2:]
    piece = part_refs[0].shape[0]
    parity, place = group_place()
    copies = []
    for n, ref in enumerate(part_refs):
        row = ((parity ^ core) * count + (place ^ (count - 1 - n))) * piece
        copy = pltpu.make_async_copy(ref, out_hbm.at[pl.ds(pl.multiple_of(row, piece), piece), :], sems.at[n])
        copy.start()
        copies.append(copy)
    for copy in copies:
        copy.wait()


def on_device(vis_rows, vis_gain, key_value_proj, pieces, text_kv, queries, grad_out):
    rows, width = vis_rows.shape
    columns = key_value_proj.shape[1]
    seq_n = lax.axis_size("seq")
    tp_n = lax.axis_size("tp")
    n = lax.axis_size("sec") * tp_n
    count = n // 2
    piece = rows // n
    bf16, f32 = jnp.bfloat16, jnp.float32
    names = ("sec", "tp")
    core_pairs = [(i, (i // tp_n ^ 1) * tp_n + i % tp_n) for i in range(n)]

    def far_pairs(step):
        pairs = []
        for i in range(n):
            sec, tp = divmod(i, tp_n)
            place = (sec // 2 * tp_n + tp) ^ step
            pairs.append((i, (place // tp_n * 2 + sec % 2) * tp_n + place % tp_n))
        return pairs

    gain = vis_gain.reshape(width // HD, HD)
    owners = [owner_block(j, seq_n) for j in range(seq_n)]
    held = [owners.index(b) for b in range(seq_n)]
    home = [(owners[j], j) for j in range(seq_n)]
    edges = {(owners[j], d) for j in range(seq_n) for d in range(j + 1, seq_n) if owners[j] != d}
    tables, forth, left = [], [], set(edges)
    for pairs in rounds_of(sorted(edges), seq_n):
        table = [seq_n] * seq_n
        for s, t in enumerate(pairs):
            if (s, t) in left:
                table[t] = held[s]
        left -= set(enumerate(pairs))
        tables.append(table)
        forth.append(list(enumerate(pairs)))
    text = lax.ppermute(text_kv, "seq", list(enumerate(owners)))
    chunks = len(cuts(width))
    hbm = pl.BlockSpec(memory_space=pltpu.HBM)
    image_kv, own_rows = call(
        functools.partial(project_body, piece),
        [jax.ShapeDtypeStruct((rows, columns), bf16), jax.ShapeDtypeStruct((piece, width), bf16)],
        [hbm, hbm, hbm],
        [WHOLE, WHOLE],
        2 * rows * width * columns,
        2 * width * (rows + columns),
        limit=WIDE_LIMIT,
        scratch_shapes=[
            pltpu.VMEM((rows, width), bf16),
            pltpu.VMEM(gain.shape, f32),
            pltpu.VMEM((width, columns), bf16),
            pltpu.SemaphoreType.DMA((chunks,)),
            pltpu.SemaphoreType.DMA((chunks,)),
            pltpu.SemaphoreType.DMA,
        ],
    )(vis_rows, gain, key_value_proj)
    raw = lax.ppermute(image_kv, "seq", home)
    block = call(
        functools.partial(place_body, seq_n),
        jax.ShapeDtypeStruct((rows, columns), bf16),
        [SCALARS, WHOLE, WHOLE],
        WHOLE,
        0,
        6 * rows * columns,
    )(pieces, image_kv, text)
    blocks = [lax.ppermute(block, "seq", pairs) for pairs in forth]
    total = 2 + len(blocks)
    pairs_back, backs = [], []
    for r in range(seq_n - 1, 0, -1):
        pairs_back.append([(d, d ^ r) for d in range(seq_n)])
        table = []
        for d in range(seq_n):
            block_of = [held[d], d] + [t[d] for t in tables]
            want = held[d ^ r]
            if want > d:
                want = max(block_of)
            table.append(block_of.index(want, 1))
        backs.append(table)
    kv_shape = jax.ShapeDtypeStruct((rows, columns), bf16)
    wide_shape = jax.ShapeDtypeStruct((total * rows, queries.shape[1] // HD * rows), bf16)
    low, dscore, values, *grads = call(
        functools.partial(weigh_body, seq_n, tables, backs),
        [wide_shape, wide_shape, jax.ShapeDtypeStruct((total * rows, HD), bf16)] + [kv_shape] * len(backs),
        [SCALARS] + [WHOLE] * (3 + total),
        [WHOLE] * (3 + len(backs)),
        8 * total * rows * rows * queries.shape[1],
        4 * rows * queries.shape[1] + 4 * total * rows * columns,
    )(pieces, queries, grad_out, text_kv, block, raw, *blocks)
    attended, own_grad = call(
        functools.partial(mix_body, [0]),
        [jax.ShapeDtypeStruct(queries.shape, bf16), kv_shape],
        [WHOLE] * 5,
        [WHOLE, WHOLE],
        2 * total * rows * rows * queries.shape[1],
        6 * rows * queries.shape[1] + 4 * total * rows * columns,
    )(queries, grad_out, low, dscore, values)
    parts = [lax.ppermute(g, "seq", pairs) for g, pairs in zip(grads, pairs_back)]

    keep, send = call(
        functools.partial(back_body, seq_n, piece),
        [jax.ShapeDtypeStruct((rows // 2, width), f32), jax.ShapeDtypeStruct((rows // 2, width), bf16)],
        [SCALARS] + [WHOLE] * (2 + len(parts)),
        [WHOLE, WHOLE],
        2 * rows * width * columns,
        2 * width * columns + 3 * rows * width,
    )(pieces, key_value_proj, own_grad, *parts)
    other = lax.ppermute(send, names, core_pairs)
    steps = list(range(1, count))
    own_sum, *sends = call(
        functools.partial(pair_body, piece),
        [jax.ShapeDtypeStruct((piece, width), f32)] + [jax.ShapeDtypeStruct((piece, width), bf16)] * len(steps),
        [WHOLE, WHOLE],
        [WHOLE] * count,
        0,
        6 * rows // 2 * width,
    )(keep, other)
    shares = [lax.ppermute(sends[d - 1], names, far_pairs(d)) for d in steps[::-1]]
    mine = call(
        final_body,
        jax.ShapeDtypeStruct((piece, width), bf16),
        [WHOLE] * (3 + len(shares)),
        WHOLE,
        0,
        12 * piece * width,
    )(own_sum, own_rows, gain, *shares)
    mines = {0: mine}
    for d in steps:
        mines[d] = lax.ppermute(mine, names, far_pairs(d))
    theirs = {d: lax.ppermute(mines[d], names, core_pairs) for d in range(count)}
    vis_grad = None
    for core, parts in enumerate((mines, theirs)):
        done = [] if vis_grad is None else [vis_grad]
        vis_grad = call(
            functools.partial(gather_body, count, core),
            jax.ShapeDtypeStruct((rows, width), bf16),
            [WHOLE] * count + [hbm] * len(done),
            hbm,
            0,
            2 * rows * width,
            scratch_shapes=[pltpu.SemaphoreType.DMA((count,))],
            input_output_aliases={count: 0} if done else {},
        )(*[parts[d] for d in reversed(range(count))], *done)
    return (attended, vis_grad)


def solution(mesh):
    in_specs = (
        P("seq", None),
        P(),
        P(None, ("sec", "tp")),
        P(),
        P("seq", ("sec", "tp")),
        P("seq", ("sec", "tp")),
        P("seq", ("sec", "tp")),
    )
    out_specs = (P("seq", ("sec", "tp")), P("seq", None))
    return jax.shard_map(
        on_device, mesh=mesh, in_specs=in_specs, out_specs=out_specs, check_vma=False
    )
```

```python
import functools
import itertools
import math

import jax
import jax.numpy as jnp
from jax import lax
from jax.experimental import pallas as pl
from jax.experimental.pallas import tpu as pltpu
from jax.sharding import PartitionSpec as P

HD = 128
EPS = 1e-06
NEG = -1e30
VMEM_LIMIT = 48 * 1024 * 1024
WIDE_LIMIT = 854 * 64 * 1024
WHOLE = pl.BlockSpec(memory_space=pltpu.VMEM)
SCALARS = pl.BlockSpec(memory_space=pltpu.SMEM)


def owner_block(image, count):
    half = count // 2
    return image - half if image >= half else half + (image + 1) % half


def held_image(block, count):
    half = count // 2
    return jnp.where(block < half, block + half, lax.rem(block + half - 1, half))


def flows(rounds, count):
    load = [0] * (2 * count)
    for pairs in rounds:
        for s, t in enumerate(pairs):
            for k in range(min(s, t), max(s, t)):
                load[2 * k + (t > s)] += 1
    return max(load), sum(load)


def rounds_of(edges, count):
    best = [tuple(d ^ r for d in range(count)) for r in range(count - 1, 0, -1)]
    if count > 4:
        return best
    whole = [p for p in itertools.permutations(range(count)) if all(s != t for s, t in enumerate(p))]
    for size in range(1, count):
        found = [c for c in itertools.combinations(whole, size) if all(any(p[s] == t for p in c) for s, t in edges)]
        if found:
            far = lambda p: max(abs(s - t) for s, t in enumerate(p))
            return sorted(min(found, key=lambda c: flows(c, count)), key=far)
    return best


def pick_static(table, index):
    value = jnp.int32(table[0])
    for n in range(1, len(table)):
        value = jnp.where(index == n, table[n], value)
    return value


def group_place():
    sec, tp = lax.axis_index("sec"), lax.axis_index("tp")
    return lax.rem(sec, 2), lax.div(sec, 2) * lax.axis_size("tp") + tp


def dot(a, b, dims):
    return lax.dot_general(a, b, (dims, ((), ())), preferred_element_type=jnp.float32)


def call(body, out_shape, in_specs, out_specs, flops, moved, limit=VMEM_LIMIT, **more):
    return pl.pallas_call(
        body,
        out_shape=out_shape,
        in_specs=in_specs,
        out_specs=out_specs,
        compiler_params=pltpu.CompilerParams(vmem_limit_bytes=limit),
        cost_estimate=pl.CostEstimate(flops=flops, bytes_accessed=moved, transcendentals=0),
        **more,
    )


def cuts(width):
    size = max(width // (4 * 256), 1) * 256
    edges = [i * size for i in range(4)] + [width]
    return list(zip(edges[:-1], edges[1:]))


def project_body(piece, vis_hbm, gain_hbm, proj_hbm, kv_ref, own_ref, vis, gain_ref, proj, vis_sems, proj_sems, gain_sem):
    rows, width = vis.shape
    gain_copy = pltpu.make_async_copy(gain_hbm, gain_ref, gain_sem)
    gain_copy.start()
    copies = []
    for n, (low, high) in enumerate(cuts(width)):
        vis_copy = pltpu.make_async_copy(vis_hbm.at[:, low:high], vis.at[:, low:high], vis_sems.at[n])
        proj_copy = pltpu.make_async_copy(proj_hbm.at[low:high, :], proj.at[low:high, :], proj_sems.at[n])
        vis_copy.start()
        proj_copy.start()
        copies.append((vis_copy, proj_copy))
    gain_copy.wait()
    squares = jnp.zeros((rows, HD), jnp.float32)
    total = jnp.zeros(kv_ref.shape, jnp.float32)
    for (low, high), (vis_copy, proj_copy) in zip(cuts(width), copies):
        vis_copy.wait()
        scaled = []
        for c in range(low, high, HD):
            wide = vis[:, c : c + HD].astype(jnp.float32)
            squares += wide * wide
            scaled.append((wide * gain_ref[c // HD : c // HD + 1, :]).astype(jnp.bfloat16))
        proj_copy.wait()
        total += jnp.dot(jnp.concatenate(scaled, axis=1), proj[low:high, :], preferred_element_type=jnp.float32)
    inverse = lax.rsqrt(jnp.sum(squares, axis=1, keepdims=True) / width + EPS)
    kv_ref[...] = (total * inverse).astype(jnp.bfloat16)
    parity, place = group_place()
    start = pl.multiple_of(parity * (rows // 2) + place * piece, piece)
    own_ref[...] = vis[pl.ds(start, piece), :]


def placed(before, rows, image_ref, text_ref):
    ahead = lax.broadcasted_iota(jnp.int32, (rows, rows), 0) - lax.broadcasted_iota(jnp.int32, (rows, rows), 1)
    pick = jnp.where(ahead == before, 1.0, 0.0).astype(jnp.bfloat16)
    image = jnp.dot(pick, image_ref[...], preferred_element_type=jnp.float32)
    row = lax.broadcasted_iota(jnp.int32, image.shape, 0)
    return jnp.where(row < before, text_ref[...].astype(jnp.float32), image).astype(jnp.bfloat16)


def place_body(seq_n, pieces_ref, image_ref, text_ref, out_ref):
    rows = image_ref.shape[0]
    before = pieces_ref[2 * held_image(lax.axis_index("seq"), seq_n)]
    out_ref[...] = placed(before, rows, image_ref, text_ref)


def heads_of(ref, heads):
    return jnp.concatenate([ref[:, h * HD : (h + 1) * HD] for h in heads], axis=0)


def head_groups(group, keys):
    together = group if keys <= 1024 else 1
    return [range(first, first + together) for first in range(0, group, together)]


def grad_parts(chosen, rows, scale, low_ref, dscore_ref, q_ref, g_ref, grad_refs):
    totals = [None] * len(chosen)
    for heads in head_groups(q_ref.shape[1] // HD, low_ref.shape[0]):
        q, g = heads_of(q_ref, heads), heads_of(g_ref, heads)
        span = slice(heads[0] * rows, (heads[-1] + 1) * rows)
        for n, r in enumerate(chosen):
            part = pl.ds(pl.multiple_of(r * rows, rows), rows)
            dkeys = jnp.dot(dscore_ref[part, span], q, preferred_element_type=jnp.float32)
            dvalues = jnp.dot(low_ref[part, span], g, preferred_element_type=jnp.float32)
            if totals[n] is not None:
                dkeys, dvalues = totals[n][0] + dkeys, totals[n][1] + dvalues
            totals[n] = dkeys, dvalues
    for (dkeys, dvalues), ref in zip(totals, grad_refs):
        ref[:, :HD] = (dkeys * scale).astype(jnp.bfloat16)
        ref[:, HD:] = dvalues.astype(jnp.bfloat16)


def weigh_body(seq_n, tables, backs, pieces_ref, q_ref, g_ref, text_ref, own_ref, raw_ref, *refs):
    count = len(tables)
    block_refs, (low_ref, dscore_ref, values_ref) = refs[:count], refs[count : count + 3]
    grad_refs = refs[count + 3 :]
    rows = q_ref.shape[0]
    group = q_ref.shape[1] // HD
    scale = 1.0 / math.sqrt(HD)
    me = lax.axis_index("seq")
    mine = placed(pieces_ref[2 * me], rows, raw_ref, text_ref)
    kv = jnp.concatenate([own_ref[...], mine] + [ref[...] for ref in block_refs], axis=0)
    keys, values = kv[:, :HD], kv[:, HD:]
    values_ref[...] = values
    images = [held_image(me, seq_n), me] + [pick_static(table, me) for table in tables]
    for heads in head_groups(group, kv.shape[0]):
        q, g = heads_of(q_ref, heads), heads_of(g_ref, heads)
        offset = lax.broadcasted_iota(jnp.int32, (rows, q.shape[0]), 0)
        offset = offset - lax.rem(lax.broadcasted_iota(jnp.int32, (rows, q.shape[0]), 1), rows)
        scores = dot(keys, q, ((1,), (1,)))
        scores = jnp.concatenate(
            [
                jnp.where(offset <= (me - image) * rows, scores[n * rows : (n + 1) * rows], NEG)
                for n, image in enumerate(images)
            ],
            axis=0,
        )
        top = jnp.max(scores, axis=0, keepdims=True)
        weights = jnp.exp2((scores - top) * (scale * math.log2(math.e)))
        weights = weights * (1.0 / jnp.sum(weights, axis=0, keepdims=True))
        low = weights.astype(jnp.bfloat16)
        dprob = dot(values, g, ((1,), (1,)))
        drift = jnp.sum(low.astype(jnp.float32) * dprob, axis=0, keepdims=True)
        span = slice(heads[0] * rows, (heads[-1] + 1) * rows)
        low_ref[:, span] = low
        dscore_ref[:, span] = (weights * (dprob - drift)).astype(jnp.bfloat16)
    early = [pick_static(table, me) for table in backs]
    grad_parts(early, rows, scale, low_ref, dscore_ref, q_ref, g_ref, grad_refs)


def mix_body(late, q_ref, g_ref, low_ref, dscore_ref, values_ref, out_ref, *grad_refs):
    rows = q_ref.shape[0]
    grad_parts(late, rows, 1.0 / math.sqrt(HD), low_ref, dscore_ref, q_ref, g_ref, grad_refs)
    for heads in head_groups(q_ref.shape[1] // HD, low_ref.shape[0]):
        span = slice(heads[0] * rows, (heads[-1] + 1) * rows)
        mixed = dot(values_ref[...], low_ref[:, span], ((0,), (0,)))
        for n, h in enumerate(heads):
            part = jnp.transpose(mixed[:, n * rows : (n + 1) * rows])
            out_ref[:, h * HD : (h + 1) * HD] = part.astype(jnp.bfloat16)


def back_body(seq_n, count, piece, pieces_ref, proj_ref, *refs):
    part_refs, (rest_ref, keep_ref, send_ref) = refs[:-3], refs[-3:]
    rows = part_refs[0].shape[0]
    before = pieces_ref[2 * held_image(lax.axis_index("seq"), seq_n)]
    parity, place = group_place()
    total = part_refs[0][...].astype(jnp.float32)
    for ref in part_refs[1:]:
        total += ref[...].astype(jnp.float32)
    slot = lax.broadcasted_iota(jnp.int32, (rows, rows), 0)
    group = lax.div(slot, piece)
    core = jnp.where(group < 2, group, jnp.where(group > count, 1, 0))
    step = jnp.where(group < 2, count - 1, lax.rem(group + count - 3, count - 1))
    to = ((core ^ parity) * count + (step ^ place)) * piece + lax.rem(slot, piece)
    source = lax.broadcasted_iota(jnp.int32, (rows, rows), 1)
    pick = jnp.where(source == to + before, 1.0, 0.0).astype(jnp.bfloat16)
    image_grad = jnp.dot(pick, total.astype(jnp.bfloat16), preferred_element_type=jnp.float32)
    image_grad = image_grad.astype(jnp.bfloat16)
    product = dot(image_grad[: 2 * piece], proj_ref[...], ((1,), (1,)))
    keep_ref[...] = product[:piece]
    send_ref[...] = product[piece:].astype(jnp.bfloat16)
    rest_ref[...] = image_grad[2 * piece :]


def rest_body(rest_ref, proj_ref, keep_ref, send_ref):
    half = rest_ref.shape[0] // 2
    product = dot(rest_ref[...], proj_ref[...], ((1,), (1,)))
    keep_ref[...] = product[:half]
    send_ref[...] = product[half:].astype(jnp.bfloat16)


def last_body(keep_ref, other_ref, send_ref):
    send_ref[...] = (keep_ref[...] + other_ref[...].astype(jnp.float32)).astype(jnp.bfloat16)


def pair_body(piece, keep_ref, other_ref, own_ref, *send_refs):
    own_ref[...] = keep_ref[:piece] + other_ref[:piece].astype(jnp.float32)
    for n, ref in enumerate(send_refs):
        part = slice((n + 1) * piece, (n + 2) * piece)
        ref[...] = (keep_ref[part] + other_ref[part].astype(jnp.float32)).astype(jnp.bfloat16)


def final_body(total_ref, own_ref, gain_ref, *refs):
    out_ref = refs[-1]
    width = own_ref.shape[1]
    square = stat = None
    scaled = []
    for c in range(0, width, HD):
        cols = slice(c, c + HD)
        total = total_ref[:, cols]
        for ref in refs[:-1]:
            total += ref[:, cols].astype(jnp.float32)
        own = own_ref[:, cols].astype(jnp.float32)
        grad = total * gain_ref[c // HD : c // HD + 1, :]
        scaled.append(grad)
        square = own * own if square is None else square + own * own
        stat = own * grad if stat is None else stat + own * grad
    inverse = lax.rsqrt(jnp.sum(square, axis=1, keepdims=True) / width + EPS)
    lead = inverse * inverse * inverse * (jnp.sum(stat, axis=1, keepdims=True) / width)
    for n, c in enumerate(range(0, width, HD)):
        own = own_ref[:, c : c + HD].astype(jnp.float32)
        out_ref[:, c : c + HD] = (scaled[n] * inverse - own * lead).astype(jnp.bfloat16)


def gather_body(count, chosen, *refs):
    part_refs, (out_hbm, sems) = refs[: len(chosen)], refs[-2:]
    piece = part_refs[0].shape[0]
    parity, place = group_place()
    copies = []
    for n, (ref, (core, step)) in enumerate(zip(part_refs, chosen)):
        row = ((parity ^ core) * count + (place ^ step)) * piece
        copy = pltpu.make_async_copy(ref, out_hbm.at[pl.ds(pl.multiple_of(row, piece), piece), :], sems.at[n])
        copy.start()
        copies.append(copy)
    for copy in copies:
        copy.wait()


def on_device(vis_rows, vis_gain, key_value_proj, pieces, text_kv, queries, grad_out):
    rows, width = vis_rows.shape
    columns = key_value_proj.shape[1]
    seq_n = lax.axis_size("seq")
    tp_n = lax.axis_size("tp")
    n = lax.axis_size("sec") * tp_n
    count = n // 2
    piece = rows // n
    bf16, f32 = jnp.bfloat16, jnp.float32
    names = ("sec", "tp")
    core_pairs = [(i, (i // tp_n ^ 1) * tp_n + i % tp_n) for i in range(n)]

    def far_pairs(step):
        pairs = []
        for i in range(n):
            sec, tp = divmod(i, tp_n)
            place = (sec // 2 * tp_n + tp) ^ step
            pairs.append((i, (place // tp_n * 2 + sec % 2) * tp_n + place % tp_n))
        return pairs

    gain = vis_gain.reshape(width // HD, HD)
    owners = [owner_block(j, seq_n) for j in range(seq_n)]
    held = [owners.index(b) for b in range(seq_n)]
    home = [(owners[j], j) for j in range(seq_n)]
    edges = {(owners[j], d) for j in range(seq_n) for d in range(j + 1, seq_n) if owners[j] != d}
    tables, forth, left = [], [], set(edges)
    for pairs in rounds_of(sorted(edges), seq_n):
        table = [seq_n] * seq_n
        for s, t in enumerate(pairs):
            if (s, t) in left:
                table[t] = held[s]
        left -= set(enumerate(pairs))
        tables.append(table)
        forth.append(list(enumerate(pairs)))
    text = lax.ppermute(text_kv, "seq", list(enumerate(owners)))
    chunks = len(cuts(width))
    hbm = pl.BlockSpec(memory_space=pltpu.HBM)
    image_kv, own_rows = call(
        functools.partial(project_body, piece),
        [jax.ShapeDtypeStruct((rows, columns), bf16), jax.ShapeDtypeStruct((piece, width), bf16)],
        [hbm, hbm, hbm],
        [WHOLE, WHOLE],
        2 * rows * width * columns,
        2 * width * (rows + columns),
        limit=WIDE_LIMIT,
        scratch_shapes=[
            pltpu.VMEM((rows, width), bf16),
            pltpu.VMEM(gain.shape, f32),
            pltpu.VMEM((width, columns), bf16),
            pltpu.SemaphoreType.DMA((chunks,)),
            pltpu.SemaphoreType.DMA((chunks,)),
            pltpu.SemaphoreType.DMA,
        ],
    )(vis_rows, gain, key_value_proj)
    raw = lax.ppermute(image_kv, "seq", home)
    block = call(
        functools.partial(place_body, seq_n),
        jax.ShapeDtypeStruct((rows, columns), bf16),
        [SCALARS, WHOLE, WHOLE],
        WHOLE,
        0,
        6 * rows * columns,
    )(pieces, image_kv, text)
    blocks = [lax.ppermute(block, "seq", pairs) for pairs in forth]
    total = 2 + len(blocks)
    pairs_back, backs = [], []
    for r in range(seq_n - 1, 0, -1):
        pairs_back.append([(d, d ^ r) for d in range(seq_n)])
        table = []
        for d in range(seq_n):
            block_of = [held[d], d] + [t[d] for t in tables]
            want = held[d ^ r]
            if want > d:
                want = max(block_of)
            table.append(block_of.index(want, 1))
        backs.append(table)
    kv_shape = jax.ShapeDtypeStruct((rows, columns), bf16)
    wide_shape = jax.ShapeDtypeStruct((total * rows, queries.shape[1] // HD * rows), bf16)
    low, dscore, values, *grads = call(
        functools.partial(weigh_body, seq_n, tables, backs),
        [wide_shape, wide_shape, jax.ShapeDtypeStruct((total * rows, HD), bf16)] + [kv_shape] * len(backs),
        [SCALARS] + [WHOLE] * (3 + total),
        [WHOLE] * (3 + len(backs)),
        8 * total * rows * rows * queries.shape[1],
        4 * rows * queries.shape[1] + 4 * total * rows * columns,
    )(pieces, queries, grad_out, text_kv, block, raw, *blocks)
    attended, own_grad = call(
        functools.partial(mix_body, [0]),
        [jax.ShapeDtypeStruct(queries.shape, bf16), kv_shape],
        [WHOLE] * 5,
        [WHOLE, WHOLE],
        2 * total * rows * rows * queries.shape[1],
        6 * rows * queries.shape[1] + 4 * total * rows * columns,
    )(queries, grad_out, low, dscore, values)
    parts = [lax.ppermute(g, "seq", pairs) for g, pairs in zip(grads, pairs_back)]

    def shape(height, dtype):
        return jax.ShapeDtypeStruct((height, width), dtype)

    rest, keep_last, send_last = call(
        functools.partial(back_body, seq_n, count, piece),
        [jax.ShapeDtypeStruct((rows - 2 * piece, columns), bf16), shape(piece, f32), shape(piece, bf16)],
        [SCALARS] + [WHOLE] * (2 + len(parts)),
        [WHOLE] * 3,
        4 * piece * width * columns,
        2 * width * columns + 6 * piece * width,
    )(pieces, key_value_proj, own_grad, *parts)
    other_last = lax.ppermute(send_last, names, core_pairs)
    height = rows // 2 - piece
    keep, send = call(
        rest_body,
        [shape(height, f32), shape(height, bf16)],
        [WHOLE, WHOLE],
        [WHOLE, WHOLE],
        4 * height * width * columns,
        2 * width * columns + 6 * height * width,
    )(rest, key_value_proj)
    other = lax.ppermute(send, names, core_pairs)
    weight = 64 * rows * width * columns
    far = call(last_body, shape(piece, bf16), [WHOLE, WHOLE], WHOLE, weight, 8 * piece * width)(keep_last, other_last)
    shares = [lax.ppermute(far, names, far_pairs(count - 1))]
    own_sum, *sends = call(
        functools.partial(pair_body, piece),
        [shape(piece, f32)] + [shape(piece, bf16)] * (count - 2),
        [WHOLE, WHOLE],
        [WHOLE] * (count - 1),
        0,
        8 * height * width,
    )(keep, other)
    steps = list(range(1, count))
    shares += [lax.ppermute(sends[d - 1], names, far_pairs(d)) for d in steps[-2::-1]]
    mine = call(
        final_body,
        jax.ShapeDtypeStruct((piece, width), bf16),
        [WHOLE] * (3 + len(shares)),
        WHOLE,
        0,
        12 * piece * width,
    )(own_sum, own_rows, gain, *shares)
    mines = {0: mine}
    for d in steps:
        mines[d] = lax.ppermute(mine, names, far_pairs(d))
    theirs = {d: lax.ppermute(mines[d], names, core_pairs) for d in range(count)}
    ready = {(core, d): part[d] for core, part in enumerate((mines, theirs)) for d in range(count)}
    order = sorted(ready, key=lambda key: (key[0], -key[1]))
    last = (1, count - 1)
    vis_grad = None
    for chosen in ([key for key in order if key != last], [last]):
        done = [] if vis_grad is None else [vis_grad]
        vis_grad = call(
            functools.partial(gather_body, count, chosen),
            shape(rows, bf16),
            [WHOLE] * len(chosen) + [hbm] * len(done),
            hbm,
            0,
            4 * piece * width * len(chosen),
            scratch_shapes=[pltpu.SemaphoreType.DMA((len(chosen),))],
            input_output_aliases={len(chosen): 0} if done else {},
        )(*[ready[key] for key in chosen], *done)
    return (attended, vis_grad)


def solution(mesh):
    in_specs = (
        P("seq", None),
        P(),
        P(None, ("sec", "tp")),
        P(),
        P("seq", ("sec", "tp")),
        P("seq", ("sec", "tp")),
        P("seq", ("sec", "tp")),
    )
    out_specs = (P("seq", ("sec", "tp")), P("seq", None))
    return jax.shard_map(
        on_device, mesh=mesh, in_specs=in_specs, out_specs=out_specs, check_vma=False
    )
```

```python
import functools
import itertools
import math

import jax
import jax.numpy as jnp
from jax import lax
from jax.experimental import pallas as pl
from jax.experimental.pallas import tpu as pltpu
from jax.sharding import PartitionSpec as P

HD = 128
EPS = 1e-06
NEG = -1e30
VMEM_LIMIT = 48 * 1024 * 1024
WIDE_LIMIT = 854 * 64 * 1024
WHOLE = pl.BlockSpec(memory_space=pltpu.VMEM)


def owner_block(image, count):
    half = count // 2
    return image - half if image >= half else half + (image + 1) % half


def held_image(block, count):
    half = count // 2
    return jnp.where(block < half, block + half, lax.rem(block + half - 1, half))


def flows(rounds, count):
    load = [0] * (2 * count)
    for pairs in rounds:
        for s, t in enumerate(pairs):
            for k in range(min(s, t), max(s, t)):
                load[2 * k + (t > s)] += 1
    return max(load), sum(load)


def rounds_of(edges, count):
    best = [tuple(d ^ r for d in range(count)) for r in range(count - 1, 0, -1)]
    if count > 4:
        return best
    whole = [p for p in itertools.permutations(range(count)) if all(s != t for s, t in enumerate(p))]
    for size in range(1, count):
        found = [c for c in itertools.combinations(whole, size) if all(any(p[s] == t for p in c) for s, t in edges)]
        if found:
            far = lambda p: max(abs(s - t) for s, t in enumerate(p))
            found = [sorted(c, key=far) for c in found]
            return min(found, key=lambda c: (flows(c, count)[0], flows(c[-1:], count), flows(c, count)))
    return best


def pick_static(table, index):
    value = jnp.int32(table[0])
    for n in range(1, len(table)):
        value = jnp.where(index == n, table[n], value)
    return value


def group_place():
    sec, tp = lax.axis_index("sec"), lax.axis_index("tp")
    return lax.rem(sec, 2), lax.div(sec, 2) * lax.axis_size("tp") + tp


def dot(a, b, dims):
    return lax.dot_general(a, b, (dims, ((), ())), preferred_element_type=jnp.float32)


def call(body, out_shape, in_specs, out_specs, flops, moved, limit=VMEM_LIMIT, **more):
    return pl.pallas_call(
        body,
        out_shape=out_shape,
        in_specs=in_specs,
        out_specs=out_specs,
        compiler_params=pltpu.CompilerParams(vmem_limit_bytes=limit),
        cost_estimate=pl.CostEstimate(flops=flops, bytes_accessed=moved, transcendentals=0),
        **more,
    )


def cuts(width):
    size = max(width // (4 * 256), 1) * 256
    edges = [i * size for i in range(4)] + [width]
    return list(zip(edges[:-1], edges[1:]))


def project_body(piece, vis_hbm, gain_hbm, proj_hbm, kv_ref, own_ref, vis, gain_ref, proj, vis_sems, proj_sems, gain_sem):
    rows, width = vis.shape
    gain_copy = pltpu.make_async_copy(gain_hbm, gain_ref, gain_sem)
    gain_copy.start()
    copies = []
    for n, (low, high) in enumerate(cuts(width)):
        vis_copy = pltpu.make_async_copy(vis_hbm.at[:, low:high], vis.at[:, low:high], vis_sems.at[n])
        proj_copy = pltpu.make_async_copy(proj_hbm.at[low:high, :], proj.at[low:high, :], proj_sems.at[n])
        vis_copy.start()
        proj_copy.start()
        copies.append((vis_copy, proj_copy))
    gain_copy.wait()
    squares = jnp.zeros((rows, HD), jnp.float32)
    total = jnp.zeros(kv_ref.shape, jnp.float32)
    for (low, high), (vis_copy, proj_copy) in zip(cuts(width), copies):
        vis_copy.wait()
        scaled = []
        for c in range(low, high, HD):
            wide = vis[:, c : c + HD].astype(jnp.float32)
            squares += wide * wide
            scaled.append((wide * gain_ref[c // HD : c // HD + 1, :]).astype(jnp.bfloat16))
        proj_copy.wait()
        total += jnp.dot(jnp.concatenate(scaled, axis=1), proj[low:high, :], preferred_element_type=jnp.float32)
    inverse = lax.rsqrt(jnp.sum(squares, axis=1, keepdims=True) / width + EPS)
    kv_ref[...] = (total * inverse).astype(jnp.bfloat16)
    parity, place = group_place()
    start = pl.multiple_of(parity * (rows // 2) + place * piece, piece)
    own_ref[...] = vis[pl.ds(start, piece), :]


def text_rows(pieces_ref, image):
    values = pieces_ref[...].astype(jnp.float32)
    lane = lax.broadcasted_iota(jnp.int32, values.shape, 1)
    return jnp.sum(jnp.where(lane == 2 * image, values, 0.0), axis=1, keepdims=True).astype(jnp.int32)


def placed(before, rows, image_ref, text_ref):
    ahead = lax.broadcasted_iota(jnp.int32, (rows, rows), 0) - lax.broadcasted_iota(jnp.int32, (rows, rows), 1)
    pick = jnp.where(ahead == before, 1.0, 0.0).astype(jnp.bfloat16)
    image = jnp.dot(pick, image_ref[...], preferred_element_type=jnp.float32)
    row = lax.broadcasted_iota(jnp.int32, image.shape, 0)
    return jnp.where(row < before, text_ref[...].astype(jnp.float32), image).astype(jnp.bfloat16)


def place_body(seq_n, pieces_ref, image_ref, text_ref, out_ref):
    rows = image_ref.shape[0]
    before = text_rows(pieces_ref, held_image(lax.axis_index("seq"), seq_n))
    out_ref[...] = placed(before, rows, image_ref, text_ref)


def heads_of(ref, heads):
    return jnp.concatenate([ref[:, h * HD : (h + 1) * HD] for h in heads], axis=0)


def head_groups(group, keys):
    together = group if keys <= 1024 else 1
    return [range(first, first + together) for first in range(0, group, together)]


def grad_parts(chosen, rows, scale, low_ref, dscore_ref, q_ref, g_ref, grad_refs):
    totals = [None] * len(chosen)
    for heads in head_groups(q_ref.shape[1] // HD, low_ref.shape[0]):
        q, g = heads_of(q_ref, heads), heads_of(g_ref, heads)
        span = slice(heads[0] * rows, (heads[-1] + 1) * rows)
        for n, r in enumerate(chosen):
            part = pl.ds(pl.multiple_of(r * rows, rows), rows)
            dkeys = jnp.dot(dscore_ref[part, span], q, preferred_element_type=jnp.float32)
            dvalues = jnp.dot(low_ref[part, span], g, preferred_element_type=jnp.float32)
            if totals[n] is not None:
                dkeys, dvalues = totals[n][0] + dkeys, totals[n][1] + dvalues
            totals[n] = dkeys, dvalues
    for (dkeys, dvalues), ref in zip(totals, grad_refs):
        ref[:, :HD] = (dkeys * scale).astype(jnp.bfloat16)
        ref[:, HD:] = dvalues.astype(jnp.bfloat16)


def weigh_body(seq_n, tables, backs, pieces_ref, q_ref, g_ref, text_ref, own_ref, raw_ref, *refs):
    count = len(tables)
    block_refs, (low_ref, dscore_ref, values_ref) = refs[:count], refs[count : count + 3]
    grad_refs, (scores, dprob) = refs[count + 3 : -2], refs[-2:]
    rows = q_ref.shape[0]
    group = q_ref.shape[1] // HD
    scale = 1.0 / math.sqrt(HD)
    me = lax.axis_index("seq")
    mine = placed(text_rows(pieces_ref, me), rows, raw_ref, text_ref)
    kv = jnp.concatenate([own_ref[...], mine] + [ref[...] for ref in block_refs], axis=0)
    keys, values = kv[:, :HD], kv[:, HD:]
    values_ref[...] = values
    images = [held_image(me, seq_n), me] + [pick_static(table, me) for table in tables]
    shifts = [jnp.where(image < me, 0.0, NEG) for image in images]
    seen = lax.broadcasted_iota(jnp.int32, (rows, rows), 0) <= lax.broadcasted_iota(jnp.int32, (rows, rows), 1)
    parts = [slice(n * rows, (n + 1) * rows) for n in range(len(images))]

    def score(n, cols):
        block = scores[parts[n], cols]
        return jnp.where(seen, block, NEG) if n == 1 else block + shifts[n]

    for heads in head_groups(group, kv.shape[0]):
        scores[...] = dot(keys, heads_of(q_ref, heads), ((1,), (1,)))
        dprob[...] = dot(values, heads_of(g_ref, heads), ((1,), (1,)))
        for h in heads:
            cols = slice((h - heads[0]) * rows, (h - heads[0] + 1) * rows)
            wide = slice(h * rows, (h + 1) * rows)
            top = score(0, cols)
            for n in range(1, len(parts)):
                top = jnp.maximum(top, score(n, cols))
            top = jnp.max(top, axis=0, keepdims=True)
            total = None
            for n, part in enumerate(parts):
                weights = jnp.exp2((score(n, cols) - top) * (scale * math.log2(math.e)))
                scores[part, cols] = weights
                total = weights if total is None else total + weights
            inverse = 1.0 / jnp.sum(total, axis=0, keepdims=True)
            drift = None
            for part in parts:
                weights = scores[part, cols] * inverse
                scores[part, cols] = weights
                low = weights.astype(jnp.bfloat16)
                low_ref[part, wide] = low
                term = low.astype(jnp.float32) * dprob[part, cols]
                drift = term if drift is None else drift + term
            drift = jnp.sum(drift, axis=0, keepdims=True)
            for part in parts:
                dscore_ref[part, wide] = (scores[part, cols] * (dprob[part, cols] - drift)).astype(jnp.bfloat16)
    early = [pick_static(table, me) for table in backs]
    grad_parts(early, rows, scale, low_ref, dscore_ref, q_ref, g_ref, grad_refs)


def mix_body(late, q_ref, g_ref, low_ref, dscore_ref, values_ref, out_ref, *grad_refs):
    rows = q_ref.shape[0]
    grad_parts(late, rows, 1.0 / math.sqrt(HD), low_ref, dscore_ref, q_ref, g_ref, grad_refs)
    for heads in head_groups(q_ref.shape[1] // HD, low_ref.shape[0]):
        span = slice(heads[0] * rows, (heads[-1] + 1) * rows)
        mixed = dot(values_ref[...], low_ref[:, span], ((0,), (0,)))
        for n, h in enumerate(heads):
            part = jnp.transpose(mixed[:, n * rows : (n + 1) * rows])
            out_ref[:, h * HD : (h + 1) * HD] = part.astype(jnp.bfloat16)


def back_body(seq_n, count, piece, pieces_ref, proj_ref, *refs):
    part_refs, (rest_ref, keep_ref, send_ref) = refs[:-3], refs[-3:]
    rows = part_refs[0].shape[0]
    before = text_rows(pieces_ref, held_image(lax.axis_index("seq"), seq_n))
    parity, place = group_place()
    total = part_refs[0][...].astype(jnp.float32)
    for ref in part_refs[1:]:
        total += ref[...].astype(jnp.float32)
    slot = lax.broadcasted_iota(jnp.int32, (rows, rows), 0)
    group = lax.div(slot, piece)
    core = jnp.where(group < 2, group, jnp.where(group > count, 1, 0))
    step = jnp.where(group < 2, count - 1, lax.rem(group + count - 3, count - 1))
    to = ((core ^ parity) * count + (step ^ place)) * piece + lax.rem(slot, piece)
    source = lax.broadcasted_iota(jnp.int32, (rows, rows), 1)
    pick = jnp.where(source == to + before, 1.0, 0.0).astype(jnp.bfloat16)
    image_grad = jnp.dot(pick, total.astype(jnp.bfloat16), preferred_element_type=jnp.float32)
    image_grad = image_grad.astype(jnp.bfloat16)
    product = dot(image_grad[: 2 * piece], proj_ref[...], ((1,), (1,)))
    keep_ref[...] = product[:piece]
    send_ref[...] = product[piece:].astype(jnp.bfloat16)
    rest_ref[...] = image_grad[2 * piece :]


def rest_body(rest_ref, proj_ref, keep_ref, send_ref):
    half = rest_ref.shape[0] // 2
    product = dot(rest_ref[...], proj_ref[...], ((1,), (1,)))
    keep_ref[...] = product[:half]
    send_ref[...] = product[half:].astype(jnp.bfloat16)


def last_body(keep_ref, other_ref, send_ref):
    send_ref[...] = (keep_ref[...] + other_ref[...].astype(jnp.float32)).astype(jnp.bfloat16)


def pair_body(piece, keep_ref, other_ref, own_ref, *send_refs):
    own_ref[...] = keep_ref[:piece] + other_ref[:piece].astype(jnp.float32)
    for n, ref in enumerate(send_refs):
        part = slice((n + 1) * piece, (n + 2) * piece)
        ref[...] = (keep_ref[part] + other_ref[part].astype(jnp.float32)).astype(jnp.bfloat16)


def final_body(total_ref, own_ref, gain_ref, *refs):
    out_ref = refs[-1]
    width = own_ref.shape[1]
    square = stat = None
    scaled = []
    for c in range(0, width, HD):
        cols = slice(c, c + HD)
        total = total_ref[:, cols]
        for ref in refs[:-1]:
            total += ref[:, cols].astype(jnp.float32)
        own = own_ref[:, cols].astype(jnp.float32)
        grad = total * gain_ref[c // HD : c // HD + 1, :]
        scaled.append(grad)
        square = own * own if square is None else square + own * own
        stat = own * grad if stat is None else stat + own * grad
    inverse = lax.rsqrt(jnp.sum(square, axis=1, keepdims=True) / width + EPS)
    lead = inverse * inverse * inverse * (jnp.sum(stat, axis=1, keepdims=True) / width)
    for n, c in enumerate(range(0, width, HD)):
        own = own_ref[:, c : c + HD].astype(jnp.float32)
        out_ref[:, c : c + HD] = (scaled[n] * inverse - own * lead).astype(jnp.bfloat16)


def gather_body(count, chosen, *refs):
    part_refs, (out_hbm, sems) = refs[: len(chosen)], refs[-2:]
    piece = part_refs[0].shape[0]
    parity, place = group_place()
    copies = []
    for n, (ref, (core, step)) in enumerate(zip(part_refs, chosen)):
        row = ((parity ^ core) * count + (place ^ step)) * piece
        copy = pltpu.make_async_copy(ref, out_hbm.at[pl.ds(pl.multiple_of(row, piece), piece), :], sems.at[n])
        copy.start()
        copies.append(copy)
    for copy in copies:
        copy.wait()


def on_device(vis_rows, vis_gain, key_value_proj, pieces, text_kv, queries, grad_out):
    rows, width = vis_rows.shape
    columns = key_value_proj.shape[1]
    seq_n = lax.axis_size("seq")
    tp_n = lax.axis_size("tp")
    n = lax.axis_size("sec") * tp_n
    count = n // 2
    piece = rows // n
    bf16, f32 = jnp.bfloat16, jnp.float32
    names = ("sec", "tp")
    core_pairs = [(i, (i // tp_n ^ 1) * tp_n + i % tp_n) for i in range(n)]

    def far_pairs(step):
        pairs = []
        for i in range(n):
            sec, tp = divmod(i, tp_n)
            place = (sec // 2 * tp_n + tp) ^ step
            pairs.append((i, (place // tp_n * 2 + sec % 2) * tp_n + place % tp_n))
        return pairs

    gain = vis_gain.reshape(width // HD, HD)
    pieces = pieces.reshape(1, -1)
    owners = [owner_block(j, seq_n) for j in range(seq_n)]
    held = [owners.index(b) for b in range(seq_n)]
    home = [(owners[j], j) for j in range(seq_n)]
    edges = {(owners[j], d) for j in range(seq_n) for d in range(j + 1, seq_n) if owners[j] != d}
    tables, forth, left = [], [], set(edges)
    for pairs in rounds_of(sorted(edges), seq_n):
        table = [seq_n] * seq_n
        for s, t in enumerate(pairs):
            if (s, t) in left:
                table[t] = held[s]
        left -= set(enumerate(pairs))
        tables.append(table)
        forth.append(list(enumerate(pairs)))
    text = lax.ppermute(text_kv, "seq", list(enumerate(owners)))
    chunks = len(cuts(width))
    hbm = pl.BlockSpec(memory_space=pltpu.HBM)
    image_kv, own_rows = call(
        functools.partial(project_body, piece),
        [jax.ShapeDtypeStruct((rows, columns), bf16), jax.ShapeDtypeStruct((piece, width), bf16)],
        [hbm, hbm, hbm],
        [WHOLE, WHOLE],
        2 * rows * width * columns,
        2 * width * (rows + columns),
        limit=WIDE_LIMIT,
        scratch_shapes=[
            pltpu.VMEM((rows, width), bf16),
            pltpu.VMEM(gain.shape, f32),
            pltpu.VMEM((width, columns), bf16),
            pltpu.SemaphoreType.DMA((chunks,)),
            pltpu.SemaphoreType.DMA((chunks,)),
            pltpu.SemaphoreType.DMA,
        ],
    )(vis_rows, gain, key_value_proj)
    raw = lax.ppermute(image_kv, "seq", home)
    block = call(
        functools.partial(place_body, seq_n),
        jax.ShapeDtypeStruct((rows, columns), bf16),
        [WHOLE] * 3,
        WHOLE,
        0,
        6 * rows * columns,
    )(pieces, image_kv, text)
    blocks = [lax.ppermute(block, "seq", pairs) for pairs in forth]
    total = 2 + len(blocks)
    pairs_back, backs = [], []
    for r in sorted(range(1, seq_n), key=lambda r: (r < seq_n // 2, r)):
        pairs_back.append([(d, d ^ r) for d in range(seq_n)])
        table = []
        for d in range(seq_n):
            block_of = [held[d], d] + [t[d] for t in tables]
            want = held[d ^ r]
            if want > d:
                want = max(block_of)
            table.append(block_of.index(want, 1))
        backs.append(table)
    kv_shape = jax.ShapeDtypeStruct((rows, columns), bf16)
    wide_shape = jax.ShapeDtypeStruct((total * rows, queries.shape[1] // HD * rows), bf16)
    low, dscore, values, *grads = call(
        functools.partial(weigh_body, seq_n, tables, backs),
        [wide_shape, wide_shape, jax.ShapeDtypeStruct((total * rows, HD), bf16)] + [kv_shape] * len(backs),
        [WHOLE] * (4 + total),
        [WHOLE] * (3 + len(backs)),
        8 * total * rows * rows * queries.shape[1],
        4 * rows * queries.shape[1] + 4 * total * rows * columns,
        scratch_shapes=[pltpu.VMEM((total * rows, len(head_groups(queries.shape[1] // HD, total * rows)[0]) * rows), f32)] * 2,
    )(pieces, queries, grad_out, text_kv, block, raw, *blocks)
    attended, own_grad = call(
        functools.partial(mix_body, [0]),
        [jax.ShapeDtypeStruct(queries.shape, bf16), kv_shape],
        [WHOLE] * 5,
        [WHOLE, WHOLE],
        2 * total * rows * rows * queries.shape[1],
        6 * rows * queries.shape[1] + 4 * total * rows * columns,
    )(queries, grad_out, low, dscore, values)
    parts = [lax.ppermute(g, "seq", pairs) for g, pairs in zip(grads, pairs_back)]

    def shape(height, dtype):
        return jax.ShapeDtypeStruct((height, width), dtype)

    rest, keep_last, send_last = call(
        functools.partial(back_body, seq_n, count, piece),
        [jax.ShapeDtypeStruct((rows - 2 * piece, columns), bf16), shape(piece, f32), shape(piece, bf16)],
        [WHOLE] * (3 + len(parts)),
        [WHOLE] * 3,
        4 * piece * width * columns,
        2 * width * columns + 6 * piece * width,
    )(pieces, key_value_proj, own_grad, *parts)
    other_last = lax.ppermute(send_last, names, core_pairs)
    height = rows // 2 - piece
    keep, send = call(
        rest_body,
        [shape(height, f32), shape(height, bf16)],
        [WHOLE, WHOLE],
        [WHOLE, WHOLE],
        4 * height * width * columns,
        2 * width * columns + 6 * height * width,
    )(rest, key_value_proj)
    other = lax.ppermute(send, names, core_pairs)
    weight = 64 * rows * width * columns
    far = call(last_body, shape(piece, bf16), [WHOLE, WHOLE], WHOLE, weight, 8 * piece * width)(keep_last, other_last)
    shares = [lax.ppermute(far, names, far_pairs(count - 1))]
    own_sum, *sends = call(
        functools.partial(pair_body, piece),
        [shape(piece, f32)] + [shape(piece, bf16)] * (count - 2),
        [WHOLE, WHOLE],
        [WHOLE] * (count - 1),
        0,
        8 * height * width,
    )(keep, other)
    steps = list(range(1, count))
    shares += [lax.ppermute(sends[d - 1], names, far_pairs(d)) for d in steps[-2::-1]]
    mine = call(
        final_body,
        jax.ShapeDtypeStruct((piece, width), bf16),
        [WHOLE] * (3 + len(shares)),
        WHOLE,
        0,
        12 * piece * width,
    )(own_sum, own_rows, gain, *shares)
    mines = {0: mine}
    for d in steps:
        mines[d] = lax.ppermute(mine, names, far_pairs(d))
    theirs = {d: lax.ppermute(mines[d], names, core_pairs) for d in range(count)}
    ready = {(core, d): part[d] for core, part in enumerate((mines, theirs)) for d in range(count)}
    early = [key for key in sorted(ready) if key[0] == 0 or key[1] in (0, count - 1)]
    vis_grad = None
    for chosen in (early, [key for key in sorted(ready) if key not in early]):
        done = [] if vis_grad is None else [vis_grad]
        vis_grad = call(
            functools.partial(gather_body, count, chosen),
            shape(rows, bf16),
            [WHOLE] * len(chosen) + [hbm] * len(done),
            hbm,
            0,
            4 * piece * width * len(chosen),
            scratch_shapes=[pltpu.SemaphoreType.DMA((len(chosen),))],
            input_output_aliases={len(chosen): 0} if done else {},
        )(*[ready[key] for key in chosen], *done)
    return (attended, vis_grad)


def solution(mesh):
    in_specs = (
        P("seq", None),
        P(),
        P(None, ("sec", "tp")),
        P(),
        P("seq", ("sec", "tp")),
        P("seq", ("sec", "tp")),
        P("seq", ("sec", "tp")),
    )
    out_specs = (P("seq", ("sec", "tp")), P("seq", None))
    return jax.shard_map(
        on_device, mesh=mesh, in_specs=in_specs, out_specs=out_specs, check_vma=False
    )
```

```python
import functools
import itertools
import math

import jax
import jax.numpy as jnp
from jax import lax
from jax.experimental import pallas as pl
from jax.experimental.pallas import tpu as pltpu
from jax.sharding import PartitionSpec as P

HD = 128
EPS = 1e-06
NEG = -1e30
VMEM_LIMIT = 48 * 1024 * 1024
WIDE_LIMIT = 854 * 64 * 1024
WHOLE = pl.BlockSpec(memory_space=pltpu.VMEM)


def owner_block(image, count):
    half = count // 2
    return image - half if image >= half else half + (image + 1) % half


def held_image(block, count):
    half = count // 2
    return jnp.where(block < half, block + half, lax.rem(block + half - 1, half))


def flows(rounds, count):
    load = [0] * (2 * count)
    for pairs in rounds:
        for s, t in enumerate(pairs):
            for k in range(min(s, t), max(s, t)):
                load[2 * k + (t > s)] += 1
    return max(load), sum(load)


def rounds_of(edges, count):
    best = [tuple(d ^ r for d in range(count)) for r in range(count - 1, 0, -1)]
    if count > 4:
        return best
    whole = [p for p in itertools.permutations(range(count)) if all(s != t for s, t in enumerate(p))]
    for size in range(1, count):
        found = [c for c in itertools.combinations(whole, size) if all(any(p[s] == t for p in c) for s, t in edges)]
        if found:
            far = lambda p: max(abs(s - t) for s, t in enumerate(p))
            found = [sorted(c, key=far) for c in found]
            return min(found, key=lambda c: (flows(c, count)[0], flows(c[-1:], count), flows(c, count)))
    return best


def pick_static(table, index):
    value = jnp.int32(table[0])
    for n in range(1, len(table)):
        value = jnp.where(index == n, table[n], value)
    return value


def group_place():
    sec, tp = lax.axis_index("sec"), lax.axis_index("tp")
    return lax.rem(sec, 2), lax.div(sec, 2) * lax.axis_size("tp") + tp


def dot(a, b, dims):
    return lax.dot_general(a, b, (dims, ((), ())), preferred_element_type=jnp.float32)


def call(body, out_shape, in_specs, out_specs, flops, moved, limit=VMEM_LIMIT, **more):
    return pl.pallas_call(
        body,
        out_shape=out_shape,
        in_specs=in_specs,
        out_specs=out_specs,
        compiler_params=pltpu.CompilerParams(vmem_limit_bytes=limit),
        cost_estimate=pl.CostEstimate(flops=flops, bytes_accessed=moved, transcendentals=0),
        **more,
    )


def cuts(width):
    size = max(width // (4 * 256), 1) * 256
    edges = [i * size for i in range(4)] + [width]
    return list(zip(edges[:-1], edges[1:]))


def project_body(piece, vis_hbm, gain_hbm, proj_hbm, kv_ref, own_ref, vis, gain_ref, proj, vis_sems, proj_sems, gain_sem):
    rows, width = vis.shape
    gain_copy = pltpu.make_async_copy(gain_hbm, gain_ref, gain_sem)
    gain_copy.start()
    copies = []
    for n, (low, high) in enumerate(cuts(width)):
        vis_copy = pltpu.make_async_copy(vis_hbm.at[:, low:high], vis.at[:, low:high], vis_sems.at[n])
        proj_copy = pltpu.make_async_copy(proj_hbm.at[low:high, :], proj.at[low:high, :], proj_sems.at[n])
        vis_copy.start()
        proj_copy.start()
        copies.append((vis_copy, proj_copy))
    gain_copy.wait()
    squares = jnp.zeros((rows, HD), jnp.float32)
    total = jnp.zeros(kv_ref.shape, jnp.float32)
    for (low, high), (vis_copy, proj_copy) in zip(cuts(width), copies):
        vis_copy.wait()
        scaled = []
        for c in range(low, high, HD):
            wide = vis[:, c : c + HD].astype(jnp.float32)
            squares += wide * wide
            scaled.append((wide * gain_ref[c // HD : c // HD + 1, :]).astype(jnp.bfloat16))
        proj_copy.wait()
        total += jnp.dot(jnp.concatenate(scaled, axis=1), proj[low:high, :], preferred_element_type=jnp.float32)
    inverse = lax.rsqrt(jnp.sum(squares, axis=1, keepdims=True) / width + EPS)
    kv_ref[...] = (total * inverse).astype(jnp.bfloat16)
    parity, place = group_place()
    start = pl.multiple_of(parity * (rows // 2) + place * piece, piece)
    own_ref[...] = vis[pl.ds(start, piece), :]


def text_rows(pieces_ref, image):
    values = pieces_ref[...].astype(jnp.float32)
    lane = lax.broadcasted_iota(jnp.int32, values.shape, 1)
    return jnp.sum(jnp.where(lane == 2 * image, values, 0.0), axis=1, keepdims=True).astype(jnp.int32)


def placed(before, rows, image_ref, text_ref):
    ahead = lax.broadcasted_iota(jnp.int32, (rows, rows), 0) - lax.broadcasted_iota(jnp.int32, (rows, rows), 1)
    pick = jnp.where(ahead == before, 1.0, 0.0).astype(jnp.bfloat16)
    image = jnp.dot(pick, image_ref[...], preferred_element_type=jnp.float32)
    row = lax.broadcasted_iota(jnp.int32, image.shape, 0)
    return jnp.where(row < before, text_ref[...].astype(jnp.float32), image).astype(jnp.bfloat16)


def place_body(seq_n, pieces_ref, image_ref, text_ref, out_ref):
    rows = image_ref.shape[0]
    before = text_rows(pieces_ref, held_image(lax.axis_index("seq"), seq_n))
    out_ref[...] = placed(before, rows, image_ref, text_ref)


def heads_of(ref, heads):
    return jnp.concatenate([ref[:, h * HD : (h + 1) * HD] for h in heads], axis=0)


def head_groups(group, keys):
    together = group if keys <= 1024 else 1
    return [range(first, first + together) for first in range(0, group, together)]


def grad_parts(chosen, rows, scale, low_ref, dscore_ref, q_ref, g_ref, grad_refs):
    totals = [None] * len(chosen)
    for heads in head_groups(q_ref.shape[1] // HD, low_ref.shape[0]):
        q, g = heads_of(q_ref, heads), heads_of(g_ref, heads)
        span = slice(heads[0] * rows, (heads[-1] + 1) * rows)
        for n, r in enumerate(chosen):
            part = pl.ds(pl.multiple_of(r * rows, rows), rows)
            dkeys = jnp.dot(dscore_ref[part, span], q, preferred_element_type=jnp.float32)
            dvalues = jnp.dot(low_ref[part, span], g, preferred_element_type=jnp.float32)
            if totals[n] is not None:
                dkeys, dvalues = totals[n][0] + dkeys, totals[n][1] + dvalues
            totals[n] = dkeys, dvalues
    for (dkeys, dvalues), ref in zip(totals, grad_refs):
        ref[:, :HD] = (dkeys * scale).astype(jnp.bfloat16)
        ref[:, HD:] = dvalues.astype(jnp.bfloat16)


def weigh_body(seq_n, tables, backs, pieces_ref, q_ref, g_ref, text_ref, own_ref, raw_ref, *refs):
    count = len(tables)
    block_refs, (low_ref, dscore_ref, values_ref) = refs[:count], refs[count : count + 3]
    grad_refs, (scores, dprob) = refs[count + 3 : -2], refs[-2:]
    rows = q_ref.shape[0]
    group = q_ref.shape[1] // HD
    scale = 1.0 / math.sqrt(HD)
    me = lax.axis_index("seq")
    mine = placed(text_rows(pieces_ref, me), rows, raw_ref, text_ref)
    kv = jnp.concatenate([own_ref[...], mine] + [ref[...] for ref in block_refs], axis=0)
    keys, values = kv[:, :HD], kv[:, HD:]
    values_ref[...] = values
    images = [held_image(me, seq_n), me] + [pick_static(table, me) for table in tables]
    shifts = [jnp.where(image < me, 0.0, NEG) for image in images]
    seen = lax.broadcasted_iota(jnp.int32, (rows, rows), 0) <= lax.broadcasted_iota(jnp.int32, (rows, rows), 1)
    parts = [slice(n * rows, (n + 1) * rows) for n in range(len(images))]

    def score(n, cols):
        block = scores[parts[n], cols]
        return jnp.where(seen, block, NEG) if n == 1 else block + shifts[n]

    for heads in head_groups(group, kv.shape[0]):
        scores[...] = dot(keys, heads_of(q_ref, heads), ((1,), (1,)))
        dprob[...] = dot(values, heads_of(g_ref, heads), ((1,), (1,)))
        for h in heads:
            cols = slice((h - heads[0]) * rows, (h - heads[0] + 1) * rows)
            wide = slice(h * rows, (h + 1) * rows)
            top = score(0, cols)
            for n in range(1, len(parts)):
                top = jnp.maximum(top, score(n, cols))
            top = jnp.max(top, axis=0, keepdims=True)
            total = None
            for n, part in enumerate(parts):
                weights = jnp.exp2((score(n, cols) - top) * (scale * math.log2(math.e)))
                scores[part, cols] = weights
                total = weights if total is None else total + weights
            inverse = 1.0 / jnp.sum(total, axis=0, keepdims=True)
            drift = None
            for part in parts:
                weights = scores[part, cols] * inverse
                scores[part, cols] = weights
                low = weights.astype(jnp.bfloat16)
                low_ref[part, wide] = low
                term = low.astype(jnp.float32) * dprob[part, cols]
                drift = term if drift is None else drift + term
            drift = jnp.sum(drift, axis=0, keepdims=True)
            for part in parts:
                dscore_ref[part, wide] = (scores[part, cols] * (dprob[part, cols] - drift)).astype(jnp.bfloat16)
    early = [pick_static(table, me) for table in backs]
    grad_parts(early, rows, scale, low_ref, dscore_ref, q_ref, g_ref, grad_refs)


def mix_body(late, q_ref, g_ref, low_ref, dscore_ref, values_ref, out_ref, *grad_refs):
    rows = q_ref.shape[0]
    grad_parts(late, rows, 1.0 / math.sqrt(HD), low_ref, dscore_ref, q_ref, g_ref, grad_refs)
    for heads in head_groups(q_ref.shape[1] // HD, low_ref.shape[0]):
        span = slice(heads[0] * rows, (heads[-1] + 1) * rows)
        mixed = dot(values_ref[...], low_ref[:, span], ((0,), (0,)))
        for n, h in enumerate(heads):
            part = jnp.transpose(mixed[:, n * rows : (n + 1) * rows])
            out_ref[:, h * HD : (h + 1) * HD] = part.astype(jnp.bfloat16)


def back_body(seq_n, count, piece, first, pieces_ref, proj_ref, *refs):
    part_refs, (rest_ref, keep_ref, send_ref) = refs[:-3], refs[-3:]
    rows = part_refs[0].shape[0]
    before = text_rows(pieces_ref, held_image(lax.axis_index("seq"), seq_n))
    parity, place = group_place()
    total = part_refs[0][...].astype(jnp.float32)
    for ref in part_refs[1:]:
        total += ref[...].astype(jnp.float32)
    slot = lax.broadcasted_iota(jnp.int32, (rows, rows), 0)
    group = lax.div(slot, piece)
    core = jnp.where(group < 2, group, jnp.where(group > count, 1, 0))
    step = lax.rem(group + count - 3, count - 1)
    step = jnp.where(group < 2, first, jnp.where(step >= first, step + 1, step))
    to = ((core ^ parity) * count + (step ^ place)) * piece + lax.rem(slot, piece)
    source = lax.broadcasted_iota(jnp.int32, (rows, rows), 1)
    pick = jnp.where(source == to + before, 1.0, 0.0).astype(jnp.bfloat16)
    image_grad = jnp.dot(pick, total.astype(jnp.bfloat16), preferred_element_type=jnp.float32)
    image_grad = image_grad.astype(jnp.bfloat16)
    product = dot(image_grad[: 2 * piece], proj_ref[...], ((1,), (1,)))
    keep_ref[...] = product[:piece]
    send_ref[...] = product[piece:].astype(jnp.bfloat16)
    rest_ref[...] = image_grad[2 * piece :]


def rest_body(rest_ref, proj_ref, keep_ref, send_ref):
    half = rest_ref.shape[0] // 2
    product = dot(rest_ref[...], proj_ref[...], ((1,), (1,)))
    keep_ref[...] = product[:half]
    send_ref[...] = product[half:].astype(jnp.bfloat16)


def last_body(keep_ref, other_ref, send_ref):
    send_ref[...] = (keep_ref[...] + other_ref[...].astype(jnp.float32)).astype(jnp.bfloat16)


def pair_body(piece, keep_ref, other_ref, own_ref, *send_refs):
    own_ref[...] = keep_ref[:piece] + other_ref[:piece].astype(jnp.float32)
    for n, ref in enumerate(send_refs):
        part = slice((n + 1) * piece, (n + 2) * piece)
        ref[...] = (keep_ref[part] + other_ref[part].astype(jnp.float32)).astype(jnp.bfloat16)


def final_body(total_ref, own_ref, gain_ref, *refs):
    out_ref = refs[-1]
    width = own_ref.shape[1]
    square = stat = None
    scaled = []
    for c in range(0, width, HD):
        cols = slice(c, c + HD)
        total = total_ref[:, cols]
        for ref in refs[:-1]:
            total += ref[:, cols].astype(jnp.float32)
        own = own_ref[:, cols].astype(jnp.float32)
        grad = total * gain_ref[c // HD : c // HD + 1, :]
        scaled.append(grad)
        square = own * own if square is None else square + own * own
        stat = own * grad if stat is None else stat + own * grad
    inverse = lax.rsqrt(jnp.sum(square, axis=1, keepdims=True) / width + EPS)
    lead = inverse * inverse * inverse * (jnp.sum(stat, axis=1, keepdims=True) / width)
    for n, c in enumerate(range(0, width, HD)):
        own = own_ref[:, c : c + HD].astype(jnp.float32)
        out_ref[:, c : c + HD] = (scaled[n] * inverse - own * lead).astype(jnp.bfloat16)


def gather_body(count, chosen, *refs):
    part_refs, (out_hbm, sems) = refs[: len(chosen)], refs[-2:]
    piece = part_refs[0].shape[0]
    parity, place = group_place()
    copies = []
    for n, (ref, (core, step)) in enumerate(zip(part_refs, chosen)):
        row = ((parity ^ core) * count + (place ^ step)) * piece
        copy = pltpu.make_async_copy(ref, out_hbm.at[pl.ds(pl.multiple_of(row, piece), piece), :], sems.at[n])
        copy.start()
        copies.append(copy)
    for copy in copies:
        copy.wait()


def on_device(vis_rows, vis_gain, key_value_proj, pieces, text_kv, queries, grad_out):
    rows, width = vis_rows.shape
    columns = key_value_proj.shape[1]
    seq_n = lax.axis_size("seq")
    tp_n = lax.axis_size("tp")
    n = lax.axis_size("sec") * tp_n
    count = n // 2
    piece = rows // n
    bf16, f32 = jnp.bfloat16, jnp.float32
    names = ("sec", "tp")
    core_pairs = [(i, (i // tp_n ^ 1) * tp_n + i % tp_n) for i in range(n)]

    def far_pairs(step):
        pairs = []
        for i in range(n):
            sec, tp = divmod(i, tp_n)
            place = (sec // 2 * tp_n + tp) ^ step
            pairs.append((i, (place // tp_n * 2 + sec % 2) * tp_n + place % tp_n))
        return pairs

    gain = vis_gain.reshape(width // HD, HD)
    pieces = pieces.reshape(1, -1)
    owners = [owner_block(j, seq_n) for j in range(seq_n)]
    held = [owners.index(b) for b in range(seq_n)]
    home = [(owners[j], j) for j in range(seq_n)]
    edges = {(owners[j], d) for j in range(seq_n) for d in range(j + 1, seq_n) if owners[j] != d}
    tables, forth, left = [], [], set(edges)
    for pairs in rounds_of(sorted(edges), seq_n):
        table = [seq_n] * seq_n
        for s, t in enumerate(pairs):
            if (s, t) in left:
                table[t] = held[s]
        left -= set(enumerate(pairs))
        tables.append(table)
        forth.append(list(enumerate(pairs)))
    text = lax.ppermute(text_kv, "seq", list(enumerate(owners)))
    chunks = len(cuts(width))
    hbm = pl.BlockSpec(memory_space=pltpu.HBM)
    image_kv, own_rows = call(
        functools.partial(project_body, piece),
        [jax.ShapeDtypeStruct((rows, columns), bf16), jax.ShapeDtypeStruct((piece, width), bf16)],
        [hbm, hbm, hbm],
        [WHOLE, WHOLE],
        2 * rows * width * columns,
        2 * width * (rows + columns),
        limit=WIDE_LIMIT,
        scratch_shapes=[
            pltpu.VMEM((rows, width), bf16),
            pltpu.VMEM(gain.shape, f32),
            pltpu.VMEM((width, columns), bf16),
            pltpu.SemaphoreType.DMA((chunks,)),
            pltpu.SemaphoreType.DMA((chunks,)),
            pltpu.SemaphoreType.DMA,
        ],
    )(vis_rows, gain, key_value_proj)
    raw = lax.ppermute(image_kv, "seq", home)
    block = call(
        functools.partial(place_body, seq_n),
        jax.ShapeDtypeStruct((rows, columns), bf16),
        [WHOLE] * 3,
        WHOLE,
        0,
        6 * rows * columns,
    )(pieces, image_kv, text)
    blocks = [lax.ppermute(block, "seq", pairs) for pairs in forth]
    total = 2 + len(blocks)
    pairs_back, backs = [], []
    for r in sorted(range(1, seq_n), key=lambda r: (r < seq_n // 2, r)):
        pairs_back.append([(d, d ^ r) for d in range(seq_n)])
        table = []
        for d in range(seq_n):
            block_of = [held[d], d] + [t[d] for t in tables]
            want = held[d ^ r]
            if want > d:
                want = max(block_of)
            table.append(block_of.index(want, 1))
        backs.append(table)
    kv_shape = jax.ShapeDtypeStruct((rows, columns), bf16)
    wide_shape = jax.ShapeDtypeStruct((total * rows, queries.shape[1] // HD * rows), bf16)
    low, dscore, values, *grads = call(
        functools.partial(weigh_body, seq_n, tables, backs),
        [wide_shape, wide_shape, jax.ShapeDtypeStruct((total * rows, HD), bf16)] + [kv_shape] * len(backs),
        [WHOLE] * (4 + total),
        [WHOLE] * (3 + len(backs)),
        8 * total * rows * rows * queries.shape[1],
        4 * rows * queries.shape[1] + 4 * total * rows * columns,
        scratch_shapes=[pltpu.VMEM((total * rows, len(head_groups(queries.shape[1] // HD, total * rows)[0]) * rows), f32)] * 2,
    )(pieces, queries, grad_out, text_kv, block, raw, *blocks)
    attended, own_grad = call(
        functools.partial(mix_body, [0]),
        [jax.ShapeDtypeStruct(queries.shape, bf16), kv_shape],
        [WHOLE] * 5,
        [WHOLE, WHOLE],
        2 * total * rows * rows * queries.shape[1],
        6 * rows * queries.shape[1] + 4 * total * rows * columns,
    )(queries, grad_out, low, dscore, values)
    parts = [lax.ppermute(g, "seq", pairs) for g, pairs in zip(grads, pairs_back)]

    def shape(height, dtype):
        return jax.ShapeDtypeStruct((height, width), dtype)

    first, *others = [1] + list(range(count - 1, 1, -1))
    rest, keep_last, send_last = call(
        functools.partial(back_body, seq_n, count, piece, first),
        [jax.ShapeDtypeStruct((rows - 2 * piece, columns), bf16), shape(piece, f32), shape(piece, bf16)],
        [WHOLE] * (3 + len(parts)),
        [WHOLE] * 3,
        4 * piece * width * columns,
        2 * width * columns + 6 * piece * width,
    )(pieces, key_value_proj, own_grad, *parts)
    other_last = lax.ppermute(send_last, names, core_pairs)
    height = rows // 2 - piece
    keep, send = call(
        rest_body,
        [shape(height, f32), shape(height, bf16)],
        [WHOLE, WHOLE],
        [WHOLE, WHOLE],
        4 * height * width * columns,
        2 * width * columns + 6 * height * width,
    )(rest, key_value_proj)
    other = lax.ppermute(send, names, core_pairs)
    weight = 64 * rows * width * columns
    far = call(last_body, shape(piece, bf16), [WHOLE, WHOLE], WHOLE, weight, 8 * piece * width)(keep_last, other_last)
    shares = [lax.ppermute(far, names, far_pairs(first))]
    own_sum, *sends = call(
        functools.partial(pair_body, piece),
        [shape(piece, f32)] + [shape(piece, bf16)] * (count - 2),
        [WHOLE, WHOLE],
        [WHOLE] * (count - 1),
        0,
        8 * height * width,
    )(keep, other)
    shares += [lax.ppermute(sends[d - 2], names, far_pairs(d)) for d in others]
    mine = call(
        final_body,
        jax.ShapeDtypeStruct((piece, width), bf16),
        [WHOLE] * (3 + len(shares)),
        WHOLE,
        0,
        12 * piece * width,
    )(own_sum, own_rows, gain, *shares)
    mines = {0: mine}
    for d in [first] + others:
        mines[d] = lax.ppermute(mine, names, far_pairs(d))
    theirs = {d: lax.ppermute(mines[d], names, core_pairs) for d in range(count)}
    ready = {(core, d): part[d] for core, part in enumerate((mines, theirs)) for d in range(count)}
    rank = [0] + others[::-1] + [first]
    order = sorted(ready, key=lambda key: (key[0], rank.index(key[1])))
    early = [key for key in order if key[0] == 0 or key[1] in (0, first)]
    vis_grad = None
    for chosen in (early, [key for key in order if key not in early]):
        done = [] if vis_grad is None else [vis_grad]
        vis_grad = call(
            functools.partial(gather_body, count, chosen),
            shape(rows, bf16),
            [WHOLE] * len(chosen) + [hbm] * len(done),
            hbm,
            0,
            4 * piece * width * len(chosen),
            scratch_shapes=[pltpu.SemaphoreType.DMA((len(chosen),))],
            input_output_aliases={len(chosen): 0} if done else {},
        )(*[ready[key] for key in chosen], *done)
    return (attended, vis_grad)


def solution(mesh):
    in_specs = (
        P("seq", None),
        P(),
        P(None, ("sec", "tp")),
        P(),
        P("seq", ("sec", "tp")),
        P("seq", ("sec", "tp")),
        P("seq", ("sec", "tp")),
    )
    out_specs = (P("seq", ("sec", "tp")), P("seq", None))
    return jax.shard_map(
        on_device, mesh=mesh, in_specs=in_specs, out_specs=out_specs, check_vma=False
    )
```

```python
import functools
import itertools
import math

import jax
import jax.numpy as jnp
from jax import lax
from jax.experimental import pallas as pl
from jax.experimental.pallas import tpu as pltpu
from jax.sharding import PartitionSpec as P

HD = 128
EPS = 1e-06
NEG = -1e30
VMEM_LIMIT = 48 * 1024 * 1024
WIDE_LIMIT = 854 * 64 * 1024
WHOLE = pl.BlockSpec(memory_space=pltpu.VMEM)


def owner_block(image, count):
    half = count // 2
    return image - half if image >= half else half + (image + 1) % half


def held_image(block, count):
    half = count // 2
    return jnp.where(block < half, block + half, lax.rem(block + half - 1, half))


def flows(rounds, count):
    load = [0] * (2 * count)
    for pairs in rounds:
        for s, t in enumerate(pairs):
            for k in range(min(s, t), max(s, t)):
                load[2 * k + (t > s)] += 1
    return max(load), sum(load)


def rounds_of(edges, count):
    best = [tuple(d ^ r for d in range(count)) for r in range(count - 1, 0, -1)]
    if count > 4:
        return best
    whole = [p for p in itertools.permutations(range(count)) if all(s != t for s, t in enumerate(p))]
    for size in range(1, count):
        found = [c for c in itertools.combinations(whole, size) if all(any(p[s] == t for p in c) for s, t in edges)]
        if found:
            far = lambda p: max(abs(s - t) for s, t in enumerate(p))
            found = [sorted(c, key=far) for c in found]
            return min(found, key=lambda c: (flows(c, count)[0], flows(c[-1:], count), flows(c, count)))
    return best


def pick_static(table, index):
    value = jnp.int32(table[0])
    for n in range(1, len(table)):
        value = jnp.where(index == n, table[n], value)
    return value


def group_place():
    sec, tp = lax.axis_index("sec"), lax.axis_index("tp")
    return lax.rem(sec, 2), lax.div(sec, 2) * lax.axis_size("tp") + tp


def dot(a, b, dims):
    return lax.dot_general(a, b, (dims, ((), ())), preferred_element_type=jnp.float32)


def call(body, out_shape, in_specs, out_specs, flops, moved, limit=VMEM_LIMIT, **more):
    return pl.pallas_call(
        body,
        out_shape=out_shape,
        in_specs=in_specs,
        out_specs=out_specs,
        compiler_params=pltpu.CompilerParams(vmem_limit_bytes=limit),
        cost_estimate=pl.CostEstimate(flops=flops, bytes_accessed=moved, transcendentals=0),
        **more,
    )


def cuts(width):
    size = max(width // (4 * 256), 1) * 256
    edges = [i * size for i in range(4)] + [width]
    return list(zip(edges[:-1], edges[1:]))


def project_body(piece, vis_hbm, gain_hbm, proj_hbm, kv_ref, own_ref, vis, scaled, gain_ref, proj, vis_sems, proj_sems, gain_sem):
    rows, width = vis.shape
    gain_copy = pltpu.make_async_copy(gain_hbm, gain_ref, gain_sem)
    gain_copy.start()
    chunks = cuts(width)
    vis_copies, proj_copies = [], []
    for n, (low, high) in enumerate(chunks):
        vis_copies.append(pltpu.make_async_copy(vis_hbm.at[:, low:high], vis.at[:, low:high], vis_sems.at[n]))
        proj_copies.append(pltpu.make_async_copy(proj_hbm.at[low:high, :], proj.at[low:high, :], proj_sems.at[n]))
    for copy in vis_copies + proj_copies[:2]:
        copy.start()
    gain_copy.wait()
    squares = jnp.zeros((rows, HD), jnp.float32)
    for n, (low, high) in enumerate(chunks):
        vis_copies[n].wait()
        for copy in proj_copies[n + 2 : n + 3]:
            copy.start()
        for c in range(low, high, HD):
            wide = vis[:, c : c + HD].astype(jnp.float32)
            squares += wide * wide
            scaled[:, c : c + HD] = (wide * gain_ref[c // HD : c // HD + 1, :]).astype(jnp.bfloat16)
    total = jnp.zeros(kv_ref.shape, jnp.float32)
    for copy, (low, high) in zip(proj_copies, chunks):
        copy.wait()
        total += jnp.dot(scaled[:, low:high], proj[low:high, :], preferred_element_type=jnp.float32)
    inverse = lax.rsqrt(jnp.sum(squares, axis=1, keepdims=True) / width + EPS)
    kv_ref[...] = (total * inverse).astype(jnp.bfloat16)
    parity, place = group_place()
    start = pl.multiple_of(parity * (rows // 2) + place * piece, piece)
    own_ref[...] = vis[pl.ds(start, piece), :]


def text_rows(pieces_ref, image):
    values = pieces_ref[...].astype(jnp.float32)
    lane = lax.broadcasted_iota(jnp.int32, values.shape, 1)
    return jnp.sum(jnp.where(lane == 2 * image, values, 0.0), axis=1, keepdims=True).astype(jnp.int32)


def placed(before, rows, image_ref, text_ref):
    ahead = lax.broadcasted_iota(jnp.int32, (rows, rows), 0) - lax.broadcasted_iota(jnp.int32, (rows, rows), 1)
    pick = jnp.where(ahead == before, 1.0, 0.0).astype(jnp.bfloat16)
    image = jnp.dot(pick, image_ref[...], preferred_element_type=jnp.float32)
    row = lax.broadcasted_iota(jnp.int32, image.shape, 0)
    return jnp.where(row < before, text_ref[...].astype(jnp.float32), image).astype(jnp.bfloat16)


def place_body(seq_n, pieces_ref, image_ref, text_ref, out_ref):
    rows = image_ref.shape[0]
    before = text_rows(pieces_ref, held_image(lax.axis_index("seq"), seq_n))
    out_ref[...] = placed(before, rows, image_ref, text_ref)


def heads_of(ref, heads):
    return jnp.concatenate([ref[:, h * HD : (h + 1) * HD] for h in heads], axis=0)


def head_groups(group, keys):
    together = group if keys <= 1024 else 1
    return [range(first, first + together) for first in range(0, group, together)]


def grad_parts(chosen, rows, scale, low_ref, dscore_ref, q_ref, g_ref, grad_refs):
    totals = [None] * len(chosen)
    for heads in head_groups(q_ref.shape[1] // HD, low_ref.shape[0]):
        q, g = heads_of(q_ref, heads), heads_of(g_ref, heads)
        span = slice(heads[0] * rows, (heads[-1] + 1) * rows)
        for n, r in enumerate(chosen):
            part = pl.ds(pl.multiple_of(r * rows, rows), rows)
            dkeys = jnp.dot(dscore_ref[part, span], q, preferred_element_type=jnp.float32)
            dvalues = jnp.dot(low_ref[part, span], g, preferred_element_type=jnp.float32)
            if totals[n] is not None:
                dkeys, dvalues = totals[n][0] + dkeys, totals[n][1] + dvalues
            totals[n] = dkeys, dvalues
    for (dkeys, dvalues), ref in zip(totals, grad_refs):
        ref[:, :HD] = (dkeys * scale).astype(jnp.bfloat16)
        ref[:, HD:] = dvalues.astype(jnp.bfloat16)


def weigh_body(seq_n, tables, backs, pieces_ref, q_ref, g_ref, text_ref, own_ref, raw_ref, *refs):
    count = len(tables)
    block_refs, (low_ref, dscore_ref, values_ref) = refs[:count], refs[count : count + 3]
    grad_refs, (scores, dprob) = refs[count + 3 : -2], refs[-2:]
    rows = q_ref.shape[0]
    group = q_ref.shape[1] // HD
    scale = 1.0 / math.sqrt(HD)
    me = lax.axis_index("seq")
    mine = placed(text_rows(pieces_ref, me), rows, raw_ref, text_ref)
    kv = jnp.concatenate([own_ref[...], mine] + [ref[...] for ref in block_refs], axis=0)
    keys, values = kv[:, :HD], kv[:, HD:]
    values_ref[...] = values
    images = [held_image(me, seq_n), me] + [pick_static(table, me) for table in tables]
    shifts = [jnp.where(image < me, 0.0, NEG) for image in images]
    seen = lax.broadcasted_iota(jnp.int32, (rows, rows), 0) <= lax.broadcasted_iota(jnp.int32, (rows, rows), 1)
    parts = [slice(n * rows, (n + 1) * rows) for n in range(len(images))]

    def score(n, cols):
        block = scores[parts[n], cols]
        return jnp.where(seen, block, NEG) if n == 1 else block + shifts[n]

    for heads in head_groups(group, kv.shape[0]):
        scores[...] = dot(keys, heads_of(q_ref, heads), ((1,), (1,)))
        dprob[...] = dot(values, heads_of(g_ref, heads), ((1,), (1,)))
        for h in heads:
            cols = slice((h - heads[0]) * rows, (h - heads[0] + 1) * rows)
            wide = slice(h * rows, (h + 1) * rows)
            top = score(0, cols)
            for n in range(1, len(parts)):
                top = jnp.maximum(top, score(n, cols))
            top = jnp.max(top, axis=0, keepdims=True)
            total = None
            for n, part in enumerate(parts):
                weights = jnp.exp2((score(n, cols) - top) * (scale * math.log2(math.e)))
                scores[part, cols] = weights
                total = weights if total is None else total + weights
            inverse = 1.0 / jnp.sum(total, axis=0, keepdims=True)
            drift = None
            for part in parts:
                weights = scores[part, cols] * inverse
                scores[part, cols] = weights
                low = weights.astype(jnp.bfloat16)
                low_ref[part, wide] = low
                term = low.astype(jnp.float32) * dprob[part, cols]
                drift = term if drift is None else drift + term
            drift = jnp.sum(drift, axis=0, keepdims=True)
            for part in parts:
                dscore_ref[part, wide] = (scores[part, cols] * (dprob[part, cols] - drift)).astype(jnp.bfloat16)
    early = [pick_static(table, me) for table in backs]
    grad_parts(early, rows, scale, low_ref, dscore_ref, q_ref, g_ref, grad_refs)


def mix_body(late, q_ref, g_ref, low_ref, dscore_ref, values_ref, out_ref, *grad_refs):
    rows = q_ref.shape[0]
    grad_parts(late, rows, 1.0 / math.sqrt(HD), low_ref, dscore_ref, q_ref, g_ref, grad_refs)
    for heads in head_groups(q_ref.shape[1] // HD, low_ref.shape[0]):
        span = slice(heads[0] * rows, (heads[-1] + 1) * rows)
        mixed = dot(values_ref[...], low_ref[:, span], ((0,), (0,)))
        for n, h in enumerate(heads):
            part = jnp.transpose(mixed[:, n * rows : (n + 1) * rows])
            out_ref[:, h * HD : (h + 1) * HD] = part.astype(jnp.bfloat16)


def back_body(seq_n, count, piece, pieces_ref, proj_ref, *refs):
    part_refs, (rest_ref, keep_ref, send_ref) = refs[:-3], refs[-3:]
    rows = part_refs[0].shape[0]
    before = text_rows(pieces_ref, held_image(lax.axis_index("seq"), seq_n))
    parity, place = group_place()
    total = part_refs[0][...].astype(jnp.float32)
    for ref in part_refs[1:]:
        total += ref[...].astype(jnp.float32)
    slot = lax.broadcasted_iota(jnp.int32, (rows, rows), 0)
    group = lax.div(slot, piece)
    core = jnp.where(group < 2, group, jnp.where(group > count, 1, 0))
    step = jnp.where(group < 2, count - 1, lax.rem(group + count - 3, count - 1))
    to = ((core ^ parity) * count + (step ^ place)) * piece + lax.rem(slot, piece)
    source = lax.broadcasted_iota(jnp.int32, (rows, rows), 1)
    pick = jnp.where(source == to + before, 1.0, 0.0).astype(jnp.bfloat16)
    image_grad = jnp.dot(pick, total.astype(jnp.bfloat16), preferred_element_type=jnp.float32)
    image_grad = image_grad.astype(jnp.bfloat16)
    product = dot(image_grad[: 2 * piece], proj_ref[...], ((1,), (1,)))
    keep_ref[...] = product[:piece]
    send_ref[...] = product[piece:].astype(jnp.bfloat16)
    rest_ref[...] = image_grad[2 * piece :]


def rest_body(rest_ref, proj_ref, keep_ref, send_ref):
    half = rest_ref.shape[0] // 2
    product = dot(rest_ref[...], proj_ref[...], ((1,), (1,)))
    keep_ref[...] = product[:half]
    send_ref[...] = product[half:].astype(jnp.bfloat16)


def last_body(keep_ref, other_ref, send_ref):
    send_ref[...] = (keep_ref[...] + other_ref[...].astype(jnp.float32)).astype(jnp.bfloat16)


def pair_body(piece, keep_ref, other_ref, own_ref, *send_refs):
    own_ref[...] = keep_ref[:piece] + other_ref[:piece].astype(jnp.float32)
    for n, ref in enumerate(send_refs):
        part = slice((n + 1) * piece, (n + 2) * piece)
        ref[...] = (keep_ref[part] + other_ref[part].astype(jnp.float32)).astype(jnp.bfloat16)


def final_body(total_ref, own_ref, gain_ref, *refs):
    out_ref = refs[-1]
    width = own_ref.shape[1]
    square = stat = None
    scaled = []
    for c in range(0, width, HD):
        cols = slice(c, c + HD)
        total = total_ref[:, cols]
        for ref in refs[:-1]:
            total += ref[:, cols].astype(jnp.float32)
        own = own_ref[:, cols].astype(jnp.float32)
        grad = total * gain_ref[c // HD : c // HD + 1, :]
        scaled.append(grad)
        square = own * own if square is None else square + own * own
        stat = own * grad if stat is None else stat + own * grad
    inverse = lax.rsqrt(jnp.sum(square, axis=1, keepdims=True) / width + EPS)
    lead = inverse * inverse * inverse * (jnp.sum(stat, axis=1, keepdims=True) / width)
    for n, c in enumerate(range(0, width, HD)):
        own = own_ref[:, c : c + HD].astype(jnp.float32)
        out_ref[:, c : c + HD] = (scaled[n] * inverse - own * lead).astype(jnp.bfloat16)


def gather_body(count, chosen, *refs):
    part_refs, (out_hbm, sems) = refs[: len(chosen)], refs[-2:]
    piece = part_refs[0].shape[0]
    parity, place = group_place()
    copies = []
    for n, (ref, (core, step)) in enumerate(zip(part_refs, chosen)):
        row = ((parity ^ core) * count + (place ^ step)) * piece
        copy = pltpu.make_async_copy(ref, out_hbm.at[pl.ds(pl.multiple_of(row, piece), piece), :], sems.at[n])
        copy.start()
        copies.append(copy)
    for copy in copies:
        copy.wait()


def on_device(vis_rows, vis_gain, key_value_proj, pieces, text_kv, queries, grad_out):
    rows, width = vis_rows.shape
    columns = key_value_proj.shape[1]
    seq_n = lax.axis_size("seq")
    tp_n = lax.axis_size("tp")
    n = lax.axis_size("sec") * tp_n
    count = n // 2
    piece = rows // n
    bf16, f32 = jnp.bfloat16, jnp.float32
    names = ("sec", "tp")
    core_pairs = [(i, (i // tp_n ^ 1) * tp_n + i % tp_n) for i in range(n)]

    def far_pairs(step):
        pairs = []
        for i in range(n):
            sec, tp = divmod(i, tp_n)
            place = (sec // 2 * tp_n + tp) ^ step
            pairs.append((i, (place // tp_n * 2 + sec % 2) * tp_n + place % tp_n))
        return pairs

    gain = vis_gain.reshape(width // HD, HD)
    pieces = pieces.reshape(1, -1)
    owners = [owner_block(j, seq_n) for j in range(seq_n)]
    held = [owners.index(b) for b in range(seq_n)]
    home = [(owners[j], j) for j in range(seq_n)]
    edges = {(owners[j], d) for j in range(seq_n) for d in range(j + 1, seq_n) if owners[j] != d}
    tables, forth, left = [], [], set(edges)
    for pairs in rounds_of(sorted(edges), seq_n):
        table = [seq_n] * seq_n
        for s, t in enumerate(pairs):
            if (s, t) in left:
                table[t] = held[s]
        left -= set(enumerate(pairs))
        tables.append(table)
        forth.append(list(enumerate(pairs)))
    text = lax.ppermute(text_kv, "seq", list(enumerate(owners)))
    chunks = len(cuts(width))
    hbm = pl.BlockSpec(memory_space=pltpu.HBM)
    image_kv, own_rows = call(
        functools.partial(project_body, piece),
        [jax.ShapeDtypeStruct((rows, columns), bf16), jax.ShapeDtypeStruct((piece, width), bf16)],
        [hbm, hbm, hbm],
        [WHOLE, WHOLE],
        2 * rows * width * columns,
        2 * width * (rows + columns),
        limit=WIDE_LIMIT,
        scratch_shapes=[
            pltpu.VMEM((rows, width), bf16),
            pltpu.VMEM((rows, width), bf16),
            pltpu.VMEM(gain.shape, f32),
            pltpu.VMEM((width, columns), bf16),
            pltpu.SemaphoreType.DMA((chunks,)),
            pltpu.SemaphoreType.DMA((chunks,)),
            pltpu.SemaphoreType.DMA,
        ],
    )(vis_rows, gain, key_value_proj)
    raw = lax.ppermute(image_kv, "seq", home)
    block = call(
        functools.partial(place_body, seq_n),
        jax.ShapeDtypeStruct((rows, columns), bf16),
        [WHOLE] * 3,
        WHOLE,
        0,
        6 * rows * columns,
    )(pieces, image_kv, text)
    blocks = [lax.ppermute(block, "seq", pairs) for pairs in forth]
    total = 2 + len(blocks)
    pairs_back, backs = [], []
    for r in sorted(range(1, seq_n), key=lambda r: (r < seq_n // 2, r)):
        pairs_back.append([(d, d ^ r) for d in range(seq_n)])
        table = []
        for d in range(seq_n):
            block_of = [held[d], d] + [t[d] for t in tables]
            want = held[d ^ r]
            if want > d:
                want = max(block_of)
            table.append(block_of.index(want, 1))
        backs.append(table)
    kv_shape = jax.ShapeDtypeStruct((rows, columns), bf16)
    wide_shape = jax.ShapeDtypeStruct((total * rows, queries.shape[1] // HD * rows), bf16)
    low, dscore, values, *grads = call(
        functools.partial(weigh_body, seq_n, tables, backs),
        [wide_shape, wide_shape, jax.ShapeDtypeStruct((total * rows, HD), bf16)] + [kv_shape] * len(backs),
        [WHOLE] * (4 + total),
        [WHOLE] * (3 + len(backs)),
        8 * total * rows * rows * queries.shape[1],
        4 * rows * queries.shape[1] + 4 * total * rows * columns,
        scratch_shapes=[pltpu.VMEM((total * rows, len(head_groups(queries.shape[1] // HD, total * rows)[0]) * rows), f32)] * 2,
    )(pieces, queries, grad_out, text_kv, block, raw, *blocks)
    attended, own_grad = call(
        functools.partial(mix_body, [0]),
        [jax.ShapeDtypeStruct(queries.shape, bf16), kv_shape],
        [WHOLE] * 5,
        [WHOLE, WHOLE],
        2 * total * rows * rows * queries.shape[1],
        6 * rows * queries.shape[1] + 4 * total * rows * columns,
    )(queries, grad_out, low, dscore, values)
    parts = [lax.ppermute(g, "seq", pairs) for g, pairs in zip(grads, pairs_back)]

    def shape(height, dtype):
        return jax.ShapeDtypeStruct((height, width), dtype)

    rest, keep_last, send_last = call(
        functools.partial(back_body, seq_n, count, piece),
        [jax.ShapeDtypeStruct((rows - 2 * piece, columns), bf16), shape(piece, f32), shape(piece, bf16)],
        [WHOLE] * (3 + len(parts)),
        [WHOLE] * 3,
        4 * piece * width * columns,
        2 * width * columns + 6 * piece * width,
    )(pieces, key_value_proj, own_grad, *parts)
    other_last = lax.ppermute(send_last, names, core_pairs)
    height = rows // 2 - piece
    keep, send = call(
        rest_body,
        [shape(height, f32), shape(height, bf16)],
        [WHOLE, WHOLE],
        [WHOLE, WHOLE],
        4 * height * width * columns,
        2 * width * columns + 6 * height * width,
    )(rest, key_value_proj)
    other = lax.ppermute(send, names, core_pairs)
    weight = 64 * rows * width * columns
    far = call(last_body, shape(piece, bf16), [WHOLE, WHOLE], WHOLE, weight, 8 * piece * width)(keep_last, other_last)
    shares = [lax.ppermute(far, names, far_pairs(count - 1))]
    own_sum, *sends = call(
        functools.partial(pair_body, piece),
        [shape(piece, f32)] + [shape(piece, bf16)] * (count - 2),
        [WHOLE, WHOLE],
        [WHOLE] * (count - 1),
        0,
        8 * height * width,
    )(keep, other)
    steps = list(range(1, count))
    shares += [lax.ppermute(sends[d - 1], names, far_pairs(d)) for d in steps[-2::-1]]
    mine = call(
        final_body,
        jax.ShapeDtypeStruct((piece, width), bf16),
        [WHOLE] * (3 + len(shares)),
        WHOLE,
        0,
        12 * piece * width,
    )(own_sum, own_rows, gain, *shares)
    mines = {0: mine}
    for d in steps:
        mines[d] = lax.ppermute(mine, names, far_pairs(d))
    theirs = {d: lax.ppermute(mines[d], names, core_pairs) for d in range(count)}
    ready = {(core, d): part[d] for core, part in enumerate((mines, theirs)) for d in range(count)}
    early = [key for key in sorted(ready) if key[0] == 0 or key[1] in (0, count - 1)]
    vis_grad = None
    for chosen in (early, [key for key in sorted(ready) if key not in early]):
        done = [] if vis_grad is None else [vis_grad]
        vis_grad = call(
            functools.partial(gather_body, count, chosen),
            shape(rows, bf16),
            [WHOLE] * len(chosen) + [hbm] * len(done),
            hbm,
            0,
            4 * piece * width * len(chosen),
            scratch_shapes=[pltpu.SemaphoreType.DMA((len(chosen),))],
            input_output_aliases={len(chosen): 0} if done else {},
        )(*[ready[key] for key in chosen], *done)
    return (attended, vis_grad)


def solution(mesh):
    in_specs = (
        P("seq", None),
        P(),
        P(None, ("sec", "tp")),
        P(),
        P("seq", ("sec", "tp")),
        P("seq", ("sec", "tp")),
        P("seq", ("sec", "tp")),
    )
    out_specs = (P("seq", ("sec", "tp")), P("seq", None))
    return jax.shard_map(
        on_device, mesh=mesh, in_specs=in_specs, out_specs=out_specs, check_vma=False
    )
```

```python
import functools
import itertools
import math

import jax
import jax.numpy as jnp
from jax import lax
from jax.experimental import pallas as pl
from jax.experimental.pallas import tpu as pltpu
from jax.sharding import PartitionSpec as P

HD = 128
EPS = 1e-06
NEG = -1e30
VMEM_LIMIT = 48 * 1024 * 1024
WIDE_LIMIT = 854 * 64 * 1024
WHOLE = pl.BlockSpec(memory_space=pltpu.VMEM)


def owner_block(image, count):
    half = count // 2
    return image - half if image >= half else half + (image + 1) % half


def held_image(block, count):
    half = count // 2
    return jnp.where(block < half, block + half, lax.rem(block + half - 1, half))


def flows(rounds, count):
    load = [0] * (2 * count)
    for pairs in rounds:
        for s, t in enumerate(pairs):
            for k in range(min(s, t), max(s, t)):
                load[2 * k + (t > s)] += 1
    return max(load), sum(load)


def rounds_of(edges, count):
    best = [tuple(d ^ r for d in range(count)) for r in range(count - 1, 0, -1)]
    if count > 4:
        return best
    whole = [p for p in itertools.permutations(range(count)) if all(s != t for s, t in enumerate(p))]
    for size in range(1, count):
        found = [c for c in itertools.combinations(whole, size) if all(any(p[s] == t for p in c) for s, t in edges)]
        if found:
            far = lambda p: max(abs(s - t) for s, t in enumerate(p))
            found = [sorted(c, key=far) for c in found]
            return min(found, key=lambda c: (flows(c, count)[0], flows(c[-1:], count), flows(c, count)))
    return best


def pick_static(table, index):
    value = jnp.int32(table[0])
    for n in range(1, len(table)):
        value = jnp.where(index == n, table[n], value)
    return value


def group_place():
    sec, tp = lax.axis_index("sec"), lax.axis_index("tp")
    return lax.rem(sec, 2), lax.div(sec, 2) * lax.axis_size("tp") + tp


def dot(a, b, dims):
    return lax.dot_general(a, b, (dims, ((), ())), preferred_element_type=jnp.float32)


def call(body, out_shape, in_specs, out_specs, flops, moved, limit=VMEM_LIMIT, **more):
    return pl.pallas_call(
        body,
        out_shape=out_shape,
        in_specs=in_specs,
        out_specs=out_specs,
        compiler_params=pltpu.CompilerParams(vmem_limit_bytes=limit),
        cost_estimate=pl.CostEstimate(flops=flops, bytes_accessed=moved, transcendentals=0),
        **more,
    )


def cuts(width):
    size = max(width // (4 * 256), 1) * 256
    edges = [i * size for i in range(4)] + [width]
    return list(zip(edges[:-1], edges[1:]))


def project_body(piece, vis_hbm, gain_hbm, proj_hbm, kv_ref, own_ref, vis, scaled, gain_ref, proj, vis_sems, proj_sems, gain_sem):
    rows, width = vis.shape
    gain_copy = pltpu.make_async_copy(gain_hbm, gain_ref, gain_sem)
    gain_copy.start()
    chunks = cuts(width)
    vis_copies, proj_copies = [], []
    for n, (low, high) in enumerate(chunks):
        vis_copies.append(pltpu.make_async_copy(vis_hbm.at[:, low:high], vis.at[:, low:high], vis_sems.at[n]))
        proj_copies.append(pltpu.make_async_copy(proj_hbm.at[low:high, :], proj.at[low:high, :], proj_sems.at[n]))
    for copy in vis_copies + proj_copies:
        copy.start()
    gain_copy.wait()
    squares = jnp.zeros((rows, HD), jnp.float32)
    for n, (low, high) in enumerate(chunks):
        vis_copies[n].wait()
        for c in range(low, high, HD):
            wide = vis[:, c : c + HD].astype(jnp.float32)
            squares += wide * wide
            scaled[:, c : c + HD] = (wide * gain_ref[c // HD : c // HD + 1, :]).astype(jnp.bfloat16)
    total = jnp.zeros(kv_ref.shape, jnp.float32)
    for copy, (low, high) in zip(proj_copies, chunks):
        copy.wait()
        total += jnp.dot(scaled[:, low:high], proj[low:high, :], preferred_element_type=jnp.float32)
    inverse = lax.rsqrt(jnp.sum(squares, axis=1, keepdims=True) / width + EPS)
    kv_ref[...] = (total * inverse).astype(jnp.bfloat16)
    parity, place = group_place()
    start = pl.multiple_of(parity * (rows // 2) + place * piece, piece)
    own_ref[...] = vis[pl.ds(start, piece), :]


def text_rows(pieces_ref, image):
    values = pieces_ref[...].astype(jnp.float32)
    lane = lax.broadcasted_iota(jnp.int32, values.shape, 1)
    return jnp.sum(jnp.where(lane == 2 * image, values, 0.0), axis=1, keepdims=True).astype(jnp.int32)


def placed(before, rows, image_ref, text_ref):
    ahead = lax.broadcasted_iota(jnp.int32, (rows, rows), 0) - lax.broadcasted_iota(jnp.int32, (rows, rows), 1)
    pick = jnp.where(ahead == before, 1.0, 0.0).astype(jnp.bfloat16)
    image = jnp.dot(pick, image_ref[...], preferred_element_type=jnp.float32)
    row = lax.broadcasted_iota(jnp.int32, image.shape, 0)
    return jnp.where(row < before, text_ref[...].astype(jnp.float32), image).astype(jnp.bfloat16)


def place_body(seq_n, pieces_ref, image_ref, text_ref, out_ref):
    rows = image_ref.shape[0]
    before = text_rows(pieces_ref, held_image(lax.axis_index("seq"), seq_n))
    out_ref[...] = placed(before, rows, image_ref, text_ref)


def heads_of(ref, heads):
    return jnp.concatenate([ref[:, h * HD : (h + 1) * HD] for h in heads], axis=0)


def head_groups(group, keys):
    together = group if keys <= 1024 else 1
    return [range(first, first + together) for first in range(0, group, together)]


def grad_parts(chosen, rows, scale, low_ref, dscore_ref, q_ref, g_ref, grad_refs):
    totals = [None] * len(chosen)
    for heads in head_groups(q_ref.shape[1] // HD, low_ref.shape[0]):
        q, g = heads_of(q_ref, heads), heads_of(g_ref, heads)
        span = slice(heads[0] * rows, (heads[-1] + 1) * rows)
        for n, r in enumerate(chosen):
            part = pl.ds(pl.multiple_of(r * rows, rows), rows)
            dkeys = jnp.dot(dscore_ref[part, span], q, preferred_element_type=jnp.float32)
            dvalues = jnp.dot(low_ref[part, span], g, preferred_element_type=jnp.float32)
            if totals[n] is not None:
                dkeys, dvalues = totals[n][0] + dkeys, totals[n][1] + dvalues
            totals[n] = dkeys, dvalues
    for (dkeys, dvalues), ref in zip(totals, grad_refs):
        ref[:, :HD] = (dkeys * scale).astype(jnp.bfloat16)
        ref[:, HD:] = dvalues.astype(jnp.bfloat16)


def weigh_body(seq_n, tables, backs, pieces_ref, q_ref, g_ref, text_ref, own_ref, raw_ref, *refs):
    count = len(tables)
    block_refs, (low_ref, dscore_ref, values_ref) = refs[:count], refs[count : count + 3]
    grad_refs, (scores, dprob) = refs[count + 3 : -2], refs[-2:]
    rows = q_ref.shape[0]
    group = q_ref.shape[1] // HD
    scale = 1.0 / math.sqrt(HD)
    me = lax.axis_index("seq")
    mine = placed(text_rows(pieces_ref, me), rows, raw_ref, text_ref)
    kv = jnp.concatenate([own_ref[...], mine] + [ref[...] for ref in block_refs], axis=0)
    keys, values = kv[:, :HD], kv[:, HD:]
    values_ref[...] = values
    images = [held_image(me, seq_n), me] + [pick_static(table, me) for table in tables]
    shifts = [jnp.where(image < me, 0.0, NEG) for image in images]
    seen = lax.broadcasted_iota(jnp.int32, (rows, rows), 0) <= lax.broadcasted_iota(jnp.int32, (rows, rows), 1)
    parts = [slice(n * rows, (n + 1) * rows) for n in range(len(images))]

    def score(n, cols):
        block = scores[parts[n], cols]
        return jnp.where(seen, block, NEG) if n == 1 else block + shifts[n]

    for heads in head_groups(group, kv.shape[0]):
        scores[...] = dot(keys, heads_of(q_ref, heads), ((1,), (1,)))
        dprob[...] = dot(values, heads_of(g_ref, heads), ((1,), (1,)))
        for h in heads:
            cols = slice((h - heads[0]) * rows, (h - heads[0] + 1) * rows)
            wide = slice(h * rows, (h + 1) * rows)
            top = score(0, cols)
            for n in range(1, len(parts)):
                top = jnp.maximum(top, score(n, cols))
            top = jnp.max(top, axis=0, keepdims=True)
            total = None
            for n, part in enumerate(parts):
                weights = jnp.exp2((score(n, cols) - top) * (scale * math.log2(math.e)))
                scores[part, cols] = weights
                total = weights if total is None else total + weights
            inverse = 1.0 / jnp.sum(total, axis=0, keepdims=True)
            drift = None
            for part in parts:
                weights = scores[part, cols] * inverse
                scores[part, cols] = weights
                low = weights.astype(jnp.bfloat16)
                low_ref[part, wide] = low
                term = low.astype(jnp.float32) * dprob[part, cols]
                drift = term if drift is None else drift + term
            drift = jnp.sum(drift, axis=0, keepdims=True)
            for part in parts:
                dscore_ref[part, wide] = (scores[part, cols] * (dprob[part, cols] - drift)).astype(jnp.bfloat16)
    early = [pick_static(table, me) for table in backs]
    grad_parts(early, rows, scale, low_ref, dscore_ref, q_ref, g_ref, grad_refs)


def mix_body(late, q_ref, g_ref, low_ref, dscore_ref, values_ref, out_ref, *grad_refs):
    rows = q_ref.shape[0]
    grad_parts(late, rows, 1.0 / math.sqrt(HD), low_ref, dscore_ref, q_ref, g_ref, grad_refs)
    for heads in head_groups(q_ref.shape[1] // HD, low_ref.shape[0]):
        span = slice(heads[0] * rows, (heads[-1] + 1) * rows)
        mixed = dot(values_ref[...], low_ref[:, span], ((0,), (0,)))
        for n, h in enumerate(heads):
            part = jnp.transpose(mixed[:, n * rows : (n + 1) * rows])
            out_ref[:, h * HD : (h + 1) * HD] = part.astype(jnp.bfloat16)


def back_body(seq_n, count, piece, pieces_ref, proj_ref, *refs):
    part_refs, (rest_ref, keep_ref, send_ref) = refs[:-3], refs[-3:]
    rows = part_refs[0].shape[0]
    before = text_rows(pieces_ref, held_image(lax.axis_index("seq"), seq_n))
    parity, place = group_place()
    total = part_refs[0][...].astype(jnp.float32)
    for ref in part_refs[1:]:
        total += ref[...].astype(jnp.float32)
    slot = lax.broadcasted_iota(jnp.int32, (rows, rows), 0)
    group = lax.div(slot, piece)
    core = jnp.where(group < 2, group, jnp.where(group > count, 1, 0))
    step = jnp.where(group < 2, count - 1, lax.rem(group + count - 3, count - 1))
    to = ((core ^ parity) * count + (step ^ place)) * piece + lax.rem(slot, piece)
    source = lax.broadcasted_iota(jnp.int32, (rows, rows), 1)
    pick = jnp.where(source == to + before, 1.0, 0.0).astype(jnp.bfloat16)
    image_grad = jnp.dot(pick, total.astype(jnp.bfloat16), preferred_element_type=jnp.float32)
    image_grad = image_grad.astype(jnp.bfloat16)
    product = dot(image_grad[: 2 * piece], proj_ref[...], ((1,), (1,)))
    keep_ref[...] = product[:piece]
    send_ref[...] = product[piece:].astype(jnp.bfloat16)
    rest_ref[...] = image_grad[2 * piece :]


def rest_body(rest_ref, proj_ref, keep_ref, send_ref):
    half = rest_ref.shape[0] // 2
    product = dot(rest_ref[...], proj_ref[...], ((1,), (1,)))
    keep_ref[...] = product[:half]
    send_ref[...] = product[half:].astype(jnp.bfloat16)


def last_body(keep_ref, other_ref, send_ref):
    send_ref[...] = (keep_ref[...] + other_ref[...].astype(jnp.float32)).astype(jnp.bfloat16)


def pair_body(piece, keep_ref, other_ref, own_ref, *send_refs):
    own_ref[...] = keep_ref[:piece] + other_ref[:piece].astype(jnp.float32)
    for n, ref in enumerate(send_refs):
        part = slice((n + 1) * piece, (n + 2) * piece)
        ref[...] = (keep_ref[part] + other_ref[part].astype(jnp.float32)).astype(jnp.bfloat16)


def final_body(total_ref, own_ref, gain_ref, *refs):
    out_ref = refs[-1]
    width = own_ref.shape[1]
    square = stat = None
    scaled = []
    for c in range(0, width, HD):
        cols = slice(c, c + HD)
        total = total_ref[:, cols]
        for ref in refs[:-1]:
            total += ref[:, cols].astype(jnp.float32)
        own = own_ref[:, cols].astype(jnp.float32)
        grad = total * gain_ref[c // HD : c // HD + 1, :]
        scaled.append(grad)
        square = own * own if square is None else square + own * own
        stat = own * grad if stat is None else stat + own * grad
    inverse = lax.rsqrt(jnp.sum(square, axis=1, keepdims=True) / width + EPS)
    lead = inverse * inverse * inverse * (jnp.sum(stat, axis=1, keepdims=True) / width)
    for n, c in enumerate(range(0, width, HD)):
        own = own_ref[:, c : c + HD].astype(jnp.float32)
        out_ref[:, c : c + HD] = (scaled[n] * inverse - own * lead).astype(jnp.bfloat16)


def gather_body(count, chosen, *refs):
    part_refs, (out_hbm, sems) = refs[: len(chosen)], refs[-2:]
    piece = part_refs[0].shape[0]
    parity, place = group_place()
    copies = []
    for n, (ref, (core, step)) in enumerate(zip(part_refs, chosen)):
        row = ((parity ^ core) * count + (place ^ step)) * piece
        copy = pltpu.make_async_copy(ref, out_hbm.at[pl.ds(pl.multiple_of(row, piece), piece), :], sems.at[n])
        copy.start()
        copies.append(copy)
    for copy in copies:
        copy.wait()


def on_device(vis_rows, vis_gain, key_value_proj, pieces, text_kv, queries, grad_out):
    rows, width = vis_rows.shape
    columns = key_value_proj.shape[1]
    seq_n = lax.axis_size("seq")
    tp_n = lax.axis_size("tp")
    n = lax.axis_size("sec") * tp_n
    count = n // 2
    piece = rows // n
    bf16, f32 = jnp.bfloat16, jnp.float32
    names = ("sec", "tp")
    core_pairs = [(i, (i // tp_n ^ 1) * tp_n + i % tp_n) for i in range(n)]

    def far_pairs(step):
        pairs = []
        for i in range(n):
            sec, tp = divmod(i, tp_n)
            place = (sec // 2 * tp_n + tp) ^ step
            pairs.append((i, (place // tp_n * 2 + sec % 2) * tp_n + place % tp_n))
        return pairs

    gain = vis_gain.reshape(width // HD, HD)
    pieces = pieces.reshape(1, -1)
    owners = [owner_block(j, seq_n) for j in range(seq_n)]
    held = [owners.index(b) for b in range(seq_n)]
    home = [(owners[j], j) for j in range(seq_n)]
    edges = {(owners[j], d) for j in range(seq_n) for d in range(j + 1, seq_n) if owners[j] != d}
    tables, forth, left = [], [], set(edges)
    for pairs in rounds_of(sorted(edges), seq_n):
        table = [seq_n] * seq_n
        for s, t in enumerate(pairs):
            if (s, t) in left:
                table[t] = held[s]
        left -= set(enumerate(pairs))
        tables.append(table)
        forth.append(list(enumerate(pairs)))
    text = lax.ppermute(text_kv, "seq", list(enumerate(owners)))
    chunks = len(cuts(width))
    hbm = pl.BlockSpec(memory_space=pltpu.HBM)
    image_kv, own_rows = call(
        functools.partial(project_body, piece),
        [jax.ShapeDtypeStruct((rows, columns), bf16), jax.ShapeDtypeStruct((piece, width), bf16)],
        [hbm, hbm, hbm],
        [WHOLE, WHOLE],
        2 * rows * width * columns,
        2 * width * (rows + columns),
        limit=WIDE_LIMIT,
        scratch_shapes=[
            pltpu.VMEM((rows, width), bf16),
            pltpu.VMEM((rows, width), bf16),
            pltpu.VMEM(gain.shape, f32),
            pltpu.VMEM((width, columns), bf16),
            pltpu.SemaphoreType.DMA((chunks,)),
            pltpu.SemaphoreType.DMA((chunks,)),
            pltpu.SemaphoreType.DMA,
        ],
    )(vis_rows, gain, key_value_proj)
    raw = lax.ppermute(image_kv, "seq", home)
    block = call(
        functools.partial(place_body, seq_n),
        jax.ShapeDtypeStruct((rows, columns), bf16),
        [WHOLE] * 3,
        WHOLE,
        0,
        6 * rows * columns,
    )(pieces, image_kv, text)
    blocks = [lax.ppermute(block, "seq", pairs) for pairs in forth]
    total = 2 + len(blocks)
    pairs_back, backs = [], []
    for r in sorted(range(1, seq_n), key=lambda r: (r < seq_n // 2, r)):
        pairs_back.append([(d, d ^ r) for d in range(seq_n)])
        table = []
        for d in range(seq_n):
            block_of = [held[d], d] + [t[d] for t in tables]
            want = held[d ^ r]
            if want > d:
                want = max(block_of)
            table.append(block_of.index(want, 1))
        backs.append(table)
    kv_shape = jax.ShapeDtypeStruct((rows, columns), bf16)
    wide_shape = jax.ShapeDtypeStruct((total * rows, queries.shape[1] // HD * rows), bf16)
    low, dscore, values, *grads = call(
        functools.partial(weigh_body, seq_n, tables, backs),
        [wide_shape, wide_shape, jax.ShapeDtypeStruct((total * rows, HD), bf16)] + [kv_shape] * len(backs),
        [WHOLE] * (4 + total),
        [WHOLE] * (3 + len(backs)),
        8 * total * rows * rows * queries.shape[1],
        4 * rows * queries.shape[1] + 4 * total * rows * columns,
        scratch_shapes=[pltpu.VMEM((total * rows, len(head_groups(queries.shape[1] // HD, total * rows)[0]) * rows), f32)] * 2,
    )(pieces, queries, grad_out, text_kv, block, raw, *blocks)
    attended, own_grad = call(
        functools.partial(mix_body, [0]),
        [jax.ShapeDtypeStruct(queries.shape, bf16), kv_shape],
        [WHOLE] * 5,
        [WHOLE, WHOLE],
        2 * total * rows * rows * queries.shape[1],
        6 * rows * queries.shape[1] + 4 * total * rows * columns,
    )(queries, grad_out, low, dscore, values)
    parts = [lax.ppermute(g, "seq", pairs) for g, pairs in zip(grads, pairs_back)]

    def shape(height, dtype):
        return jax.ShapeDtypeStruct((height, width), dtype)

    rest, keep_last, send_last = call(
        functools.partial(back_body, seq_n, count, piece),
        [jax.ShapeDtypeStruct((rows - 2 * piece, columns), bf16), shape(piece, f32), shape(piece, bf16)],
        [WHOLE] * (3 + len(parts)),
        [WHOLE] * 3,
        4 * piece * width * columns,
        2 * width * columns + 6 * piece * width,
    )(pieces, key_value_proj, own_grad, *parts)
    other_last = lax.ppermute(send_last, names, core_pairs)
    height = rows // 2 - piece
    keep, send = call(
        rest_body,
        [shape(height, f32), shape(height, bf16)],
        [WHOLE, WHOLE],
        [WHOLE, WHOLE],
        4 * height * width * columns,
        2 * width * columns + 6 * height * width,
    )(rest, key_value_proj)
    other = lax.ppermute(send, names, core_pairs)
    weight = 64 * rows * width * columns
    far = call(last_body, shape(piece, bf16), [WHOLE, WHOLE], WHOLE, weight, 8 * piece * width)(keep_last, other_last)
    shares = [lax.ppermute(far, names, far_pairs(count - 1))]
    own_sum, *sends = call(
        functools.partial(pair_body, piece),
        [shape(piece, f32)] + [shape(piece, bf16)] * (count - 2),
        [WHOLE, WHOLE],
        [WHOLE] * (count - 1),
        0,
        8 * height * width,
    )(keep, other)
    steps = list(range(1, count))
    shares += [lax.ppermute(sends[d - 1], names, far_pairs(d)) for d in steps[-2::-1]]
    mine = call(
        final_body,
        jax.ShapeDtypeStruct((piece, width), bf16),
        [WHOLE] * (3 + len(shares)),
        WHOLE,
        0,
        12 * piece * width,
    )(own_sum, own_rows, gain, *shares)
    mines = {0: mine}
    for d in steps:
        mines[d] = lax.ppermute(mine, names, far_pairs(d))
    theirs = {d: lax.ppermute(mines[d], names, core_pairs) for d in range(count)}
    ready = {(core, d): part[d] for core, part in enumerate((mines, theirs)) for d in range(count)}
    early = [key for key in sorted(ready) if key[0] == 0 or key[1] in (0, count - 1)]
    vis_grad = None
    for chosen in (early, [key for key in sorted(ready) if key not in early]):
        done = [] if vis_grad is None else [vis_grad]
        vis_grad = call(
            functools.partial(gather_body, count, chosen),
            shape(rows, bf16),
            [WHOLE] * len(chosen) + [hbm] * len(done),
            hbm,
            0,
            4 * piece * width * len(chosen),
            scratch_shapes=[pltpu.SemaphoreType.DMA((len(chosen),))],
            input_output_aliases={len(chosen): 0} if done else {},
        )(*[ready[key] for key in chosen], *done)
    return (attended, vis_grad)


def solution(mesh):
    in_specs = (
        P("seq", None),
        P(),
        P(None, ("sec", "tp")),
        P(),
        P("seq", ("sec", "tp")),
        P("seq", ("sec", "tp")),
        P("seq", ("sec", "tp")),
    )
    out_specs = (P("seq", ("sec", "tp")), P("seq", None))
    return jax.shard_map(
        on_device, mesh=mesh, in_specs=in_specs, out_specs=out_specs, check_vma=False
    )
```
